512 devices in a mesh: batch: 32 (over y_lo, z), seq: 16 (over y_hi, x, core).
Axes of the slice: x: 4, y: 4 (y_hi: 2, y_lo: 2; y = y_hi * 2 + y_lo), z: 16, core: 2. Of those that a mesh axis runs over, the one named last changes fastest.
Arguments:
- events: bfloat16 [32, 4096, 256], P('batch', 'seq'), may hold values from -6 to 6
- cotangent: bfloat16 [32, 4096, 256], P('batch', 'seq'), may hold values from -6 to 6
- bucket_ids: int32 [32, 4096, 128], P('batch', 'seq'), may hold values from 0 to 127
- history_lengths: int32 [32], P('batch'), may hold values from 256 to 4096, as said below
- w_in: bfloat16 [256, 1024], replicated, may hold values from -0.375 to 0.375
- b_in: float32 [1024], replicated, may hold values from -3 to 3
- w_out: bfloat16 [256, 256], replicated, may hold values from -0.375 to 0.375
- pos_table: float32 [4, 128], replicated, may hold values from -4 to 4
- time_table: float32 [4, 128], replicated, may hold values from -4 to 4
Outputs:
- layer_out: bfloat16 [32, 4096, 256], P('batch', 'seq')
- grad_events: bfloat16 [32, 4096, 256], P('batch', 'seq')
- grad_w_in: float32 [256, 1024], replicated
- grad_b_in: float32 [1024], replicated
- grad_w_out: float32 [256, 256], replicated
The draws below stay inside these ranges and needn't reach their ends.
Inputs may be any that keep to these rules, and one draw needn't show every extreme that they name: `history_lengths`: each user has at least one slab of 256 real events; some user fills all 4096 positions and some user has exactly 256.
All inputs are finite; a program needn't handle non-finite values.
Results may differ from the reference program's by a relative error of at most 0.0064.
Values may be sent and summed in bfloat16 or wider, within the bound.
No kernel may reach another device: no remote copies, remote signals or barrier semaphores. Data moves between devices by JAX's collectives and lax.ppermute only.
A program may use at most 64 MiB of HBM per device.

```python
import math
import jax
import jax.numpy as jnp
from jax import lax

D = 256
HEADS = 4
WINDOW = 128
BUCKETS = 128
SEQ_DEV = 256
LENGTH = 4096
USERS = 32


def draw_history_lengths(key, part):
    key = jax.random.fold_in(key, 11)
    pick_key, len_key = jax.random.split(key)
    lengths = jax.random.randint(len_key, (USERS,), SEQ_DEV, LENGTH + 1)
    shuffled = jax.random.permutation(pick_key, USERS)
    lengths = lengths.at[shuffled[0]].set(LENGTH)
    lengths = lengths.at[shuffled[1]].set(SEQ_DEV)
    return lengths.astype(jnp.int32)


def with_ends(entries, rng, low, top_value):
    extent = entries.shape
    index_at = [jax.random.randint(jax.random.fold_in(rng, axis), (), 0, extent[axis]) for axis in range(len(extent))]
    entries = entries.at[tuple(index_at)].set(low)
    longest = extent.index(max(extent))
    index_at[longest] = (index_at[longest] + 1) % extent[longest]
    return entries.at[tuple(index_at)].set(top_value)


def levels(own_key, extent, cuts, least, top_value):
    factor_of, own = 1.0, jax.random.fold_in(own_key, 6)
    for dim, blocks in cuts:
        steps = jnp.exp(jax.random.uniform(jax.random.fold_in(own, dim), (blocks,), jnp.float32, least / len(cuts), top_value / len(cuts)))
        factor_of = factor_of * jnp.repeat(steps, extent[dim] // blocks).reshape([-1 if axis == dim else 1 for axis in range(len(extent))])
    return factor_of


def noise(own_key, dims, scale, bound, shards=(), kind=jnp.bfloat16):
    gain = levels(own_key, dims, shards, -0.22, 0.18) if shards else 1.0
    drawn = jax.random.normal(own_key, dims, jnp.float32) * scale * gain
    return jnp.minimum(jnp.maximum(drawn, -bound), bound).astype(kind)


def setup_inputs(seed: int = 0) -> dict:
    seeds = jax.random.split(jax.random.key(seed), 10)
    events = noise(seeds[0], (USERS, LENGTH, D), 1.0, 6.0, ((0, 32), (1, 16)))
    cotangent = noise(seeds[1], (USERS, LENGTH, D), 1.0, 6.0, ((0, 32), (1, 16)))
    bucket_ids = with_ends(jax.random.randint(seeds[2], (USERS, LENGTH, WINDOW), 0, BUCKETS), jax.random.fold_in(seeds[2], 1), 0, BUCKETS - 1).astype(jnp.int32)
    history_lengths = draw_history_lengths(jax.random.fold_in(seeds[9], 71), 0)
    w_in = noise(seeds[4], (D, 4 * D), D ** -0.5, 0.375)
    b_in = noise(seeds[5], (4 * D,), 0.5, 3.0, (), jnp.float32)
    w_out = noise(seeds[6], (D, D), D ** -0.5, 0.375)
    pos_table = noise(seeds[7], (HEADS, WINDOW), 1.0, 4.0, (), jnp.float32)
    time_table = noise(seeds[8], (HEADS, BUCKETS), 1.0, 4.0, (), jnp.float32)
    return dict(events=events, cotangent=cotangent, bucket_ids=bucket_ids, history_lengths=history_lengths, w_in=w_in, b_in=b_in, w_out=w_out, pos_table=pos_table, time_table=time_table)


EPS = 1e-05

def norm_rows(values):
    row_mean = lax.optimization_barrier(jnp.mean(values, axis=-1, keepdims=True))
    centred = values - row_mean
    variance = lax.optimization_barrier(jnp.mean(centred * centred, axis=-1, keepdims=True))
    inv_std = lax.rsqrt(variance + EPS)
    return (centred * inv_std, inv_std)

def norm_back(upstream, normed, inv_std):
    first = lax.optimization_barrier(jnp.mean(upstream, axis=-1, keepdims=True))
    second = lax.optimization_barrier(jnp.mean(upstream * normed, axis=-1, keepdims=True))
    return inv_std * (upstream - first - normed * second)

def silu_slope(pre_act):
    sigmoid = jax.nn.sigmoid(pre_act)
    return sigmoid * (1.0 + pre_act * (1.0 - sigmoid))

def skew_band(offset_bias):
    heads, window, _ = offset_bias.shape
    flipped = offset_bias[:, :, ::-1]
    padded = jnp.concatenate([jnp.zeros((heads, window, 1), offset_bias.dtype), flipped, jnp.zeros((heads, window, window), offset_bias.dtype)], axis=2)
    flat = padded.reshape(heads, window * (2 * window + 1))[:, :window * 2 * window]
    return flat.reshape(heads, window, 2 * window)

def band_scores(query_rows, key_rows, bucket_rows, pos_table, time_table, query_pos, key_pos, length):
    heads, window = pos_table.shape
    head_size = query_rows.shape[1] // heads
    query_heads = query_rows.astype(jnp.float32).reshape(window, heads, head_size)
    key_heads = key_rows.astype(jnp.float32).reshape(2 * window, heads, head_size)
    logits = jnp.einsum('qhd,khd->hqk', query_heads, key_heads, precision=lax.Precision.HIGHEST) / math.sqrt(head_size)
    offset_bias = pos_table[:, None, :] + time_table[:, bucket_rows]
    scores = logits + skew_band(offset_bias)
    gap = query_pos[:, None] - key_pos[None, :]
    allowed = (gap >= 0) & (gap < window) & (query_pos < length)[:, None] & (key_pos < length)[None, :] & (key_pos >= 0)[None, :]
    return (scores, allowed, query_heads, key_heads)

def reference(events, cotangent, bucket_ids, history_lengths, w_in, b_in, w_out, pos_table, time_table):
    width = w_out.shape[0]
    heads, window = pos_table.shape
    head_size = width // heads
    seq_len = events.shape[1]
    blocks = seq_len // window
    loss_scale = 1.0 / math.sqrt(events.shape[0] * seq_len)
    offsets = jnp.arange(window, dtype=jnp.int32)
    key_offsets = jnp.arange(2 * window, dtype=jnp.int32)
    highest = lax.Precision.HIGHEST

    def per_user(totals, user_in):
        user_events, user_cot, user_ids, length = user_in
        ev_float = user_events.astype(jnp.float32)
        ev_hat, ev_inv = norm_rows(ev_float)
        ev_normed = ev_hat.astype(jnp.bfloat16)
        pre_act = jnp.dot(ev_normed, w_in, preferred_element_type=jnp.float32) + b_in
        projected = jax.nn.silu(pre_act).astype(jnp.bfloat16)
        gate_u = projected[:, :width]
        queries = projected[:, 2 * width:3 * width]
        edge_zero = jnp.zeros((window, width), jnp.bfloat16)
        all_values = jnp.concatenate([edge_zero, projected[:, width:2 * width]], axis=0)
        all_keys = jnp.concatenate([edge_zero, projected[:, 3 * width:]], axis=0)

        def block_setup(block_index):
            begin_row = block_index * window
            q_rows = lax.dynamic_slice_in_dim(queries, begin_row, window, 0)
            k_rows = lax.dynamic_slice_in_dim(all_keys, begin_row, 2 * window, 0)
            v_rows = lax.dynamic_slice_in_dim(all_values, begin_row, 2 * window, 0)
            id_rows = lax.dynamic_slice_in_dim(user_ids, begin_row, window, 0)
            query_pos = begin_row + offsets
            key_pos = begin_row - window + key_offsets
            scores, allowed, query_heads, key_heads = band_scores(q_rows, k_rows, id_rows, pos_table, time_table, query_pos, key_pos, length)
            weights = jnp.where(allowed, jax.nn.silu(scores) / window, 0.0).astype(jnp.bfloat16)
            value_heads = v_rows.astype(jnp.float32).reshape(2 * window, heads, head_size)
            return (begin_row, scores, allowed, weights, query_heads, key_heads, value_heads)

        def fwd_block(state, block_index):
            begin_row, scores, allowed, weights, query_heads, key_heads, value_heads = block_setup(block_index)
            mixed = jnp.einsum('hqk,khd->qhd', weights.astype(jnp.float32), value_heads, precision=highest)
            return (state, mixed.reshape(window, width))
        _, mixed_blocks = lax.scan(fwd_block, jnp.zeros((), jnp.float32), jnp.arange(blocks, dtype=jnp.int32))
        attended = mixed_blocks.reshape(seq_len, width)
        att_hat, att_inv = norm_rows(attended)
        gated = (att_hat * gate_u.astype(jnp.float32)).astype(jnp.bfloat16)
        layer_out = (ev_float + jnp.dot(gated, w_out, preferred_element_type=jnp.float32)).astype(jnp.bfloat16)
        upstream = jnp.dot(user_cot, w_out.T, preferred_element_type=jnp.float32)
        part_out = jnp.dot(gated.T, user_cot, preferred_element_type=jnp.float32) * loss_scale
        grad_gate = upstream * att_hat
        grad_att = norm_back(upstream * gate_u.astype(jnp.float32), att_hat, att_inv).astype(jnp.bfloat16)

        def bwd_block(state, block_index):
            grad_keys, grad_values = state
            begin_row, scores, allowed, weights, query_heads, key_heads, value_heads = block_setup(block_index)
            grad_rows = lax.dynamic_slice_in_dim(grad_att, begin_row, window, 0).astype(jnp.float32).reshape(window, heads, head_size)
            grad_weights = jnp.einsum('qhd,khd->hqk', grad_rows, value_heads, precision=highest)
            grad_v = jnp.einsum('hqk,qhd->khd', weights.astype(jnp.float32), grad_rows, precision=highest).reshape(2 * window, width)
            grad_scores = jnp.where(allowed, grad_weights * silu_slope(scores) / window, 0.0).astype(jnp.bfloat16).astype(jnp.float32)
            grad_q = jnp.einsum('hqk,khd->qhd', grad_scores, key_heads, precision=highest) / math.sqrt(head_size)
            grad_k = (jnp.einsum('hqk,qhd->khd', grad_scores, query_heads, precision=highest) / math.sqrt(head_size)).reshape(2 * window, width)
            grad_keys = lax.dynamic_update_slice_in_dim(grad_keys, lax.dynamic_slice_in_dim(grad_keys, begin_row, 2 * window, 0) + grad_k, begin_row, 0)
            grad_values = lax.dynamic_update_slice_in_dim(grad_values, lax.dynamic_slice_in_dim(grad_values, begin_row, 2 * window, 0) + grad_v, begin_row, 0)
            return ((grad_keys, grad_values), grad_q.reshape(window, width))
        empty = jnp.zeros((seq_len + window, width), jnp.float32)
        (grad_keys, grad_values), grad_q_blocks = lax.scan(bwd_block, (empty, empty), jnp.arange(blocks, dtype=jnp.int32))
        grad_pre = (jnp.concatenate([grad_gate, grad_values[window:], grad_q_blocks.reshape(seq_len, width), grad_keys[window:]], axis=1) * silu_slope(pre_act)).astype(jnp.bfloat16)
        part_in = jnp.dot(ev_normed.T, grad_pre, preferred_element_type=jnp.float32) * loss_scale
        part_bias = lax.optimization_barrier(jnp.sum(grad_pre.astype(jnp.float32), axis=0)) * loss_scale
        grad_normed = jnp.dot(grad_pre, w_in.T, preferred_element_type=jnp.float32)
        grad_events = (user_cot.astype(jnp.float32) + norm_back(grad_normed, ev_hat, ev_inv)).astype(jnp.bfloat16)
        totals = (totals[0] + part_in, totals[1] + part_bias, totals[2] + part_out)
        return (totals, (layer_out, grad_events))
    start_totals = (jnp.zeros((width, 4 * width), jnp.float32), jnp.zeros((4 * width,), jnp.float32), jnp.zeros((width, width), jnp.float32))
    totals, (layer_out, grad_events) = lax.scan(per_user, start_totals, (events, cotangent, bucket_ids, history_lengths))
    return (layer_out, grad_events, totals[0], totals[1], totals[2])
```

```python
import functools
import math

import jax
import jax.numpy as jnp
from jax import lax
from jax.experimental import pallas as pl
from jax.experimental.pallas import tpu as pltpu
from jax.sharding import Mesh, PartitionSpec as P

EPS = 1e-05
F32 = jnp.float32
BF16 = jnp.bfloat16
NEAR = ("yl", "yh", "x", "c", "zl")
FAR = ("zh",)
BATCH = ("yl", "zh", "zl")
SEQ = ("yh", "x", "c")
TILE = 16
PIECE = 3 * TILE


def norm_rows(values):
    row_mean = jnp.mean(values, axis=-1, keepdims=True)
    centred = values - row_mean
    variance = jnp.mean(centred * centred, axis=-1, keepdims=True)
    inv_std = lax.rsqrt(variance + EPS)
    return (centred * inv_std, inv_std)


def norm_back(upstream, normed, inv_std):
    first = jnp.mean(upstream, axis=-1, keepdims=True)
    second = jnp.mean(upstream * normed, axis=-1, keepdims=True)
    return inv_std * (upstream - first - normed * second)


def silu_and_slope(pre_act):
    sigmoid = jax.nn.sigmoid(pre_act)
    value = pre_act * sigmoid
    return (value, sigmoid * (1.0 + pre_act * (1.0 - sigmoid)))


def dot(left, right, dims=((1,), (0,))):
    return lax.dot_general(left, right, (dims, ((), ())), preferred_element_type=F32)


ROWS_BY_ROWS = ((1,), (1,))
COLS_BY_COLS = ((0,), (0,))


def lane_gather(table, index):
    return jnp.take_along_axis(table, index, axis=1, mode="promise_in_bounds")


def layer_kernel(
    scale, length_ref, ev_ref, tail_ref, cot_ref, ids_ref, w_in_ref, b_in_ref, w_out_ref,
    pos_ref, time_ref, out_ref, parts_ref, own_ref, back_ref,
):
    rows, width = ev_ref.shape
    heads, window = pos_ref.shape
    head = width // heads
    slab = lax.axis_index(SEQ)
    real = length_ref[0] - slab * rows

    own_hat, _ = norm_rows(ev_ref[...].astype(F32))
    own_normed = own_hat.astype(BF16)
    tail_hat, _ = norm_rows(tail_ref[...].astype(F32))
    tail_normed = tail_hat.astype(BF16)

    def project(normed, first, last):
        columns = slice(first * width, last * width)
        pre_act = dot(normed, w_in_ref[:, columns]) + b_in_ref[:, columns]
        value, slope = silu_and_slope(pre_act)
        return (value.astype(BF16), slope)

    gate, gate_slope = project(own_normed, 0, 1)
    values, values_slope = project(own_normed, 1, 2)
    queries, queries_slope = project(own_normed, 2, 3)
    keys, keys_slope = project(own_normed, 3, 4)
    tail_values, tail_values_slope = project(tail_normed, 1, 2)
    tail_keys, tail_keys_slope = project(tail_normed, 3, 4)

    row = lax.broadcasted_iota(jnp.int32, (window, window), 0)
    lane = lax.broadcasted_iota(jnp.int32, (window, window), 1)
    offset = (row - lane) & (window - 1)
    stacked_row = jnp.concatenate([row] * heads, axis=0)
    stacked_lane = jnp.concatenate([lane] * heads, axis=0)
    recent = stacked_lane <= stacked_row
    pos_bias = [
        lane_gather(jnp.broadcast_to(pos_ref[h : h + 1, :], (window, window)), offset)
        for h in range(heads)
    ]
    times = [jnp.broadcast_to(time_ref[h : h + 1, :], (window, window)) for h in range(heads)]
    column_head = lax.broadcasted_iota(jnp.int32, (window, width), 1) // head

    def by_head(block):
        zero = jnp.zeros_like(block)
        return jnp.concatenate(
            [jnp.where(column_head == h, block, zero) for h in range(heads)], axis=0
        )

    def pick_heads(stack):
        total = stack[:window]
        for h in range(1, heads):
            total = jnp.where(column_head == h, stack[h * window : (h + 1) * window], total)
        return total

    def split_band(band):
        zero = jnp.zeros_like(band)
        return jnp.concatenate(
            [jnp.where(recent, band, zero), jnp.where(recent, zero, band)], axis=1
        ).astype(BF16)

    def join_band(pair):
        return jnp.where(recent, pair[:, :window], pair[:, window:])

    grad_gate, grad_queries, gated_blocks = [], [], []
    grad_keys, grad_values = [], []
    for block in range(rows // window):
        here = slice(block * window, (block + 1) * window)
        if block == 0:
            behind_keys, behind_values = tail_keys, tail_values
            behind_ok = slab > 0
        else:
            before = slice((block - 1) * window, block * window)
            behind_keys, behind_values = keys[before], values[before]
            behind_ok = True
        pair_keys = jnp.concatenate([keys[here], behind_keys], axis=0)
        pair_values = jnp.concatenate([values[here], behind_values], axis=0)
        stack_queries = by_head(queries[here])
        logits = join_band(dot(stack_queries, pair_keys, ROWS_BY_ROWS)) / math.sqrt(head)
        buckets = lane_gather(ids_ref[here, :], offset)
        bias = jnp.concatenate(
            [pos_bias[h] + lane_gather(times[h], buckets) for h in range(heads)], axis=0
        )
        scores = logits + bias
        allowed = stacked_row < real - block * window
        if block == 0:
            allowed = allowed & (recent | behind_ok)
        act, slope = silu_and_slope(scores)
        weights = split_band(jnp.where(allowed, act * (1.0 / window), 0.0))
        attended = pick_heads(dot(weights, pair_values))
        att_hat, att_inv = norm_rows(attended)
        gate_u = gate[here].astype(F32)
        gated = (att_hat * gate_u).astype(BF16)
        gated_blocks.append(gated)
        out_ref[here, :] = (ev_ref[here, :].astype(F32) + dot(gated, w_out_ref[...])).astype(BF16)
        upstream = dot(cot_ref[here, :], w_out_ref[...], ROWS_BY_ROWS)
        grad_gate.append(upstream * att_hat)
        grad_att = by_head(norm_back(upstream * gate_u, att_hat, att_inv).astype(BF16))
        grad_weights = join_band(dot(grad_att, pair_values, ROWS_BY_ROWS))
        grad_scores = split_band(jnp.where(allowed, grad_weights * slope * (1.0 / window), 0.0))
        pair_grad_values = dot(weights, grad_att, COLS_BY_COLS)
        pair_grad_keys = dot(grad_scores, stack_queries, COLS_BY_COLS) / math.sqrt(head)
        grad_queries.append(pick_heads(dot(grad_scores, pair_keys)) / math.sqrt(head))
        if block == 0:
            tail_grad_values = pair_grad_values[window:]
            tail_grad_keys = pair_grad_keys[window:]
        else:
            grad_values[-1] = grad_values[-1] + pair_grad_values[window:]
            grad_keys[-1] = grad_keys[-1] + pair_grad_keys[window:]
        grad_values.append(pair_grad_values[:window])
        grad_keys.append(pair_grad_keys[:window])

    def stacked(blocks):
        return jnp.concatenate(blocks, axis=0)

    own_pre = [
        (stacked(grad_gate) * gate_slope).astype(BF16),
        (stacked(grad_values) * values_slope).astype(BF16),
        (stacked(grad_queries) * queries_slope).astype(BF16),
        (stacked(grad_keys) * keys_slope).astype(BF16),
    ]
    tail_pre = {
        1: (tail_grad_values * tail_values_slope).astype(BF16),
        3: (tail_grad_keys * tail_keys_slope).astype(BF16),
    }
    own_total = None
    back_total = None
    bias_rows = []
    in_blocks = []
    for quarter in range(4):
        columns = slice(quarter * width, (quarter + 1) * width)
        part_in = dot(own_normed, own_pre[quarter], COLS_BY_COLS)
        part_bias = jnp.sum(own_pre[quarter].astype(F32), axis=0, keepdims=True)
        part = dot(own_pre[quarter], w_in_ref[:, columns], ROWS_BY_ROWS)
        own_total = part if own_total is None else own_total + part
        if quarter in tail_pre:
            part_in = part_in + dot(tail_normed, tail_pre[quarter], COLS_BY_COLS)
            part_bias = part_bias + jnp.sum(
                tail_pre[quarter].astype(F32), axis=0, keepdims=True
            )
            part = dot(tail_pre[quarter], w_in_ref[:, columns], ROWS_BY_ROWS)
            back_total = part if back_total is None else back_total + part
        in_blocks.append((part_in * scale).astype(BF16))
        bias_rows.append(part_bias * scale)
    own_ref[...] = own_total
    back_ref[...] = back_total
    part_out = dot(stacked(gated_blocks), cot_ref[...], COLS_BY_COLS) * scale

    low = lax.broadcasted_iota(jnp.int32, (TILE, 2 * 64), 1) < 64
    for quarter in range(4):
        half = part_out[:, (quarter // 2) * 128 : (quarter // 2 + 1) * 128]
        if quarter % 2:
            half = pltpu.roll(half, 64, 1)
        for group in range(16):
            piece = group * 4 + quarter
            here = slice(group * TILE, (group + 1) * TILE)
            for k in range(2):
                parts_ref[piece, k * TILE : (k + 1) * TILE, :] = in_blocks[quarter][
                    here, k * 128 : (k + 1) * 128
                ]
            if piece < 16:
                chunk = bias_rows[piece // 4][:, (piece // 2 % 2) * 128 : (piece // 2 % 2 + 1) * 128]
                if piece % 2 == 0:
                    chunk = pltpu.roll(chunk, 64, 1)
                chunk = jnp.broadcast_to(chunk, (TILE, 128))
            else:
                chunk = jnp.zeros((TILE, 128), F32)
            parts_ref[piece, 2 * TILE :, :] = jnp.where(low, half[here], chunk).astype(BF16)


def near_kernel(parts_ref, own_ref, back_ref, ev_ref, cot_ref, sum_ref, grad_ref):
    total = parts_ref[0].astype(F32)
    for i in range(1, parts_ref.shape[0]):
        total = total + parts_ref[i].astype(F32)
    for i in range(sum_ref.shape[0]):
        sum_ref[i] = total
    rows = ev_ref.shape[0]
    window = back_ref.shape[0]
    hat, inv = norm_rows(ev_ref[...].astype(F32))
    grad = jnp.concatenate(
        [own_ref[: rows - window, :], own_ref[rows - window :, :] + back_ref[...]], axis=0
    )
    grad_ref[...] = (cot_ref[...].astype(F32) + norm_back(grad, hat, inv)).astype(BF16)


def far_kernel(parts_ref, sum_ref):
    total = parts_ref[0]
    for i in range(1, parts_ref.shape[0]):
        total = total + parts_ref[i]
    total = total.astype(BF16)
    for i in range(sum_ref.shape[0]):
        sum_ref[i] = total


def unpack_kernel(all_ref, w_in_ref, b_in_ref, w_out_ref):
    for group in range(16):
        here = slice(group * TILE, (group + 1) * TILE)
        tiles = []
        for quarter in range(4):
            piece = group * 4 + quarter
            for k in range(2):
                first = quarter * 256 + k * 128
                w_in_ref[here, first : first + 128] = all_ref[
                    piece, k * TILE : (k + 1) * TILE, :
                ].astype(F32)
            tiles.append(all_ref[piece, 2 * TILE :, :].astype(F32))
        low = lax.broadcasted_iota(jnp.int32, (TILE, 128), 1) < 64
        for k in range(2):
            w_out_ref[here, k * 128 : (k + 1) * 128] = jnp.where(
                low, tiles[2 * k], pltpu.roll(tiles[2 * k + 1], 64, 1)
            )
        if group < 4:
            for k in range(2):
                b_in_ref[group * 2 + k : group * 2 + k + 1, :] = jnp.where(
                    low, pltpu.roll(tiles[2 * k], 64, 1), tiles[2 * k + 1]
                )[:1, :]


def call(kernel, outs, *args, scalars=0):
    return pl.pallas_call(
        kernel,
        out_shape=[jax.ShapeDtypeStruct(shape, kind) for shape, kind in outs],
        in_specs=[
            pl.BlockSpec(memory_space=pltpu.SMEM if i < scalars else pltpu.VMEM)
            for i in range(len(args))
        ],
        out_specs=[pl.BlockSpec(memory_space=pltpu.VMEM)] * len(outs),
        compiler_params=pltpu.CompilerParams(vmem_limit_bytes=48 * 1024 * 1024),
    )(*args)


def on_device(
    events, cotangent, bucket_ids, history_lengths, w_in, b_in, w_out, pos_table, time_table
):
    rows, width = events.shape[1:]
    window = pos_table.shape[1]
    slabs = lax.axis_size(SEQ)
    scale = 1.0 / math.sqrt(lax.axis_size(BATCH) * slabs * rows)
    own_events, own_cot = events[0], cotangent[0]
    near, far = lax.axis_size(NEAR), lax.axis_size(FAR)
    tail = lax.ppermute(
        own_events[rows - window :], SEQ, [(i, i + 1) for i in range(slabs - 1)]
    )
    layer_out, parts, own_grad, back_grad = call(
        functools.partial(layer_kernel, scale),
        [
            ((rows, width), BF16),
            ((near, PIECE, 128), BF16),
            ((rows, width), F32),
            ((window, width), F32),
        ],
        history_lengths, own_events, tail, own_cot, bucket_ids[0], w_in, b_in[None], w_out,
        pos_table, time_table,
        scalars=1,
    )
    back = lax.ppermute(back_grad, SEQ, [(i, i - 1) for i in range(1, slabs)])
    parts = lax.all_to_all(parts, NEAR, 0, 0)
    far_parts, grad_events = call(
        near_kernel,
        [((far, PIECE, 128), F32), ((rows, width), BF16)],
        parts, own_grad, back, own_events, own_cot,
    )
    far_parts = lax.all_to_all(far_parts, FAR, 0, 0)
    (sums,) = call(far_kernel, [((near, PIECE, 128), BF16)], far_parts)
    sums = lax.all_to_all(sums, NEAR, 0, 0)
    sum_in, sum_bias, sum_out = call(
        unpack_kernel, [((width, 4 * width), F32), ((8, 128), F32), ((width, width), F32)], sums
    )
    return (layer_out[None], grad_events[None], sum_in, sum_bias.reshape(4 * width), sum_out)


def solution(mesh):
    fine = Mesh(
        mesh.devices.reshape(2, 8, 2, 2, 4, 2), ("yl", "zh", "zl", "yh", "x", "c")
    )
    slabs = P(BATCH, SEQ, None)
    return jax.shard_map(
        on_device,
        mesh=fine,
        in_specs=(slabs, slabs, slabs, P(BATCH), P(), P(), P(), P(), P()),
        out_specs=(slabs, slabs, P(), P(), P()),
        check_vma=False,
    )
```

```python
import functools
import math

import jax
import jax.numpy as jnp
from jax import lax
from jax.experimental import pallas as pl
from jax.experimental.pallas import tpu as pltpu
from jax.sharding import Mesh, PartitionSpec as P

EPS = 1e-05
F32 = jnp.float32
BF16 = jnp.bfloat16
NEAR = ("yl", "yh", "x", "c", "zl")
FAR = ("zh",)
BATCH = ("yl", "zh", "zl")
SEQ = ("yh", "x", "c")
GROUP = 8
PIECE = 5 * GROUP


def norm_rows(values):
    row_mean = jnp.mean(values, axis=-1, keepdims=True)
    centred = values - row_mean
    variance = jnp.mean(centred * centred, axis=-1, keepdims=True)
    inv_std = lax.rsqrt(variance + EPS)
    return (centred * inv_std, inv_std)


def norm_back(upstream, normed, inv_std):
    first = jnp.mean(upstream, axis=-1, keepdims=True)
    second = jnp.mean(upstream * normed, axis=-1, keepdims=True)
    return inv_std * (upstream - first - normed * second)


def silu_and_slope(pre_act):
    sigmoid = jax.nn.sigmoid(pre_act)
    value = pre_act * sigmoid
    return (value, sigmoid * (1.0 + pre_act * (1.0 - sigmoid)))


def dot(left, right, dims=((1,), (0,))):
    return lax.dot_general(left, right, (dims, ((), ())), preferred_element_type=F32)


ROWS_BY_ROWS = ((1,), (1,))
COLS_BY_COLS = ((0,), (0,))


def lane_gather(table, index):
    return jnp.take_along_axis(table, index, axis=1, mode="promise_in_bounds")


class Band:
    def __init__(self, heads, window, width):
        self.heads, self.window, self.head = heads, window, width // heads
        row = lax.broadcasted_iota(jnp.int32, (window, window), 0)
        lane = lax.broadcasted_iota(jnp.int32, (window, window), 1)
        self.offset = (row - lane) & (window - 1)
        self.row = jnp.concatenate([row] * heads, axis=0)
        self.recent = jnp.concatenate([lane <= row] * heads, axis=0)
        self.column_head = lax.broadcasted_iota(jnp.int32, (window, width), 1) // self.head

    def bias(self, bucket_rows, pos_ref, time_ref):
        shape = (self.window, self.window)
        buckets = lane_gather(bucket_rows, self.offset)
        return jnp.concatenate(
            [
                lane_gather(jnp.broadcast_to(pos_ref[h : h + 1, :], shape), self.offset)
                + lane_gather(jnp.broadcast_to(time_ref[h : h + 1, :], shape), buckets)
                for h in range(self.heads)
            ],
            axis=0,
        )

    def by_head(self, block):
        zero = jnp.zeros_like(block)
        return jnp.concatenate(
            [jnp.where(self.column_head == h, block, zero) for h in range(self.heads)], axis=0
        )

    def pick_heads(self, stack):
        total = stack[: self.window]
        for h in range(1, self.heads):
            part = stack[h * self.window : (h + 1) * self.window]
            total = jnp.where(self.column_head == h, part, total)
        return total

    def split(self, band):
        zero = jnp.zeros_like(band)
        return jnp.concatenate(
            [jnp.where(self.recent, band, zero), jnp.where(self.recent, zero, band)], axis=1
        ).astype(BF16)

    def join(self, pair):
        return jnp.where(self.recent, pair[:, : self.window], pair[:, self.window :])

    def block(self, queries, pair_keys, pair_values, gate, bias, allowed, ev, cot, w_out):
        root = math.sqrt(self.head)
        stack_queries = self.by_head(queries)
        scores = self.join(dot(stack_queries, pair_keys, ROWS_BY_ROWS)) / root + bias
        act, slope = silu_and_slope(scores)
        weights = self.split(jnp.where(allowed, act * (1.0 / self.window), 0.0))
        att_hat, att_inv = norm_rows(self.pick_heads(dot(weights, pair_values)))
        gate_u = gate.astype(F32)
        gated = (att_hat * gate_u).astype(BF16)
        out = (ev.astype(F32) + dot(gated, w_out)).astype(BF16)
        upstream = dot(cot, w_out, ROWS_BY_ROWS)
        grad_att = self.by_head(norm_back(upstream * gate_u, att_hat, att_inv).astype(BF16))
        grad_weights = self.join(dot(grad_att, pair_values, ROWS_BY_ROWS))
        grad_scores = self.split(
            jnp.where(allowed, grad_weights * slope * (1.0 / self.window), 0.0)
        )
        grad_values = dot(weights, grad_att, COLS_BY_COLS)
        grad_queries = self.pick_heads(dot(grad_scores, pair_keys)) / root
        grad_keys = dot(grad_scores, stack_queries, COLS_BY_COLS) / root
        return (out, gated, upstream * att_hat, grad_values, grad_queries, grad_keys)


def own_kernel(
    length_ref, ev_hbm, cot_hbm, ids_hbm, w_in_hbm, b_in_hbm, w_out_hbm, pos_hbm, time_hbm,
    out_ref, gated_ref, pre_ref, own_ref, normed_ref, proj_ref, slope_ref, bias_ref, grads_ref,
    ev_ref, cot_ref, w_in_ref, b_in_ref, w_out_ref,
    ids_ref, pos_ref, time_ref, sems,
):
    pairs = [
        (ev_hbm, ev_ref), (w_in_hbm, w_in_ref), (b_in_hbm, b_in_ref), (ids_hbm, ids_ref),
        (pos_hbm, pos_ref), (time_hbm, time_ref), (cot_hbm, cot_ref), (w_out_hbm, w_out_ref),
    ]
    copies = [pltpu.make_async_copy(a, b, sems.at[i]) for i, (a, b) in enumerate(pairs)]
    for copy in copies:
        copy.start()
    rows, width = ev_ref.shape
    heads, window = pos_ref.shape
    real = length_ref[0] - lax.axis_index(SEQ) * rows
    band = Band(heads, window, width)
    copies[0].wait()
    hat, _ = norm_rows(ev_ref[...].astype(F32))
    normed = hat.astype(BF16)
    normed_ref[...] = normed
    copies[1].wait()
    copies[2].wait()
    value, slope = silu_and_slope(dot(normed, w_in_ref[...]) + b_in_ref[...])
    projected = value.astype(BF16)
    first, last = slice(0, window), slice(window, 2 * window)
    proj_ref[...] = projected[first]
    slope_ref[...] = slope[first]
    gate, values, queries, keys = [projected[:, i * width : (i + 1) * width] for i in range(4)]
    for copy in copies[3:6]:
        copy.wait()
    bias_ref[...] = band.bias(ids_ref[first, :], pos_ref, time_ref)
    bias = band.bias(ids_ref[last, :], pos_ref, time_ref)
    copies[6].wait()
    copies[7].wait()
    out, gated, grad_gate, grad_values, grad_queries, grad_keys = band.block(
        queries[last],
        jnp.concatenate([keys[last], keys[first]], axis=0),
        jnp.concatenate([values[last], values[first]], axis=0),
        gate[last], bias, band.row < real - window, ev_ref[last, :], cot_ref[last, :],
        w_out_ref[...],
    )
    out_ref[...] = out
    gated_ref[...] = gated
    grads_ref[:, :width] = grad_values[window:]
    grads_ref[:, width:] = grad_keys[window:]
    grads = jnp.concatenate(
        [grad_gate, grad_values[:window], grad_queries, grad_keys[:window]], axis=1
    )
    pre = (grads * slope[last]).astype(BF16)
    pre_ref[...] = pre
    own_ref[...] = dot(pre, w_in_ref[...], ROWS_BY_ROWS)


def edge_kernel(
    scale, length_ref, moved_ref, out_last_ref, gated_ref, pre_ref, normed_ref, proj_ref,
    slope_ref, bias_ref, grads_ref, ev_ref, cot_ref, w_in_ref, b_in_ref, w_out_ref,
    out_ref, parts_ref, bias_out_ref, own_ref, back_ref,
):
    rows, width = ev_ref.shape
    window = out_last_ref.shape[0]
    heads = bias_ref.shape[0] // window
    slab = lax.axis_index(SEQ)
    real = length_ref[0] - slab * rows
    band = Band(heads, window, width)
    first, last = slice(0, window), slice(window, 2 * window)
    tail_hat, _ = norm_rows(moved_ref[0, rows - window :, :].astype(F32))
    tail_normed = tail_hat.astype(BF16)

    def columns(i):
        return slice(i * width, (i + 1) * width)

    def project(i):
        pre_act = dot(tail_normed, w_in_ref[:, columns(i)]) + b_in_ref[:, columns(i)]
        value, slope = silu_and_slope(pre_act)
        return (value.astype(BF16), slope)

    tail_values, tail_values_slope = project(1)
    tail_keys, tail_keys_slope = project(3)
    gate, values, queries, keys = [proj_ref[:, columns(i)] for i in range(4)]
    out, gated, grad_gate, grad_values, grad_queries, grad_keys = band.block(
        queries,
        jnp.concatenate([keys, tail_keys], axis=0),
        jnp.concatenate([values, tail_values], axis=0),
        gate, bias_ref[...], (band.row < real) & (band.recent | (slab > 0)),
        ev_ref[first, :], cot_ref[first, :], w_out_ref[...],
    )
    out_ref[first, :] = out
    out_ref[last, :] = out_last_ref[...]
    grads = [
        grad_gate,
        grad_values[:window] + grads_ref[:, :width],
        grad_queries,
        grad_keys[:window] + grads_ref[:, width:],
    ]
    tail_pre = {
        1: (grad_values[window:] * tail_values_slope).astype(BF16),
        3: (grad_keys[window:] * tail_keys_slope).astype(BF16),
    }
    left = jnp.concatenate([normed_ref[...], tail_normed], axis=0)
    own_total, back_total, in_blocks, bias_rows = None, None, [], []
    for i in range(4):
        own_pre = (grads[i] * slope_ref[:, columns(i)]).astype(BF16)
        part = dot(own_pre, w_in_ref[:, columns(i)], ROWS_BY_ROWS)
        own_total = part if own_total is None else own_total + part
        right = [own_pre, pre_ref[:, columns(i)]]
        if i in tail_pre:
            part = dot(tail_pre[i], w_in_ref[:, columns(i)], ROWS_BY_ROWS)
            back_total = part if back_total is None else back_total + part
            right.append(tail_pre[i])
        right = jnp.concatenate(right, axis=0)
        in_blocks.append(dot(left[: right.shape[0]], right, COLS_BY_COLS) * scale)
        bias_rows.append(jnp.sum(right.astype(F32), axis=0, keepdims=True) * scale)
    own_ref[...] = own_total
    back_ref[...] = back_total
    part_out = dot(
        jnp.concatenate([gated, gated_ref[...]], axis=0), cot_ref[...], COLS_BY_COLS
    ) * scale
    for i in range(8):
        bias_out_ref[i : i + 1, :] = bias_rows[i // 2][:, (i % 2) * 128 : (i % 2 + 1) * 128]
    for group in range(width // GROUP):
        here = slice(group * GROUP, (group + 1) * GROUP)
        for half in range(2):
            tiles = [
                in_blocks[2 * half + k // 2][here, (k % 2) * 128 : (k % 2 + 1) * 128]
                for k in range(4)
            ]
            tiles.append(part_out[here, half * 128 : (half + 1) * 128])
            parts_ref[2 * group + half] = jnp.concatenate(tiles, axis=0).astype(BF16)


def near_kernel(parts_ref, bias_ref, sum_ref):
    total = parts_ref[0].astype(F32)
    for i in range(1, parts_ref.shape[0]):
        total = total + parts_ref[i].astype(F32)
    sums = jnp.concatenate([total, bias_ref[...]], axis=0).astype(BF16)
    for i in range(sum_ref.shape[0]):
        sum_ref[i] = sums


def far_kernel(parts_ref, sum_ref):
    total = parts_ref[0].astype(F32)
    for i in range(1, parts_ref.shape[0]):
        total = total + parts_ref[i].astype(F32)
    sums = total.astype(BF16)
    for i in range(sum_ref.shape[0]):
        sum_ref[i] = sums


def unpack_kernel(all_ref, w_in_ref, b_in_ref, w_out_ref):
    bias = None
    for piece in range(all_ref.shape[0]):
        rows = all_ref[piece].astype(F32)
        group, half = piece // 2, piece % 2
        here = slice(group * GROUP, (group + 1) * GROUP)
        tiles = [rows[k * GROUP : (k + 1) * GROUP] for k in range(6)]
        w_in_ref[here, half * 512 : (half + 1) * 512] = jnp.concatenate(tiles[:4], axis=1)
        w_out_ref[here, half * 128 : (half + 1) * 128] = tiles[4]
        bias = tiles[5] if bias is None else bias + tiles[5]
    b_in_ref[...] = bias


def grad_kernel(own_first_ref, own_last_ref, back_ref, ev_ref, cot_ref, grad_ref):
    window = back_ref.shape[0]
    for half, grad in enumerate((own_first_ref[...], own_last_ref[...] + back_ref[...])):
        here = slice(half * window, (half + 1) * window)
        hat, inv = norm_rows(ev_ref[here, :].astype(F32))
        grad_ref[here, :] = (cot_ref[here, :].astype(F32) + norm_back(grad, hat, inv)).astype(BF16)


def call(kernel, outs, *args, spaces=None, scratch=(), flops=0, moved=0):
    spaces = spaces or [pltpu.VMEM] * len(args)
    args = [
        pltpu.with_memory_space_constraint(arg, space) if space == pltpu.HBM else arg
        for arg, space in zip(args, spaces)
    ]
    return pl.pallas_call(
        kernel,
        out_shape=[
            pltpu.VMEM(shape, kind) if kept else jax.ShapeDtypeStruct(shape, kind)
            for shape, kind, *kept in outs
        ],
        in_specs=[pl.BlockSpec(memory_space=space) for space in spaces],
        out_specs=[pl.BlockSpec(memory_space=pltpu.VMEM)] * len(outs),
        scratch_shapes=scratch,
        compiler_params=pltpu.CompilerParams(vmem_limit_bytes=24 * 1024 * 1024),
        cost_estimate=pl.CostEstimate(flops=flops, bytes_accessed=moved, transcendentals=0),
    )(*args)


def on_device(
    events, cotangent, bucket_ids, history_lengths, w_in, b_in, w_out, pos_table, time_table
):
    rows, width = events.shape[1:]
    heads, window = pos_table.shape
    slabs = lax.axis_size(SEQ)
    scale = 1.0 / math.sqrt(lax.axis_size(BATCH) * slabs * rows)
    near, far = lax.axis_size(NEAR), lax.axis_size(FAR)
    moved = lax.ppermute(events, SEQ, [(i, i + 1) for i in range(slabs - 1)])
    half = (window, width)
    (
        out_last, gated, pre, own_last, normed, proj, slope, bias, grads, ev, cot, w_in_near,
        b_in_near, w_out_near,
    ) = call(
        own_kernel,
        [
            (half, BF16), (half, BF16), ((window, 4 * width), BF16), (half, F32),
            ((rows, width), BF16), ((window, 4 * width), BF16), ((window, 4 * width), F32),
            ((heads * window, window), F32), ((window, 2 * width), F32), ((rows, width), BF16),
            ((rows, width), BF16), (w_in.shape, BF16), ((1, 4 * width), F32), (w_out.shape, BF16),
        ],
        history_lengths, events[0], cotangent[0], bucket_ids[0], w_in, b_in[None], w_out,
        pos_table, time_table,
        spaces=[pltpu.SMEM] + [pltpu.HBM] * 8,
        scratch=[
            pltpu.VMEM((rows, window), jnp.int32),
            pltpu.VMEM(pos_table.shape, F32),
            pltpu.VMEM(time_table.shape, F32),
            pltpu.SemaphoreType.DMA((8,)),
        ],
        flops=10**9, moved=10**7,
    )
    layer_out, parts, bias_part, own_first, back = call(
        functools.partial(edge_kernel, scale),
        [
            ((rows, width), BF16), ((near, PIECE, 128), BF16), ((8, 128), F32), (half, F32),
            (half, F32),
        ],
        history_lengths, moved, out_last, gated, pre, normed, proj, slope, bias, grads, ev, cot,
        w_in_near, b_in_near, w_out_near,
        spaces=[pltpu.SMEM] + [pltpu.VMEM] * 14,
        flops=10**9, moved=10**7,
    )
    back = lax.ppermute(back, SEQ, [(i, i - 1) for i in range(1, slabs)])
    parts = lax.all_to_all(parts, NEAR, 0, 0)
    (grad_events,) = call(
        grad_kernel, [((rows, width), BF16)], own_first, own_last, back, ev, cot,
        flops=10**7, moved=10**6,
    )
    (sums,) = call(near_kernel, [((far, PIECE + GROUP, 128), BF16)], parts, bias_part)
    sums = lax.all_to_all(sums, FAR, 0, 0)
    (sums,) = call(far_kernel, [((near, PIECE + GROUP, 128), BF16)], sums)
    sums = lax.all_to_all(sums, NEAR, 0, 0)
    sum_in, sum_bias, sum_out = call(
        unpack_kernel, [((width, 4 * width), F32), ((8, 128), F32), ((width, width), F32)], sums
    )
    return (layer_out[None], grad_events[None], sum_in, sum_bias.reshape(4 * width), sum_out)


def solution(mesh):
    fine = Mesh(
        mesh.devices.reshape(2, 8, 2, 2, 4, 2), ("yl", "zh", "zl", "yh", "x", "c")
    )
    slabs = P(BATCH, SEQ, None)
    return jax.shard_map(
        on_device,
        mesh=fine,
        in_specs=(slabs, slabs, slabs, P(BATCH), P(), P(), P(), P(), P()),
        out_specs=(slabs, slabs, P(), P(), P()),
        check_vma=False,
    )
```

```python
import functools
import math

import jax
import jax.numpy as jnp
from jax import lax
from jax.experimental import pallas as pl
from jax.experimental.pallas import tpu as pltpu
from jax.sharding import Mesh, PartitionSpec as P

EPS = 1e-05
F32 = jnp.float32
BF16 = jnp.bfloat16
NEAR = ("yl", "yh", "x", "c", "zl")
FAR = ("zh",)
BATCH = ("yl", "zh", "zl")
SEQ = ("yh", "x", "c")
GROUP = 8
PIECE = 5 * GROUP
KEPT = True


def norm_rows(values):
    row_mean = jnp.mean(values, axis=-1, keepdims=True)
    centred = values - row_mean
    variance = jnp.mean(centred * centred, axis=-1, keepdims=True)
    inv_std = lax.rsqrt(variance + EPS)
    return (centred * inv_std, inv_std)


def norm_back(upstream, normed, inv_std):
    first = jnp.mean(upstream, axis=-1, keepdims=True)
    second = jnp.mean(upstream * normed, axis=-1, keepdims=True)
    return inv_std * (upstream - first - normed * second)


def silu_and_slope(pre_act):
    sigmoid = jax.nn.sigmoid(pre_act)
    value = pre_act * sigmoid
    return (value, sigmoid * (1.0 + pre_act * (1.0 - sigmoid)))


def dot(left, right, dims=((1,), (0,))):
    return lax.dot_general(left, right, (dims, ((), ())), preferred_element_type=F32)


ROWS_BY_ROWS = ((1,), (1,))
COLS_BY_COLS = ((0,), (0,))


def lane_gather(table, index):
    return jnp.take_along_axis(table, index, axis=1, mode="promise_in_bounds")


class Band:
    def __init__(self, heads, window, width):
        self.heads, self.window, self.head = heads, window, width // heads
        row = lax.broadcasted_iota(jnp.int32, (window, window), 0)
        lane = lax.broadcasted_iota(jnp.int32, (window, window), 1)
        self.offset = (row - lane) & (window - 1)
        self.row = jnp.concatenate([row] * heads, axis=0)
        self.recent = jnp.concatenate([lane <= row] * heads, axis=0)
        self.column_head = lax.broadcasted_iota(jnp.int32, (window, width), 1) // self.head

    def bias(self, bucket_rows, pos_ref, time_ref):
        shape = (self.window, self.window)
        buckets = lane_gather(bucket_rows, self.offset)
        return jnp.concatenate(
            [
                lane_gather(jnp.broadcast_to(pos_ref[h : h + 1, :], shape), self.offset)
                + lane_gather(jnp.broadcast_to(time_ref[h : h + 1, :], shape), buckets)
                for h in range(self.heads)
            ],
            axis=0,
        )

    def by_head(self, block):
        zero = jnp.zeros_like(block)
        return jnp.concatenate(
            [jnp.where(self.column_head == h, block, zero) for h in range(self.heads)], axis=0
        )

    def pick_heads(self, stack):
        total = stack[: self.window]
        for h in range(1, self.heads):
            part = stack[h * self.window : (h + 1) * self.window]
            total = jnp.where(self.column_head == h, part, total)
        return total

    def split(self, band):
        zero = jnp.zeros_like(band)
        return jnp.concatenate(
            [jnp.where(self.recent, band, zero), jnp.where(self.recent, zero, band)], axis=1
        ).astype(BF16)

    def join(self, pair):
        return jnp.where(self.recent, pair[:, : self.window], pair[:, self.window :])

    def block(self, queries, pair_keys, pair_values, gate, bias, allowed, ev, cot, w_out):
        root = math.sqrt(self.head)
        stack_queries = self.by_head(queries)
        scores = self.join(dot(stack_queries, pair_keys, ROWS_BY_ROWS)) / root + bias
        act, slope = silu_and_slope(scores)
        weights = self.split(jnp.where(allowed, act * (1.0 / self.window), 0.0))
        att_hat, att_inv = norm_rows(self.pick_heads(dot(weights, pair_values)))
        gate_u = gate.astype(F32)
        gated = (att_hat * gate_u).astype(BF16)
        out = (ev.astype(F32) + dot(gated, w_out)).astype(BF16)
        upstream = dot(cot, w_out, ROWS_BY_ROWS)
        grad_att = self.by_head(norm_back(upstream * gate_u, att_hat, att_inv).astype(BF16))
        grad_weights = self.join(dot(grad_att, pair_values, ROWS_BY_ROWS))
        grad_scores = self.split(
            jnp.where(allowed, grad_weights * slope * (1.0 / self.window), 0.0)
        )
        grad_values = dot(weights, grad_att, COLS_BY_COLS)
        grad_queries = self.pick_heads(dot(grad_scores, pair_keys)) / root
        grad_keys = dot(grad_scores, stack_queries, COLS_BY_COLS) / root
        return (out, gated, upstream * att_hat, grad_values, grad_queries, grad_keys)


def own_kernel(
    length_ref, ev_hbm, cot_hbm, ids_hbm, w_in_hbm, b_in_hbm, w_out_hbm, pos_hbm, time_hbm,
    out_ref, gated_ref, pre_ref, own_ref, normed_ref, proj_ref, slope_ref, bias_ref, grads_ref,
    ev_ref, cot_ref, w_in_ref, b_in_ref, w_out_ref,
    ids_ref, pos_ref, time_ref, sems,
):
    pairs = [
        (ev_hbm, ev_ref), (w_in_hbm, w_in_ref), (b_in_hbm, b_in_ref), (ids_hbm, ids_ref),
        (pos_hbm, pos_ref), (time_hbm, time_ref), (cot_hbm, cot_ref), (w_out_hbm, w_out_ref),
    ]
    copies = [pltpu.make_async_copy(a, b, sems.at[i]) for i, (a, b) in enumerate(pairs)]
    for copy in copies:
        copy.start()
    rows, width = ev_ref.shape
    heads, window = pos_ref.shape
    real = length_ref[0] - lax.axis_index(SEQ) * rows
    band = Band(heads, window, width)
    copies[0].wait()
    hat, _ = norm_rows(ev_ref[...].astype(F32))
    normed = hat.astype(BF16)
    normed_ref[...] = normed
    copies[1].wait()
    copies[2].wait()
    value, slope = silu_and_slope(dot(normed, w_in_ref[...]) + b_in_ref[...])
    projected = value.astype(BF16)
    first, last = slice(0, window), slice(window, 2 * window)
    proj_ref[...] = projected[first]
    slope_ref[...] = slope[first]
    gate, values, queries, keys = [projected[:, i * width : (i + 1) * width] for i in range(4)]
    for copy in copies[3:6]:
        copy.wait()
    bias_ref[...] = band.bias(ids_ref[first, :], pos_ref, time_ref)
    bias = band.bias(ids_ref[last, :], pos_ref, time_ref)
    copies[6].wait()
    copies[7].wait()
    out, gated, grad_gate, grad_values, grad_queries, grad_keys = band.block(
        queries[last],
        jnp.concatenate([keys[last], keys[first]], axis=0),
        jnp.concatenate([values[last], values[first]], axis=0),
        gate[last], bias, band.row < real - window, ev_ref[last, :], cot_ref[last, :],
        w_out_ref[...],
    )
    out_ref[...] = out
    gated_ref[...] = gated
    grads_ref[:, :width] = grad_values[window:]
    grads_ref[:, width:] = grad_keys[window:]
    grads = jnp.concatenate(
        [grad_gate, grad_values[:window], grad_queries, grad_keys[:window]], axis=1
    )
    pre = (grads * slope[last]).astype(BF16)
    pre_ref[...] = pre
    own_ref[...] = dot(pre, w_in_ref[...], ROWS_BY_ROWS)


def edge_kernel(
    scale, length_ref, moved_ref, out_last_ref, gated_ref, pre_ref, normed_ref, proj_ref,
    slope_ref, bias_ref, grads_ref, ev_ref, cot_ref, w_in_ref, b_in_ref, w_out_ref,
    out_ref, parts_ref, bias_out_ref, own_ref, back_ref,
):
    rows, width = ev_ref.shape
    window = out_last_ref.shape[0]
    heads = bias_ref.shape[0] // window
    slab = lax.axis_index(SEQ)
    real = length_ref[0] - slab * rows
    band = Band(heads, window, width)
    first, last = slice(0, window), slice(window, 2 * window)
    tail_hat, _ = norm_rows(moved_ref[0, rows - window :, :].astype(F32))
    tail_normed = tail_hat.astype(BF16)

    def columns(i):
        return slice(i * width, (i + 1) * width)

    def project(i):
        pre_act = dot(tail_normed, w_in_ref[:, columns(i)]) + b_in_ref[:, columns(i)]
        value, slope = silu_and_slope(pre_act)
        return (value.astype(BF16), slope)

    tail_values, tail_values_slope = project(1)
    tail_keys, tail_keys_slope = project(3)
    gate, values, queries, keys = [proj_ref[:, columns(i)] for i in range(4)]
    out, gated, grad_gate, grad_values, grad_queries, grad_keys = band.block(
        queries,
        jnp.concatenate([keys, tail_keys], axis=0),
        jnp.concatenate([values, tail_values], axis=0),
        gate, bias_ref[...], (band.row < real) & (band.recent | (slab > 0)),
        ev_ref[first, :], cot_ref[first, :], w_out_ref[...],
    )
    out_ref[first, :] = out
    out_ref[last, :] = out_last_ref[...]
    grads = [
        grad_gate,
        grad_values[:window] + grads_ref[:, :width],
        grad_queries,
        grad_keys[:window] + grads_ref[:, width:],
    ]
    tail_pre = {
        1: (grad_values[window:] * tail_values_slope).astype(BF16),
        3: (grad_keys[window:] * tail_keys_slope).astype(BF16),
    }
    left = jnp.concatenate([normed_ref[...], tail_normed], axis=0)
    own_total, back_total, in_blocks, bias_rows = None, None, [], []
    for i in range(4):
        own_pre = (grads[i] * slope_ref[:, columns(i)]).astype(BF16)
        part = dot(own_pre, w_in_ref[:, columns(i)], ROWS_BY_ROWS)
        own_total = part if own_total is None else own_total + part
        right = [own_pre, pre_ref[:, columns(i)]]
        if i in tail_pre:
            part = dot(tail_pre[i], w_in_ref[:, columns(i)], ROWS_BY_ROWS)
            back_total = part if back_total is None else back_total + part
            right.append(tail_pre[i])
        right = jnp.concatenate(right, axis=0)
        in_blocks.append(dot(left[: right.shape[0]], right, COLS_BY_COLS) * scale)
        bias_rows.append(jnp.sum(right.astype(F32), axis=0, keepdims=True) * scale)
    own_ref[...] = own_total
    back_ref[...] = back_total
    part_out = dot(
        jnp.concatenate([gated, gated_ref[...]], axis=0), cot_ref[...], COLS_BY_COLS
    ) * scale
    for i in range(8):
        bias_out_ref[i : i + 1, :] = bias_rows[i // 2][:, (i % 2) * 128 : (i % 2 + 1) * 128]
    for group in range(width // GROUP):
        here = slice(group * GROUP, (group + 1) * GROUP)
        for half in range(2):
            tiles = [
                in_blocks[2 * half + k // 2][here, (k % 2) * 128 : (k % 2 + 1) * 128]
                for k in range(4)
            ]
            tiles.append(part_out[here, half * 128 : (half + 1) * 128])
            parts_ref[2 * group + half] = jnp.concatenate(tiles, axis=0).astype(BF16)


def near_kernel(parts_ref, bias_ref, back_ref, sum_ref, back_out_ref):
    back_out_ref[...] = back_ref[...]
    total = parts_ref[0].astype(F32)
    for i in range(1, parts_ref.shape[0]):
        total = total + parts_ref[i].astype(F32)
    sums = jnp.concatenate([total, bias_ref[...]], axis=0).astype(BF16)
    for i in range(sum_ref.shape[0]):
        sum_ref[i] = sums


def far_kernel(
    parts_ref, own_first_ref, own_last_ref, back_ref, ev_ref, cot_ref, sum_ref, grad_ref
):
    total = parts_ref[0].astype(F32)
    for i in range(1, parts_ref.shape[0]):
        total = total + parts_ref[i].astype(F32)
    sums = total.astype(BF16)
    for i in range(sum_ref.shape[0]):
        sum_ref[i] = sums
    window = back_ref.shape[0]
    for half, grad in enumerate((own_first_ref[...], own_last_ref[...] + back_ref[...])):
        here = slice(half * window, (half + 1) * window)
        hat, inv = norm_rows(ev_ref[here, :].astype(F32))
        grad_ref[here, :] = (cot_ref[here, :].astype(F32) + norm_back(grad, hat, inv)).astype(BF16)


def unpack_kernel(all_ref, w_in_ref, b_in_ref, w_out_ref):
    bias = None
    for piece in range(all_ref.shape[0]):
        rows = all_ref[piece].astype(F32)
        group, half = piece // 2, piece % 2
        here = slice(group * GROUP, (group + 1) * GROUP)
        tiles = [rows[k * GROUP : (k + 1) * GROUP] for k in range(6)]
        w_in_ref[here, half * 512 : (half + 1) * 512] = jnp.concatenate(tiles[:4], axis=1)
        w_out_ref[here, half * 128 : (half + 1) * 128] = tiles[4]
        bias = tiles[5] if bias is None else bias + tiles[5]
    b_in_ref[...] = bias


def call(kernel, outs, *args, spaces=None, scratch=(), flops=0, moved=0):
    spaces = spaces or [pltpu.VMEM] * len(args)
    args = [
        pltpu.with_memory_space_constraint(arg, space) if space == pltpu.HBM else arg
        for arg, space in zip(args, spaces)
    ]
    return pl.pallas_call(
        kernel,
        out_shape=[
            pltpu.VMEM(shape, kind) if kept else jax.ShapeDtypeStruct(shape, kind)
            for shape, kind, *kept in outs
        ],
        in_specs=[pl.BlockSpec(memory_space=space) for space in spaces],
        out_specs=[pl.BlockSpec(memory_space=pltpu.VMEM)] * len(outs),
        scratch_shapes=scratch,
        compiler_params=pltpu.CompilerParams(vmem_limit_bytes=24 * 1024 * 1024),
        cost_estimate=pl.CostEstimate(flops=flops, bytes_accessed=moved, transcendentals=0),
    )(*args)


def on_device(
    events, cotangent, bucket_ids, history_lengths, w_in, b_in, w_out, pos_table, time_table
):
    rows, width = events.shape[1:]
    heads, window = pos_table.shape
    slabs = lax.axis_size(SEQ)
    scale = 1.0 / math.sqrt(lax.axis_size(BATCH) * slabs * rows)
    near, far = lax.axis_size(NEAR), lax.axis_size(FAR)
    moved = lax.ppermute(events, SEQ, [(i, i + 1) for i in range(slabs - 1)])
    half = (window, width)
    (
        out_last, gated, pre, own_last, normed, proj, slope, bias, grads, ev, cot, w_in_near,
        b_in_near, w_out_near,
    ) = call(
        own_kernel,
        [
            (half, BF16), (half, BF16), ((window, 4 * width), BF16), (half, F32),
            ((rows, width), BF16), ((window, 4 * width), BF16), ((window, 4 * width), F32),
            ((heads * window, window), F32), ((window, 2 * width), F32), ((rows, width), BF16),
            ((rows, width), BF16), (w_in.shape, BF16), ((1, 4 * width), F32), (w_out.shape, BF16),
        ],
        history_lengths, events[0], cotangent[0], bucket_ids[0], w_in, b_in[None], w_out,
        pos_table, time_table,
        spaces=[pltpu.SMEM] + [pltpu.HBM] * 8,
        scratch=[
            pltpu.VMEM((rows, window), jnp.int32),
            pltpu.VMEM(pos_table.shape, F32),
            pltpu.VMEM(time_table.shape, F32),
            pltpu.SemaphoreType.DMA((8,)),
        ],
        flops=10**9, moved=10**7,
    )
    layer_out, parts, bias_part, own_first, back = call(
        functools.partial(edge_kernel, scale),
        [
            ((rows, width), BF16), ((near, PIECE, 128), BF16), ((8, 128), F32), (half, F32),
            (half, F32),
        ],
        history_lengths, moved, out_last, gated, pre, normed, proj, slope, bias, grads, ev, cot,
        w_in_near, b_in_near, w_out_near,
        spaces=[pltpu.SMEM] + [pltpu.VMEM] * 14,
        flops=10**9, moved=10**7,
    )
    parts = lax.all_to_all(parts, NEAR, 0, 0)
    sums, back = call(
        near_kernel,
        [((far, PIECE + GROUP, 128), BF16, KEPT), (half, F32, KEPT)],
        parts, bias_part, back,
    )
    back = lax.ppermute(back, SEQ, [(i, i - 1) for i in range(1, slabs)])
    sums = lax.all_to_all(sums, FAR, 0, 0)
    sums, grad_events = call(
        far_kernel,
        [((near, PIECE + GROUP, 128), BF16, KEPT), ((rows, width), BF16)],
        sums, own_first, own_last, back, ev, cot,
    )
    sums = lax.all_to_all(sums, NEAR, 0, 0)
    sum_in, sum_bias, sum_out = call(
        unpack_kernel, [((width, 4 * width), F32), ((8, 128), F32), ((width, width), F32)], sums
    )
    return (layer_out[None], grad_events[None], sum_in, sum_bias.reshape(4 * width), sum_out)


def solution(mesh):
    fine = Mesh(
        mesh.devices.reshape(2, 8, 2, 2, 4, 2), ("yl", "zh", "zl", "yh", "x", "c")
    )
    slabs = P(BATCH, SEQ, None)
    return jax.shard_map(
        on_device,
        mesh=fine,
        in_specs=(slabs, slabs, slabs, P(BATCH), P(), P(), P(), P(), P()),
        out_specs=(slabs, slabs, P(), P(), P()),
        check_vma=False,
    )
```

```python
import functools
import math

import jax
import jax.numpy as jnp
from jax import lax
from jax.experimental import pallas as pl
from jax.experimental.pallas import tpu as pltpu
from jax.sharding import Mesh, PartitionSpec as P

EPS = 1e-05
F32 = jnp.float32
BF16 = jnp.bfloat16
NEAR = ("yl", "yh", "x", "c", "zl")
FAR = ("zh",)
BATCH = ("yl", "zh", "zl")
SEQ = ("yh", "x", "c")
GROUP = 8
PIECE = 6 * GROUP
BACK = 4
NEAR_FIRST = 48
KEPT = True


def norm_rows(values):
    row_mean = jnp.mean(values, axis=-1, keepdims=True)
    centred = values - row_mean
    variance = jnp.mean(centred * centred, axis=-1, keepdims=True)
    inv_std = lax.rsqrt(variance + EPS)
    return (centred * inv_std, inv_std)


def norm_back(upstream, normed, inv_std):
    first = jnp.mean(upstream, axis=-1, keepdims=True)
    second = jnp.mean(upstream * normed, axis=-1, keepdims=True)
    return inv_std * (upstream - first - normed * second)


def silu_and_slope(pre_act):
    sigmoid = jax.nn.sigmoid(pre_act)
    value = pre_act * sigmoid
    return (value, sigmoid * (1.0 + pre_act * (1.0 - sigmoid)))


def dot(left, right, dims=((1,), (0,))):
    return lax.dot_general(left, right, (dims, ((), ())), preferred_element_type=F32)


ROWS_BY_ROWS = ((1,), (1,))
COLS_BY_COLS = ((0,), (0,))


def lane_gather(table, index):
    return jnp.take_along_axis(table, index, axis=1, mode="promise_in_bounds")


class Band:
    def __init__(self, heads, window, width):
        self.heads, self.window, self.head = heads, window, width // heads
        row = lax.broadcasted_iota(jnp.int32, (window, window), 0)
        lane = lax.broadcasted_iota(jnp.int32, (window, window), 1)
        self.offset = (row - lane) & (window - 1)
        self.row = jnp.concatenate([row] * heads, axis=0)
        self.recent = jnp.concatenate([lane <= row] * heads, axis=0)
        self.column_head = lax.broadcasted_iota(jnp.int32, (window, width), 1) // self.head

    def bias(self, bucket_rows, pos_ref, time_ref):
        shape = (self.window, self.window)
        buckets = lane_gather(bucket_rows, self.offset)
        return jnp.concatenate(
            [
                lane_gather(jnp.broadcast_to(pos_ref[h : h + 1, :], shape), self.offset)
                + lane_gather(jnp.broadcast_to(time_ref[h : h + 1, :], shape), buckets)
                for h in range(self.heads)
            ],
            axis=0,
        )

    def by_head(self, block):
        zero = jnp.zeros_like(block)
        return jnp.concatenate(
            [jnp.where(self.column_head == h, block, zero) for h in range(self.heads)], axis=0
        )

    def pick_heads(self, stack):
        total = stack[: self.window]
        for h in range(1, self.heads):
            part = stack[h * self.window : (h + 1) * self.window]
            total = jnp.where(self.column_head == h, part, total)
        return total

    def split(self, band):
        zero = jnp.zeros_like(band)
        return jnp.concatenate(
            [jnp.where(self.recent, band, zero), jnp.where(self.recent, zero, band)], axis=1
        ).astype(BF16)

    def join(self, pair):
        return jnp.where(self.recent, pair[:, : self.window], pair[:, self.window :])

    def block(self, queries, pair_keys, pair_values, gate, bias, allowed, ev, cot, w_out):
        root = math.sqrt(self.head)
        stack_queries = self.by_head(queries)
        scores = self.join(dot(stack_queries, pair_keys, ROWS_BY_ROWS)) / root + bias
        act, slope = silu_and_slope(scores)
        weights = self.split(jnp.where(allowed, act * (1.0 / self.window), 0.0))
        att_hat, att_inv = norm_rows(self.pick_heads(dot(weights, pair_values)))
        gate_u = gate.astype(F32)
        gated = (att_hat * gate_u).astype(BF16)
        out = (ev.astype(F32) + dot(gated, w_out)).astype(BF16)
        upstream = dot(cot, w_out, ROWS_BY_ROWS)
        grad_att = self.by_head(norm_back(upstream * gate_u, att_hat, att_inv).astype(BF16))
        grad_weights = self.join(dot(grad_att, pair_values, ROWS_BY_ROWS))
        grad_scores = self.split(
            jnp.where(allowed, grad_weights * slope * (1.0 / self.window), 0.0)
        )
        grad_values = dot(weights, grad_att, COLS_BY_COLS)
        grad_queries = self.pick_heads(dot(grad_scores, pair_keys)) / root
        grad_keys = dot(grad_scores, stack_queries, COLS_BY_COLS) / root
        return (out, gated, upstream * att_hat, grad_values, grad_queries, grad_keys)


def own_kernel(
    length_ref, ev_hbm, cot_hbm, ids_hbm, w_in_hbm, b_in_hbm, w_out_hbm, pos_hbm, time_hbm,
    out_ref, gated_ref, pre_ref, own_ref, normed_ref, proj_ref, slope_ref, bias_ref, grads_ref,
    ev_ref, cot_ref, w_in_ref, b_in_ref, w_out_ref,
    ids_ref, pos_ref, time_ref, sems,
):
    pairs = [
        (ev_hbm, ev_ref), (w_in_hbm, w_in_ref), (b_in_hbm, b_in_ref), (ids_hbm, ids_ref),
        (pos_hbm, pos_ref), (time_hbm, time_ref), (cot_hbm, cot_ref), (w_out_hbm, w_out_ref),
    ]
    copies = [pltpu.make_async_copy(a, b, sems.at[i]) for i, (a, b) in enumerate(pairs)]
    for copy in copies:
        copy.start()
    rows, width = ev_ref.shape
    heads, window = pos_ref.shape
    real = length_ref[0] - lax.axis_index(SEQ) * rows
    band = Band(heads, window, width)
    copies[0].wait()
    hat, _ = norm_rows(ev_ref[...].astype(F32))
    normed = hat.astype(BF16)
    normed_ref[...] = normed
    copies[1].wait()
    copies[2].wait()
    value, slope = silu_and_slope(dot(normed, w_in_ref[...]) + b_in_ref[...])
    projected = value.astype(BF16)
    first, last = slice(0, window), slice(window, 2 * window)
    proj_ref[...] = projected[first]
    slope_ref[...] = slope[first]
    gate, values, queries, keys = [projected[:, i * width : (i + 1) * width] for i in range(4)]
    for copy in copies[3:6]:
        copy.wait()
    bias_ref[...] = band.bias(ids_ref[first, :], pos_ref, time_ref)
    bias = band.bias(ids_ref[last, :], pos_ref, time_ref)
    copies[6].wait()
    copies[7].wait()
    out, gated, grad_gate, grad_values, grad_queries, grad_keys = band.block(
        queries[last],
        jnp.concatenate([keys[last], keys[first]], axis=0),
        jnp.concatenate([values[last], values[first]], axis=0),
        gate[last], bias, band.row < real - window, ev_ref[last, :], cot_ref[last, :],
        w_out_ref[...],
    )
    out_ref[...] = out
    gated_ref[...] = gated
    grads_ref[:, :width] = grad_values[window:]
    grads_ref[:, width:] = grad_keys[window:]
    grads = jnp.concatenate(
        [grad_gate, grad_values[:window], grad_queries, grad_keys[:window]], axis=1
    )
    pre = (grads * slope[last]).astype(BF16)
    pre_ref[...] = pre
    own_ref[...] = dot(pre, w_in_ref[...], ROWS_BY_ROWS)


def edge_kernel(
    scale, length_ref, moved_ref, out_last_ref, gated_ref, pre_ref, normed_ref, proj_ref,
    slope_ref, bias_ref, grads_ref, ev_ref, cot_ref, w_in_ref, b_in_ref, w_out_ref,
    out_ref, parts_ref, own_ref,
):
    rows, width = ev_ref.shape
    window = out_last_ref.shape[0]
    heads = bias_ref.shape[0] // window
    slab = lax.axis_index(SEQ)
    real = length_ref[0] - slab * rows
    band = Band(heads, window, width)
    first, last = slice(0, window), slice(window, 2 * window)
    tail_hat, _ = norm_rows(moved_ref[0, rows - window :, :].astype(F32))
    tail_normed = tail_hat.astype(BF16)

    def columns(i):
        return slice(i * width, (i + 1) * width)

    def project(i):
        pre_act = dot(tail_normed, w_in_ref[:, columns(i)]) + b_in_ref[:, columns(i)]
        value, slope = silu_and_slope(pre_act)
        return (value.astype(BF16), slope)

    tail_values, tail_values_slope = project(1)
    tail_keys, tail_keys_slope = project(3)
    gate, values, queries, keys = [proj_ref[:, columns(i)] for i in range(4)]
    out, gated, grad_gate, grad_values, grad_queries, grad_keys = band.block(
        queries,
        jnp.concatenate([keys, tail_keys], axis=0),
        jnp.concatenate([values, tail_values], axis=0),
        gate, bias_ref[...], (band.row < real) & (band.recent | (slab > 0)),
        ev_ref[first, :], cot_ref[first, :], w_out_ref[...],
    )
    out_ref[first, :] = out
    out_ref[last, :] = out_last_ref[...]
    grads = [
        grad_gate,
        grad_values[:window] + grads_ref[:, :width],
        grad_queries,
        grad_keys[:window] + grads_ref[:, width:],
    ]
    tail_pre = {
        1: (grad_values[window:] * tail_values_slope).astype(BF16),
        3: (grad_keys[window:] * tail_keys_slope).astype(BF16),
    }
    left = jnp.concatenate([normed_ref[...], tail_normed], axis=0)
    own_total, back_total, in_blocks, bias_rows = None, None, [], []
    for i in range(4):
        own_pre = (grads[i] * slope_ref[:, columns(i)]).astype(BF16)
        part = dot(own_pre, w_in_ref[:, columns(i)], ROWS_BY_ROWS)
        own_total = part if own_total is None else own_total + part
        right = [own_pre, pre_ref[:, columns(i)]]
        if i in tail_pre:
            part = dot(tail_pre[i], w_in_ref[:, columns(i)], ROWS_BY_ROWS)
            back_total = part if back_total is None else back_total + part
            right.append(tail_pre[i])
        right = jnp.concatenate(right, axis=0)
        in_blocks.append(dot(left[: right.shape[0]], right, COLS_BY_COLS) * scale)
        bias_rows.append(jnp.sum(right.astype(F32), axis=0, keepdims=True) * scale)
    own_ref[...] = own_total
    part_out = dot(
        jnp.concatenate([gated, gated_ref[...]], axis=0), cot_ref[...], COLS_BY_COLS
    ) * scale
    tile_row = lax.broadcasted_iota(jnp.int32, (GROUP, 128), 0)
    for piece in range(parts_ref.shape[0]):
        group, half = piece // 2, piece % 2
        here = slice(group * GROUP, (group + 1) * GROUP)
        tiles = [
            in_blocks[2 * half + k // 2][here, (k % 2) * 128 : (k % 2 + 1) * 128]
            for k in range(4)
        ]
        tiles.append(part_out[here, half * 128 : (half + 1) * 128])
        rest = back_total[
            piece // 4 * GROUP : (piece // 4 + 1) * GROUP,
            piece // 2 % 2 * 128 : (piece // 2 % 2 + 1) * 128,
        ]
        if piece % 2:
            rest = pltpu.roll(rest, BACK, 0)
        line = piece // 8
        bias = bias_rows[line // 2][:, line % 2 * 128 : (line % 2 + 1) * 128]
        tiles.append(jnp.where(tile_row < BACK, rest, jnp.broadcast_to(bias, (GROUP, 128))))
        parts_ref[piece] = jnp.concatenate(tiles, axis=0).astype(BF16)


def near_kernel(parts_ref, sum_ref, back_ref):
    total = None
    for i in range(parts_ref.shape[0]):
        piece = parts_ref[i].astype(F32)
        back_ref[i] = piece[5 * GROUP :]
        total = piece if total is None else total + piece
    sums = total.astype(BF16)
    for i in range(sum_ref.shape[0]):
        sum_ref[i] = sums


def far_kernel(sources, parts_ref, back_ref, sum_ref):
    total = parts_ref[0].astype(F32)
    for i in range(1, parts_ref.shape[0]):
        total = total + parts_ref[i].astype(F32)
    tile_row = lax.broadcasted_iota(jnp.int32, (GROUP, 128), 0)
    rest = total[5 * GROUP :]
    for i, source in enumerate(sources):
        back = jnp.zeros_like(rest) if source is None else back_ref[source]
        last = jnp.where(tile_row < BACK, back, rest)
        sum_ref[i] = jnp.concatenate([total[: 5 * GROUP], last], axis=0).astype(BF16)


def unpack_kernel(
    all_ref, own_first_ref, own_last_ref, ev_ref, cot_ref, w_in_ref, b_in_ref, w_out_ref, grad_ref
):
    tile_row = lax.broadcasted_iota(jnp.int32, (GROUP, 128), 0)
    lasts = []
    for piece in range(all_ref.shape[0]):
        rows = all_ref[piece].astype(F32)
        group, half = piece // 2, piece % 2
        here = slice(group * GROUP, (group + 1) * GROUP)
        tiles = [rows[k * GROUP : (k + 1) * GROUP] for k in range(6)]
        w_in_ref[here, half * 512 : (half + 1) * 512] = jnp.concatenate(tiles[:4], axis=1)
        w_out_ref[here, half * 128 : (half + 1) * 128] = tiles[4]
        if piece % 8 == 0:
            b_in_ref[piece // 8 : piece // 8 + 1, :] = tiles[5][BACK : BACK + 1]
        lasts.append(tiles[5])
    back = jnp.concatenate(
        [
            jnp.concatenate(
                [
                    jnp.where(tile_row < BACK, lasts[i], pltpu.roll(lasts[i + 1], BACK, 0))
                    for i in (4 * t, 4 * t + 2)
                ],
                axis=1,
            )
            for t in range(len(lasts) // 4)
        ],
        axis=0,
    )
    window = back.shape[0]
    for half, grad in enumerate((own_first_ref[...], own_last_ref[...] + back)):
        here = slice(half * window, (half + 1) * window)
        hat, inv = norm_rows(ev_ref[here, :].astype(F32))
        grad_ref[here, :] = (cot_ref[here, :].astype(F32) + norm_back(grad, hat, inv)).astype(BF16)


def call(kernel, outs, *args, spaces=None, scratch=(), flops=0, moved=0):
    spaces = spaces or [pltpu.VMEM] * len(args)
    args = [
        pltpu.with_memory_space_constraint(arg, space) if space == pltpu.HBM else arg
        for arg, space in zip(args, spaces)
    ]
    return pl.pallas_call(
        kernel,
        out_shape=[
            pltpu.VMEM(shape, kind) if kept else jax.ShapeDtypeStruct(shape, kind)
            for shape, kind, *kept in outs
        ],
        in_specs=[pl.BlockSpec(memory_space=space) for space in spaces],
        out_specs=[pl.BlockSpec(memory_space=pltpu.VMEM)] * len(outs),
        scratch_shapes=scratch,
        compiler_params=pltpu.CompilerParams(vmem_limit_bytes=24 * 1024 * 1024),
        cost_estimate=pl.CostEstimate(flops=flops, bytes_accessed=moved, transcendentals=0),
    )(*args)


def on_device(
    events, cotangent, bucket_ids, history_lengths, w_in, b_in, w_out, pos_table, time_table
):
    rows, width = events.shape[1:]
    heads, window = pos_table.shape
    slabs = lax.axis_size(SEQ)
    scale = 1.0 / math.sqrt(lax.axis_size(BATCH) * slabs * rows)
    near, far = lax.axis_size(NEAR), lax.axis_size(FAR)
    moved = lax.ppermute(events, SEQ, [(i, i + 1) for i in range(slabs - 1)])
    half = (window, width)
    (
        out_last, gated, pre, own_last, normed, proj, slope, bias, grads, ev, cot, w_in_near,
        b_in_near, w_out_near,
    ) = call(
        own_kernel,
        [
            (half, BF16), (half, BF16), ((window, 4 * width), BF16), (half, F32),
            ((rows, width), BF16), ((window, 4 * width), BF16), ((window, 4 * width), F32),
            ((heads * window, window), F32), ((window, 2 * width), F32), ((rows, width), BF16),
            ((rows, width), BF16), (w_in.shape, BF16), ((1, 4 * width), F32), (w_out.shape, BF16),
        ],
        history_lengths, events[0], cotangent[0], bucket_ids[0], w_in, b_in[None], w_out,
        pos_table, time_table,
        spaces=[pltpu.SMEM] + [pltpu.HBM] * 8,
        scratch=[
            pltpu.VMEM((rows, window), jnp.int32),
            pltpu.VMEM(pos_table.shape, F32),
            pltpu.VMEM(time_table.shape, F32),
            pltpu.SemaphoreType.DMA((8,)),
        ],
        flops=10**9, moved=10**7,
    )
    layer_out, parts, own_first = call(
        functools.partial(edge_kernel, scale),
        [((rows, width), BF16), ((near, PIECE, 128), BF16, KEPT), (half, F32, KEPT)],
        history_lengths, moved, out_last, gated, pre, normed, proj, slope, bias, grads, ev, cot,
        w_in_near, b_in_near, w_out_near,
        spaces=[pltpu.SMEM] + [pltpu.VMEM] * 14,
        flops=10**9, moved=10**7,
    )
    zl = lax.axis_size("zl")
    order = [(i + NEAR_FIRST) % near for i in range(near)]
    sources = [
        order.index(i + zl) if i // zl % slabs < slabs - 1 else None for i in order
    ]
    parts = lax.all_to_all(parts, NEAR, 0, 0, axis_index_groups=[order])
    sums, back = call(
        near_kernel, [((far, PIECE, 128), BF16, KEPT), ((near, GROUP, 128), F32, KEPT)], parts
    )
    sums = lax.all_to_all(
        sums, FAR, 0, 0, axis_index_groups=[[(i + far // 2) % far for i in range(far)]]
    )
    (sums,) = call(
        functools.partial(far_kernel, sources), [((near, PIECE, 128), BF16, KEPT)], sums, back
    )
    sums = lax.all_to_all(sums, NEAR, 0, 0, axis_index_groups=[order])
    sum_in, sum_bias, sum_out, grad_events = call(
        unpack_kernel,
        [
            ((width, 4 * width), F32), ((8, 128), F32), ((width, width), F32),
            ((rows, width), BF16),
        ],
        sums, own_first, own_last, ev, cot,
    )
    return (layer_out[None], grad_events[None], sum_in, sum_bias.reshape(4 * width), sum_out)


def solution(mesh):
    fine = Mesh(
        mesh.devices.reshape(2, 8, 2, 2, 4, 2), ("yl", "zh", "zl", "yh", "x", "c")
    )
    slabs = P(BATCH, SEQ, None)
    return jax.shard_map(
        on_device,
        mesh=fine,
        in_specs=(slabs, slabs, slabs, P(BATCH), P(), P(), P(), P(), P()),
        out_specs=(slabs, slabs, P(), P(), P()),
        check_vma=False,
    )
```

```python
import functools
import math

import jax
import jax.numpy as jnp
from jax import lax
from jax.experimental import pallas as pl
from jax.experimental.pallas import tpu as pltpu
from jax.sharding import Mesh, PartitionSpec as P

EPS = 1e-05
F32 = jnp.float32
BF16 = jnp.bfloat16
NEAR = ("yl", "yh", "x", "c", "zl")
FAR = ("zh",)
BATCH = ("yl", "zh", "zl")
SEQ = ("yh", "x", "c")
GROUP = 8
PIECE = 6 * GROUP
BACK = 4
PARTS = 4
NEAR_FIRST = 24
KEPT = pltpu.VMEM
SENT = pltpu.HBM


def norm_rows(values):
    row_mean = jnp.mean(values, axis=-1, keepdims=True)
    centred = values - row_mean
    variance = jnp.mean(centred * centred, axis=-1, keepdims=True)
    inv_std = lax.rsqrt(variance + EPS)
    return (centred * inv_std, inv_std)


def norm_back(upstream, normed, inv_std):
    first = jnp.mean(upstream, axis=-1, keepdims=True)
    second = jnp.mean(upstream * normed, axis=-1, keepdims=True)
    return inv_std * (upstream - first - normed * second)


def silu_and_slope(pre_act):
    sigmoid = jax.nn.sigmoid(pre_act)
    value = pre_act * sigmoid
    return (value, sigmoid * (1.0 + pre_act * (1.0 - sigmoid)))


def dot(left, right, dims=((1,), (0,))):
    return lax.dot_general(left, right, (dims, ((), ())), preferred_element_type=F32)


ROWS_BY_ROWS = ((1,), (1,))
COLS_BY_COLS = ((0,), (0,))


def lane_gather(table, index):
    return jnp.take_along_axis(table, index, axis=1, mode="promise_in_bounds")


class Band:
    def __init__(self, heads, window, width):
        self.heads, self.window, self.head = heads, window, width // heads
        row = lax.broadcasted_iota(jnp.int32, (window, window), 0)
        lane = lax.broadcasted_iota(jnp.int32, (window, window), 1)
        self.offset = (row - lane) & (window - 1)
        self.row = jnp.concatenate([row] * heads, axis=0)
        self.recent = jnp.concatenate([lane <= row] * heads, axis=0)
        self.column_head = lax.broadcasted_iota(jnp.int32, (window, width), 1) // self.head

    def bias(self, bucket_rows, pos_ref, time_ref):
        shape = (self.window, self.window)
        buckets = lane_gather(bucket_rows, self.offset)
        return jnp.concatenate(
            [
                lane_gather(jnp.broadcast_to(pos_ref[h : h + 1, :], shape), self.offset)
                + lane_gather(jnp.broadcast_to(time_ref[h : h + 1, :], shape), buckets)
                for h in range(self.heads)
            ],
            axis=0,
        )

    def by_head(self, block):
        zero = jnp.zeros_like(block)
        return jnp.concatenate(
            [jnp.where(self.column_head == h, block, zero) for h in range(self.heads)], axis=0
        )

    def pick_heads(self, stack):
        total = stack[: self.window]
        for h in range(1, self.heads):
            part = stack[h * self.window : (h + 1) * self.window]
            total = jnp.where(self.column_head == h, part, total)
        return total

    def split(self, band):
        zero = jnp.zeros_like(band)
        return jnp.concatenate(
            [jnp.where(self.recent, band, zero), jnp.where(self.recent, zero, band)], axis=1
        ).astype(BF16)

    def join(self, pair):
        return jnp.where(self.recent, pair[:, : self.window], pair[:, self.window :])

    def block(self, queries, pair_keys, pair_values, gate, bias, allowed, ev, cot, w_out):
        root = math.sqrt(self.head)
        stack_queries = self.by_head(queries)
        scores = self.join(dot(stack_queries, pair_keys, ROWS_BY_ROWS)) / root + bias
        act, slope = silu_and_slope(scores)
        weights = self.split(jnp.where(allowed, act * (1.0 / self.window), 0.0))
        att_hat, att_inv = norm_rows(self.pick_heads(dot(weights, pair_values)))
        gate_u = gate.astype(F32)
        gated = (att_hat * gate_u).astype(BF16)
        out = (ev.astype(F32) + dot(gated, w_out)).astype(BF16)
        upstream = dot(cot, w_out, ROWS_BY_ROWS)
        grad_att = self.by_head(norm_back(upstream * gate_u, att_hat, att_inv).astype(BF16))
        grad_weights = self.join(dot(grad_att, pair_values, ROWS_BY_ROWS))
        grad_scores = self.split(
            jnp.where(allowed, grad_weights * slope * (1.0 / self.window), 0.0)
        )
        grad_values = dot(weights, grad_att, COLS_BY_COLS)
        grad_queries = self.pick_heads(dot(grad_scores, pair_keys)) / root
        grad_keys = dot(grad_scores, stack_queries, COLS_BY_COLS) / root
        return (out, gated, upstream * att_hat, grad_values, grad_queries, grad_keys)


def own_kernel(
    length_ref, ev_hbm, cot_hbm, ids_hbm, w_in_hbm, b_in_hbm, w_out_hbm, pos_hbm, time_hbm,
    out_ref, gated_ref, pre_ref, own_ref, normed_ref, proj_ref, slope_ref, bias_ref, grads_ref,
    ev_ref, cot_ref, w_in_ref, b_in_ref, w_out_ref,
    ids_ref, pos_ref, time_ref, sems,
):
    pairs = [
        (ev_hbm, ev_ref), (w_in_hbm, w_in_ref), (b_in_hbm, b_in_ref), (ids_hbm, ids_ref),
        (pos_hbm, pos_ref), (time_hbm, time_ref), (cot_hbm, cot_ref), (w_out_hbm, w_out_ref),
    ]
    copies = [pltpu.make_async_copy(a, b, sems.at[i]) for i, (a, b) in enumerate(pairs)]
    for copy in copies:
        copy.start()
    rows, width = ev_ref.shape
    heads, window = pos_ref.shape
    real = length_ref[0] - lax.axis_index(SEQ) * rows
    band = Band(heads, window, width)
    copies[0].wait()
    hat, _ = norm_rows(ev_ref[...].astype(F32))
    normed = hat.astype(BF16)
    normed_ref[...] = normed
    copies[1].wait()
    copies[2].wait()
    value, slope = silu_and_slope(dot(normed, w_in_ref[...]) + b_in_ref[...])
    projected = value.astype(BF16)
    first, last = slice(0, window), slice(window, 2 * window)
    proj_ref[...] = projected[first]
    slope_ref[...] = slope[first]
    gate, values, queries, keys = [projected[:, i * width : (i + 1) * width] for i in range(4)]
    for copy in copies[3:6]:
        copy.wait()
    bias_ref[...] = band.bias(ids_ref[first, :], pos_ref, time_ref)
    bias = band.bias(ids_ref[last, :], pos_ref, time_ref)
    copies[6].wait()
    copies[7].wait()
    out, gated, grad_gate, grad_values, grad_queries, grad_keys = band.block(
        queries[last],
        jnp.concatenate([keys[last], keys[first]], axis=0),
        jnp.concatenate([values[last], values[first]], axis=0),
        gate[last], bias, band.row < real - window, ev_ref[last, :], cot_ref[last, :],
        w_out_ref[...],
    )
    out_ref[...] = out
    gated_ref[...] = gated
    grads_ref[:, :width] = grad_values[window:]
    grads_ref[:, width:] = grad_keys[window:]
    grads = jnp.concatenate(
        [grad_gate, grad_values[:window], grad_queries, grad_keys[:window]], axis=1
    )
    pre = (grads * slope[last]).astype(BF16)
    pre_ref[...] = pre
    own_ref[...] = dot(pre, w_in_ref[...], ROWS_BY_ROWS)


def edge_kernel(
    scale, length_ref, moved_ref, out_last_ref, gated_ref, pre_ref, normed_ref, proj_ref,
    slope_ref, bias_ref, grads_ref, ev_ref, cot_ref, w_in_ref, b_in_ref, w_out_ref,
    out_ref, parts_ref, own_ref,
):
    rows, width = ev_ref.shape
    window = out_last_ref.shape[0]
    heads = bias_ref.shape[0] // window
    slab = lax.axis_index(SEQ)
    real = length_ref[0] - slab * rows
    band = Band(heads, window, width)
    first, last = slice(0, window), slice(window, 2 * window)
    tail_hat, _ = norm_rows(moved_ref[0, rows - window :, :].astype(F32))
    tail_normed = tail_hat.astype(BF16)

    def columns(i):
        return slice(i * width, (i + 1) * width)

    def project(i):
        pre_act = dot(tail_normed, w_in_ref[:, columns(i)]) + b_in_ref[:, columns(i)]
        value, slope = silu_and_slope(pre_act)
        return (value.astype(BF16), slope)

    tail_values, tail_values_slope = project(1)
    tail_keys, tail_keys_slope = project(3)
    gate, values, queries, keys = [proj_ref[:, columns(i)] for i in range(4)]
    out, gated, grad_gate, grad_values, grad_queries, grad_keys = band.block(
        queries,
        jnp.concatenate([keys, tail_keys], axis=0),
        jnp.concatenate([values, tail_values], axis=0),
        gate, bias_ref[...], (band.row < real) & (band.recent | (slab > 0)),
        ev_ref[first, :], cot_ref[first, :], w_out_ref[...],
    )
    out_ref[first, :] = out
    out_ref[last, :] = out_last_ref[...]
    grads = [
        grad_gate,
        grad_values[:window] + grads_ref[:, :width],
        grad_queries,
        grad_keys[:window] + grads_ref[:, width:],
    ]
    tail_pre = {
        1: (grad_values[window:] * tail_values_slope).astype(BF16),
        3: (grad_keys[window:] * tail_keys_slope).astype(BF16),
    }
    left = jnp.concatenate([normed_ref[...], tail_normed], axis=0)
    own_total, back_total, in_blocks, bias_rows = None, None, [], []
    for i in range(4):
        own_pre = (grads[i] * slope_ref[:, columns(i)]).astype(BF16)
        part = dot(own_pre, w_in_ref[:, columns(i)], ROWS_BY_ROWS)
        own_total = part if own_total is None else own_total + part
        right = [own_pre, pre_ref[:, columns(i)]]
        if i in tail_pre:
            part = dot(tail_pre[i], w_in_ref[:, columns(i)], ROWS_BY_ROWS)
            back_total = part if back_total is None else back_total + part
            right.append(tail_pre[i])
        right = jnp.concatenate(right, axis=0)
        in_blocks.append(dot(left[: right.shape[0]], right, COLS_BY_COLS) * scale)
        bias_rows.append(jnp.sum(right.astype(F32), axis=0, keepdims=True) * scale)
    own_ref[...] = own_total
    part_out = dot(
        jnp.concatenate([gated, gated_ref[...]], axis=0), cot_ref[...], COLS_BY_COLS
    ) * scale
    tile_row = lax.broadcasted_iota(jnp.int32, (GROUP, 128), 0)
    for piece in range(parts_ref.shape[0]):
        group, half = piece // 2, piece % 2
        here = slice(group * GROUP, (group + 1) * GROUP)
        tiles = [
            in_blocks[2 * half + k // 2][here, (k % 2) * 128 : (k % 2 + 1) * 128]
            for k in range(4)
        ]
        tiles.append(part_out[here, half * 128 : (half + 1) * 128])
        rest = back_total[
            piece // 4 * GROUP : (piece // 4 + 1) * GROUP,
            piece // 2 % 2 * 128 : (piece // 2 % 2 + 1) * 128,
        ]
        if piece % 2:
            rest = pltpu.roll(rest, BACK, 0)
        line = piece // 8
        bias = bias_rows[line // 2][:, line % 2 * 128 : (line % 2 + 1) * 128]
        tiles.append(jnp.where(tile_row < BACK, rest, jnp.broadcast_to(bias, (GROUP, 128))))
        parts_ref[piece] = jnp.concatenate(tiles, axis=0).astype(BF16)


def near_kernel(parts_ref, sum_ref, back_ref):
    total = None
    for i in range(parts_ref.shape[0]):
        piece = parts_ref[i].astype(F32)
        back_ref[i] = piece[5 * GROUP :]
        total = piece if total is None else total + piece
    sums = total.astype(BF16)
    for i in range(sum_ref.shape[0]):
        sum_ref[i] = sums


def far_kernel(sources, parts_ref, back_ref, sum_ref):
    total = parts_ref[0].astype(F32)
    for i in range(1, parts_ref.shape[0]):
        total = total + parts_ref[i].astype(F32)
    tile_row = lax.broadcasted_iota(jnp.int32, (GROUP, 128), 0)
    rest = total[5 * GROUP :]
    for i, source in enumerate(sources):
        back = jnp.zeros_like(rest) if source is None else back_ref[source]
        last = jnp.where(tile_row < BACK, back, rest)
        sum_ref[i] = jnp.concatenate([total[: 5 * GROUP], last], axis=0).astype(BF16)


def unpack_kernel(
    all_ref, own_first_ref, own_last_ref, ev_ref, cot_ref, out_ref,
    w_in_hbm, b_in_hbm, w_out_hbm, grad_hbm, out_hbm,
    w_in_ref, b_in_ref, w_out_ref, grad_ref, sems,
):
    copies = []

    def send(source, target):
        copy = pltpu.make_async_copy(source, target, sems.at[len(copies)])
        copy.start()
        copies.append(copy)

    send(out_ref, out_hbm)
    tile_row = lax.broadcasted_iota(jnp.int32, (GROUP, 128), 0)
    lasts = []
    pieces = all_ref.shape[0]
    part = pieces // PARTS
    for piece in range(pieces):
        rows = all_ref[piece].astype(F32)
        group, half = piece // 2, piece % 2
        here = slice(group * GROUP, (group + 1) * GROUP)
        tiles = [rows[k * GROUP : (k + 1) * GROUP] for k in range(6)]
        w_in_ref[here, half * 512 : (half + 1) * 512] = jnp.concatenate(tiles[:4], axis=1)
        w_out_ref[here, half * 128 : (half + 1) * 128] = tiles[4]
        if piece % 8 == 0:
            b_in_ref[piece // 8 : piece // 8 + 1, :] = tiles[5][BACK : BACK + 1]
        lasts.append(tiles[5])
        if (piece + 1) % part == 0:
            done = pl.ds((piece + 1 - part) // 2 * GROUP, part // 2 * GROUP)
            send(w_in_ref.at[done], w_in_hbm.at[done])
    send(w_out_ref, w_out_hbm)
    send(b_in_ref, b_in_hbm)
    back = jnp.concatenate(
        [
            jnp.concatenate(
                [
                    jnp.where(tile_row < BACK, lasts[i], pltpu.roll(lasts[i + 1], BACK, 0))
                    for i in (4 * t, 4 * t + 2)
                ],
                axis=1,
            )
            for t in range(len(lasts) // 4)
        ],
        axis=0,
    )
    window = back.shape[0]
    for half, grad in enumerate((own_first_ref[...], own_last_ref[...] + back)):
        here = slice(half * window, (half + 1) * window)
        hat, inv = norm_rows(ev_ref[here, :].astype(F32))
        grad_ref[here, :] = (cot_ref[here, :].astype(F32) + norm_back(grad, hat, inv)).astype(BF16)
    send(grad_ref, grad_hbm)
    for copy in copies:
        copy.wait()


def call(kernel, outs, *args, spaces=None, scratch=(), flops=0, moved=0):
    spaces = spaces or [pltpu.VMEM] * len(args)
    args = [
        pltpu.with_memory_space_constraint(arg, space) if space == pltpu.HBM else arg
        for arg, space in zip(args, spaces)
    ]
    return pl.pallas_call(
        kernel,
        out_shape=[
            pltpu.VMEM(shape, kind) if KEPT in place else jax.ShapeDtypeStruct(shape, kind)
            for shape, kind, *place in outs
        ],
        in_specs=[pl.BlockSpec(memory_space=space) for space in spaces],
        out_specs=[
            pl.BlockSpec(memory_space=SENT if SENT in place else pltpu.VMEM)
            for _, _, *place in outs
        ],
        scratch_shapes=scratch,
        compiler_params=pltpu.CompilerParams(vmem_limit_bytes=24 * 1024 * 1024),
        cost_estimate=pl.CostEstimate(flops=flops, bytes_accessed=moved, transcendentals=0),
    )(*args)


def on_device(
    events, cotangent, bucket_ids, history_lengths, w_in, b_in, w_out, pos_table, time_table
):
    rows, width = events.shape[1:]
    heads, window = pos_table.shape
    slabs = lax.axis_size(SEQ)
    scale = 1.0 / math.sqrt(lax.axis_size(BATCH) * slabs * rows)
    near, far = lax.axis_size(NEAR), lax.axis_size(FAR)
    moved = lax.ppermute(events, SEQ, [(i, i + 1) for i in range(slabs - 1)])
    half = (window, width)
    (
        out_last, gated, pre, own_last, normed, proj, slope, bias, grads, ev, cot, w_in_near,
        b_in_near, w_out_near,
    ) = call(
        own_kernel,
        [
            (half, BF16), (half, BF16), ((window, 4 * width), BF16), (half, F32),
            ((rows, width), BF16), ((window, 4 * width), BF16), ((window, 4 * width), F32),
            ((heads * window, window), F32), ((window, 2 * width), F32), ((rows, width), BF16),
            ((rows, width), BF16), (w_in.shape, BF16), ((1, 4 * width), F32), (w_out.shape, BF16),
        ],
        history_lengths, events[0], cotangent[0], bucket_ids[0], w_in, b_in[None], w_out,
        pos_table, time_table,
        spaces=[pltpu.SMEM] + [pltpu.HBM] * 8,
        scratch=[
            pltpu.VMEM((rows, window), jnp.int32),
            pltpu.VMEM(pos_table.shape, F32),
            pltpu.VMEM(time_table.shape, F32),
            pltpu.SemaphoreType.DMA((8,)),
        ],
        flops=10**9, moved=10**7,
    )
    layer_out, parts, own_first = call(
        functools.partial(edge_kernel, scale),
        [((rows, width), BF16, KEPT), ((near, PIECE, 128), BF16, KEPT), (half, F32, KEPT)],
        history_lengths, moved, out_last, gated, pre, normed, proj, slope, bias, grads, ev, cot,
        w_in_near, b_in_near, w_out_near,
        spaces=[pltpu.SMEM] + [pltpu.VMEM] * 14,
        flops=10**9, moved=10**7,
    )
    zl = lax.axis_size("zl")
    order = [(i + NEAR_FIRST) % near for i in range(near)]
    sources = [
        order.index(i + zl) if i // zl % slabs < slabs - 1 else None for i in order
    ]
    parts = lax.all_to_all(parts, NEAR, 0, 0, axis_index_groups=[order])
    sums, back = call(
        near_kernel, [((far, PIECE, 128), BF16, KEPT), ((near, GROUP, 128), F32, KEPT)], parts
    )
    sums = lax.all_to_all(
        sums, FAR, 0, 0, axis_index_groups=[[(i + 5) % far for i in range(far)]]
    )
    (sums,) = call(
        functools.partial(far_kernel, sources), [((near, PIECE, 128), BF16, KEPT)], sums, back
    )
    sums = lax.all_to_all(sums, NEAR, 0, 0, axis_index_groups=[order])
    sum_in, sum_bias, sum_out, grad_events, layer_out = call(
        unpack_kernel,
        [
            ((width, 4 * width), F32, SENT), ((8, 128), F32, SENT), ((width, width), F32, SENT),
            ((rows, width), BF16, SENT), ((rows, width), BF16, SENT),
        ],
        sums, own_first, own_last, ev, cot, layer_out,
        scratch=[
            pltpu.VMEM((width, 4 * width), F32), pltpu.VMEM((8, 128), F32),
            pltpu.VMEM((width, width), F32), pltpu.VMEM((rows, width), BF16),
            pltpu.SemaphoreType.DMA((PARTS + 4,)),
        ],
    )
    return (layer_out[None], grad_events[None], sum_in, sum_bias.reshape(4 * width), sum_out)


def solution(mesh):
    fine = Mesh(
        mesh.devices.reshape(2, 8, 2, 2, 4, 2), ("yl", "zh", "zl", "yh", "x", "c")
    )
    slabs = P(BATCH, SEQ, None)
    return jax.shard_map(
        on_device,
        mesh=fine,
        in_specs=(slabs, slabs, slabs, P(BATCH), P(), P(), P(), P(), P()),
        out_specs=(slabs, slabs, P(), P(), P()),
        check_vma=False,
    )
```

```python
import functools
import math

import jax
import jax.numpy as jnp
from jax import lax
from jax.experimental import pallas as pl
from jax.experimental.pallas import tpu as pltpu
from jax.sharding import Mesh, PartitionSpec as P

EPS = 1e-05
F32 = jnp.float32
BF16 = jnp.bfloat16
NEAR = ("yl", "yh", "x", "c", "zl")
FAR = ("zh",)
BATCH = ("yl", "zh", "zl")
SEQ = ("yh", "x", "c")
GROUP = 8
PIECE = 6 * GROUP
BACK = 4
PARTS = 4
NEAR_FIRST = 24
KEPT = pltpu.VMEM
SENT = pltpu.HBM


def norm_rows(values):
    row_mean = jnp.mean(values, axis=-1, keepdims=True)
    centred = values - row_mean
    variance = jnp.mean(centred * centred, axis=-1, keepdims=True)
    inv_std = lax.rsqrt(variance + EPS)
    return (centred * inv_std, inv_std)


def norm_back(upstream, normed, inv_std):
    first = jnp.mean(upstream, axis=-1, keepdims=True)
    second = jnp.mean(upstream * normed, axis=-1, keepdims=True)
    return inv_std * (upstream - first - normed * second)


def silu_and_slope(pre_act):
    sigmoid = jax.nn.sigmoid(pre_act)
    value = pre_act * sigmoid
    return (value, sigmoid * (1.0 + pre_act * (1.0 - sigmoid)))


def dot(left, right, dims=((1,), (0,))):
    return lax.dot_general(left, right, (dims, ((), ())), preferred_element_type=F32)


ROWS_BY_ROWS = ((1,), (1,))
COLS_BY_COLS = ((0,), (0,))


def lane_gather(table, index):
    return jnp.take_along_axis(table, index, axis=1, mode="promise_in_bounds")


class Band:
    def __init__(self, heads, window, width):
        self.heads, self.window, self.head = heads, window, width // heads
        row = lax.broadcasted_iota(jnp.int32, (window, window), 0)
        lane = lax.broadcasted_iota(jnp.int32, (window, window), 1)
        self.offset = (row - lane) & (window - 1)
        self.row = jnp.concatenate([row] * heads, axis=0)
        self.recent = jnp.concatenate([lane <= row] * heads, axis=0)
        self.column_head = lax.broadcasted_iota(jnp.int32, (window, width), 1) // self.head

    def bias(self, bucket_rows, pos_ref, time_ref):
        shape = (self.window, self.window)
        buckets = lane_gather(bucket_rows, self.offset)
        return jnp.concatenate(
            [
                lane_gather(jnp.broadcast_to(pos_ref[h : h + 1, :], shape), self.offset)
                + lane_gather(jnp.broadcast_to(time_ref[h : h + 1, :], shape), buckets)
                for h in range(self.heads)
            ],
            axis=0,
        )

    def by_head(self, block):
        zero = jnp.zeros_like(block)
        return jnp.concatenate(
            [jnp.where(self.column_head == h, block, zero) for h in range(self.heads)], axis=0
        )

    def pick_heads(self, stack):
        total = stack[: self.window]
        for h in range(1, self.heads):
            part = stack[h * self.window : (h + 1) * self.window]
            total = jnp.where(self.column_head == h, part, total)
        return total

    def split(self, band):
        zero = jnp.zeros_like(band)
        return jnp.concatenate(
            [jnp.where(self.recent, band, zero), jnp.where(self.recent, zero, band)], axis=1
        ).astype(BF16)

    def join(self, pair):
        return jnp.where(self.recent, pair[:, : self.window], pair[:, self.window :])

    def block(self, queries, pair_keys, pair_values, gate, bias, allowed, ev, cot, w_out):
        root = math.sqrt(self.head)
        stack_queries = self.by_head(queries)
        scores = self.join(dot(stack_queries, pair_keys, ROWS_BY_ROWS)) / root + bias
        act, slope = silu_and_slope(scores)
        weights = self.split(jnp.where(allowed, act * (1.0 / self.window), 0.0))
        att_hat, att_inv = norm_rows(self.pick_heads(dot(weights, pair_values)))
        gate_u = gate.astype(F32)
        gated = (att_hat * gate_u).astype(BF16)
        out = (ev.astype(F32) + dot(gated, w_out)).astype(BF16)
        upstream = dot(cot, w_out, ROWS_BY_ROWS)
        grad_att = self.by_head(norm_back(upstream * gate_u, att_hat, att_inv).astype(BF16))
        grad_weights = self.join(dot(grad_att, pair_values, ROWS_BY_ROWS))
        grad_scores = self.split(
            jnp.where(allowed, grad_weights * slope * (1.0 / self.window), 0.0)
        )
        grad_values = dot(weights, grad_att, COLS_BY_COLS)
        grad_queries = self.pick_heads(dot(grad_scores, pair_keys)) / root
        grad_keys = dot(grad_scores, stack_queries, COLS_BY_COLS) / root
        return (out, gated, upstream * att_hat, grad_values, grad_queries, grad_keys)


def own_kernel(
    length_ref, ev_hbm, cot_hbm, ids_hbm, w_in_hbm, b_in_hbm, w_out_hbm, pos_hbm, time_hbm,
    out_ref, gated_ref, pre_ref, own_ref, normed_ref, proj_ref, slope_ref, base_ref, mask_ref,
    grads_ref, stack_ref, att_ref, ratio_ref, ev_ref, cot_ref, w_in_ref, b_in_ref, w_out_ref,
    ids_ref, pos_ref, time_ref, sems,
):
    pairs = [
        (ev_hbm, ev_ref), (w_in_hbm, w_in_ref), (b_in_hbm, b_in_ref), (ids_hbm, ids_ref),
        (pos_hbm, pos_ref), (time_hbm, time_ref), (cot_hbm, cot_ref), (w_out_hbm, w_out_ref),
    ]
    copies = [pltpu.make_async_copy(a, b, sems.at[i]) for i, (a, b) in enumerate(pairs)]
    for copy in copies:
        copy.start()
    rows, width = ev_ref.shape
    heads, window = pos_ref.shape
    slab = lax.axis_index(SEQ)
    band = Band(heads, window, width)
    copies[0].wait()
    hat, _ = norm_rows(ev_ref[...].astype(F32))
    normed = hat.astype(BF16)
    normed_ref[...] = normed
    copies[1].wait()
    copies[2].wait()
    value, slope = silu_and_slope(dot(normed, w_in_ref[...]) + b_in_ref[...])
    projected = value.astype(BF16)
    first, last = slice(0, window), slice(window, 2 * window)
    proj_ref[...] = projected[first]
    slope_ref[...] = slope[first]
    gate, values, queries, keys = [projected[:, i * width : (i + 1) * width] for i in range(4)]
    for copy in copies[3:]:
        copy.wait()
    real = length_ref[0] - slab * rows
    bias = band.bias(ids_ref[last, :], pos_ref, time_ref)
    out, gated, grad_gate, grad_values, grad_queries, grad_keys = band.block(
        queries[last],
        jnp.concatenate([keys[last], keys[first]], axis=0),
        jnp.concatenate([values[last], values[first]], axis=0),
        gate[last], bias, band.row < real - window, ev_ref[last, :], cot_ref[last, :],
        w_out_ref[...],
    )
    out_ref[...] = out
    gated_ref[...] = gated
    grads_ref[:, :width] = grad_values[window:]
    grads_ref[:, width:] = grad_keys[window:]
    grads = jnp.concatenate(
        [grad_gate, grad_values[:window], grad_queries, grad_keys[:window]], axis=1
    )
    pre = (grads * slope[last]).astype(BF16)
    pre_ref[...] = pre
    own_ref[...] = dot(pre, w_in_ref[...], ROWS_BY_ROWS)

    stack = band.by_head(queries[first])
    stack_ref[...] = stack
    near = dot(stack, keys[first], ROWS_BY_ROWS) / math.sqrt(band.head)
    bias = band.bias(ids_ref[first, :], pos_ref, time_ref)
    base = jnp.where(band.recent, near, 0.0) + bias
    base_ref[...] = base
    allowed = (band.row < real) & (band.recent | (slab > 0))
    mask = jnp.where(allowed, 1.0 / window, 0.0)
    mask_ref[...] = mask
    act, _ = silu_and_slope(base)
    weights = jnp.where(band.recent, act * mask, 0.0).astype(BF16)
    att_ref[...] = band.pick_heads(dot(weights, values[first]))
    upstream = dot(cot_ref[first, :], w_out_ref[...], ROWS_BY_ROWS)
    ratio_ref[:, :width] = upstream * gate[first].astype(F32)
    ratio_ref[:, width:] = upstream * slope[first, :width]


def edge_kernel(
    scale, moved_ref, out_last_ref, gated_ref, pre_ref, normed_ref, proj_ref, slope_ref, base_ref,
    mask_ref, grads_ref, stack_ref, att_ref, ratio_ref, ev_ref, cot_ref, w_in_ref, b_in_ref,
    w_out_ref,
    out_ref, parts_ref, own_ref,
):
    rows, width = ev_ref.shape
    window = out_last_ref.shape[0]
    heads = base_ref.shape[0] // window
    band = Band(heads, window, width)
    root = math.sqrt(band.head)
    first, last = slice(0, window), slice(window, 2 * window)
    tail_hat, _ = norm_rows(moved_ref[0, rows - window :, :].astype(F32))
    tail_normed = tail_hat.astype(BF16)

    def columns(i):
        return slice(i * width, (i + 1) * width)

    def project(i):
        pre_act = dot(tail_normed, w_in_ref[:, columns(i)]) + b_in_ref[:, columns(i)]
        value, slope = silu_and_slope(pre_act)
        return (value.astype(BF16), slope)

    tail_keys, tail_keys_slope = project(3)
    stack = stack_ref[...]
    behind = dot(stack, tail_keys, ROWS_BY_ROWS) / root
    tail_values, tail_values_slope = project(1)
    act, slope = silu_and_slope(base_ref[...] + jnp.where(band.recent, 0.0, behind))
    weights = band.split(act * mask_ref[...])
    attended = att_ref[...] + band.pick_heads(dot(weights[:, window:], tail_values))
    att_hat, att_inv = norm_rows(attended)
    grad_att = band.by_head(
        norm_back(ratio_ref[:, :width], att_hat, att_inv).astype(BF16)
    )
    pair_values = jnp.concatenate([proj_ref[:, columns(1)], tail_values], axis=0)
    grad_weights = band.join(dot(grad_att, pair_values, ROWS_BY_ROWS))
    grad_scores = band.split(grad_weights * slope * mask_ref[...])
    grad_values = dot(weights, grad_att, COLS_BY_COLS)
    pair_keys = jnp.concatenate([proj_ref[:, columns(3)], tail_keys], axis=0)
    grad_queries = band.pick_heads(dot(grad_scores, pair_keys)) / root
    grad_keys = dot(grad_scores, stack, COLS_BY_COLS) / root
    gated = (att_hat * proj_ref[:, columns(0)].astype(F32)).astype(BF16)
    out_ref[first, :] = (ev_ref[first, :].astype(F32) + dot(gated, w_out_ref[...])).astype(BF16)
    out_ref[last, :] = out_last_ref[...]
    own_pre = [
        (ratio_ref[:, width:] * att_hat).astype(BF16),
        ((grad_values[:window] + grads_ref[:, :width]) * slope_ref[:, columns(1)]).astype(BF16),
        (grad_queries * slope_ref[:, columns(2)]).astype(BF16),
        ((grad_keys[:window] + grads_ref[:, width:]) * slope_ref[:, columns(3)]).astype(BF16),
    ]
    tail_pre = {
        1: (grad_values[window:] * tail_values_slope).astype(BF16),
        3: (grad_keys[window:] * tail_keys_slope).astype(BF16),
    }
    left = jnp.concatenate([normed_ref[...], tail_normed], axis=0)
    own_total, back_total, in_blocks, bias_rows = None, None, [], []
    for i in range(4):
        part = dot(own_pre[i], w_in_ref[:, columns(i)], ROWS_BY_ROWS)
        own_total = part if own_total is None else own_total + part
        right = [own_pre[i], pre_ref[:, columns(i)]]
        if i in tail_pre:
            part = dot(tail_pre[i], w_in_ref[:, columns(i)], ROWS_BY_ROWS)
            back_total = part if back_total is None else back_total + part
            right.append(tail_pre[i])
        right = jnp.concatenate(right, axis=0)
        in_blocks.append(dot(left[: right.shape[0]], right, COLS_BY_COLS) * scale)
        bias_rows.append(jnp.sum(right.astype(F32), axis=0, keepdims=True) * scale)
    own_ref[...] = own_total
    part_out = dot(
        jnp.concatenate([gated, gated_ref[...]], axis=0), cot_ref[...], COLS_BY_COLS
    ) * scale
    tile_row = lax.broadcasted_iota(jnp.int32, (GROUP, 128), 0)
    for piece in range(parts_ref.shape[0]):
        group, half = piece // 2, piece % 2
        here = slice(group * GROUP, (group + 1) * GROUP)
        tiles = [
            in_blocks[2 * half + k // 2][here, (k % 2) * 128 : (k % 2 + 1) * 128]
            for k in range(4)
        ]
        tiles.append(part_out[here, half * 128 : (half + 1) * 128])
        rest = back_total[
            piece // 4 * GROUP : (piece // 4 + 1) * GROUP,
            piece // 2 % 2 * 128 : (piece // 2 % 2 + 1) * 128,
        ]
        if piece % 2:
            rest = pltpu.roll(rest, BACK, 0)
        line = piece // 8
        bias = bias_rows[line // 2][:, line % 2 * 128 : (line % 2 + 1) * 128]
        tiles.append(jnp.where(tile_row < BACK, rest, jnp.broadcast_to(bias, (GROUP, 128))))
        parts_ref[piece] = jnp.concatenate(tiles, axis=0).astype(BF16)


def near_kernel(parts_ref, sum_ref, back_ref):
    total = None
    for i in range(parts_ref.shape[0]):
        piece = parts_ref[i].astype(F32)
        back_ref[i] = piece[5 * GROUP :]
        total = piece if total is None else total + piece
    sums = total.astype(BF16)
    for i in range(sum_ref.shape[0]):
        sum_ref[i] = sums


def far_kernel(sources, parts_ref, back_ref, sum_ref):
    total = parts_ref[0].astype(F32)
    for i in range(1, parts_ref.shape[0]):
        total = total + parts_ref[i].astype(F32)
    tile_row = lax.broadcasted_iota(jnp.int32, (GROUP, 128), 0)
    rest = total[5 * GROUP :]
    for i, source in enumerate(sources):
        back = jnp.zeros_like(rest) if source is None else back_ref[source]
        last = jnp.where(tile_row < BACK, back, rest)
        sum_ref[i] = jnp.concatenate([total[: 5 * GROUP], last], axis=0).astype(BF16)


def unpack_kernel(
    all_ref, own_first_ref, own_last_ref, ev_ref, cot_ref, out_ref,
    w_in_hbm, b_in_hbm, w_out_hbm, grad_hbm, out_hbm,
    w_in_ref, b_in_ref, w_out_ref, grad_ref, sems,
):
    copies = []

    def send(source, target):
        copy = pltpu.make_async_copy(source, target, sems.at[len(copies)])
        copy.start()
        copies.append(copy)

    send(out_ref, out_hbm)
    tile_row = lax.broadcasted_iota(jnp.int32, (GROUP, 128), 0)
    lasts = []
    pieces = all_ref.shape[0]
    part = pieces // PARTS
    for piece in range(pieces):
        rows = all_ref[piece].astype(F32)
        group, half = piece // 2, piece % 2
        here = slice(group * GROUP, (group + 1) * GROUP)
        tiles = [rows[k * GROUP : (k + 1) * GROUP] for k in range(6)]
        w_in_ref[here, half * 512 : (half + 1) * 512] = jnp.concatenate(tiles[:4], axis=1)
        w_out_ref[here, half * 128 : (half + 1) * 128] = tiles[4]
        if piece % 8 == 0:
            b_in_ref[piece // 8 : piece // 8 + 1, :] = tiles[5][BACK : BACK + 1]
        lasts.append(tiles[5])
        if (piece + 1) % part == 0:
            done = pl.ds((piece + 1 - part) // 2 * GROUP, part // 2 * GROUP)
            send(w_in_ref.at[done], w_in_hbm.at[done])
    send(w_out_ref, w_out_hbm)
    send(b_in_ref, b_in_hbm)
    back = jnp.concatenate(
        [
            jnp.concatenate(
                [
                    jnp.where(tile_row < BACK, lasts[i], pltpu.roll(lasts[i + 1], BACK, 0))
                    for i in (4 * t, 4 * t + 2)
                ],
                axis=1,
            )
            for t in range(len(lasts) // 4)
        ],
        axis=0,
    )
    window = back.shape[0]
    for half, grad in enumerate((own_first_ref[...], own_last_ref[...] + back)):
        here = slice(half * window, (half + 1) * window)
        hat, inv = norm_rows(ev_ref[here, :].astype(F32))
        grad_ref[here, :] = (cot_ref[here, :].astype(F32) + norm_back(grad, hat, inv)).astype(BF16)
    send(grad_ref, grad_hbm)
    for copy in copies:
        copy.wait()


def call(kernel, outs, *args, spaces=None, scratch=(), flops=0, moved=0):
    spaces = spaces or [pltpu.VMEM] * len(args)
    args = [
        pltpu.with_memory_space_constraint(arg, space) if space == pltpu.HBM else arg
        for arg, space in zip(args, spaces)
    ]
    return pl.pallas_call(
        kernel,
        out_shape=[
            pltpu.VMEM(shape, kind) if KEPT in place else jax.ShapeDtypeStruct(shape, kind)
            for shape, kind, *place in outs
        ],
        in_specs=[pl.BlockSpec(memory_space=space) for space in spaces],
        out_specs=[
            pl.BlockSpec(memory_space=SENT if SENT in place else pltpu.VMEM)
            for _, _, *place in outs
        ],
        scratch_shapes=scratch,
        compiler_params=pltpu.CompilerParams(vmem_limit_bytes=24 * 1024 * 1024),
        cost_estimate=pl.CostEstimate(flops=flops, bytes_accessed=moved, transcendentals=0),
    )(*args)


def on_device(
    events, cotangent, bucket_ids, history_lengths, w_in, b_in, w_out, pos_table, time_table
):
    rows, width = events.shape[1:]
    heads, window = pos_table.shape
    slabs = lax.axis_size(SEQ)
    scale = 1.0 / math.sqrt(lax.axis_size(BATCH) * slabs * rows)
    near, far = lax.axis_size(NEAR), lax.axis_size(FAR)
    moved = lax.ppermute(events, SEQ, [(i, i + 1) for i in range(slabs - 1)])
    half = (window, width)
    band = (heads * window, window)
    own_last, *kept = call(
        own_kernel,
        [
            (shape, kind, KEPT)
            for shape, kind in [
                (half, BF16), (half, BF16), ((window, 4 * width), BF16), (half, F32),
                ((rows, width), BF16), ((window, 4 * width), BF16), ((window, 4 * width), F32),
                (band, F32), (band, F32), ((window, 2 * width), F32),
                ((heads * window, width), BF16), (half, F32), ((window, 2 * width), F32),
                ((rows, width), BF16), ((rows, width), BF16), (w_in.shape, BF16),
                ((1, 4 * width), F32), (w_out.shape, BF16),
            ]
        ],
        history_lengths, events[0], cotangent[0], bucket_ids[0], w_in, b_in[None], w_out,
        pos_table, time_table,
        spaces=[pltpu.SMEM] + [pltpu.HBM] * 8,
        scratch=[
            pltpu.VMEM((rows, window), jnp.int32),
            pltpu.VMEM(pos_table.shape, F32),
            pltpu.VMEM(time_table.shape, F32),
            pltpu.SemaphoreType.DMA((8,)),
        ],
        flops=10**9, moved=10**7,
    )
    own_last, kept = kept[2], [own_last, *kept[:2], *kept[3:]]
    ev, cot = kept[12:14]
    layer_out, parts, own_first = call(
        functools.partial(edge_kernel, scale),
        [((rows, width), BF16, KEPT), ((near, PIECE, 128), BF16, KEPT), (half, F32, KEPT)],
        moved, *kept,
        flops=10**9, moved=10**7,
    )
    zl = lax.axis_size("zl")
    order = [(i + NEAR_FIRST) % near for i in range(near)]
    sources = [
        order.index(i + zl) if i // zl % slabs < slabs - 1 else None for i in order
    ]
    parts = lax.all_to_all(parts, NEAR, 0, 0, axis_index_groups=[order])
    sums, back = call(
        near_kernel, [((far, PIECE, 128), BF16, KEPT), ((near, GROUP, 128), F32, KEPT)], parts
    )
    sums = lax.all_to_all(
        sums, FAR, 0, 0, axis_index_groups=[[(i + 5) % far for i in range(far)]]
    )
    (sums,) = call(
        functools.partial(far_kernel, sources), [((near, PIECE, 128), BF16, KEPT)], sums, back
    )
    sums = lax.all_to_all(sums, NEAR, 0, 0, axis_index_groups=[order])
    sum_in, sum_bias, sum_out, grad_events, layer_out = call(
        unpack_kernel,
        [
            ((width, 4 * width), F32, SENT), ((8, 128), F32, SENT), ((width, width), F32, SENT),
            ((rows, width), BF16, SENT), ((rows, width), BF16, SENT),
        ],
        sums, own_first, own_last, ev, cot, layer_out,
        scratch=[
            pltpu.VMEM((width, 4 * width), F32), pltpu.VMEM((8, 128), F32),
            pltpu.VMEM((width, width), F32), pltpu.VMEM((rows, width), BF16),
            pltpu.SemaphoreType.DMA((PARTS + 4,)),
        ],
    )
    return (layer_out[None], grad_events[None], sum_in, sum_bias.reshape(4 * width), sum_out)


def solution(mesh):
    fine = Mesh(
        mesh.devices.reshape(2, 8, 2, 2, 4, 2), ("yl", "zh", "zl", "yh", "x", "c")
    )
    slabs = P(BATCH, SEQ, None)
    return jax.shard_map(
        on_device,
        mesh=fine,
        in_specs=(slabs, slabs, slabs, P(BATCH), P(), P(), P(), P(), P()),
        out_specs=(slabs, slabs, P(), P(), P()),
        check_vma=False,
    )
```

```python
import functools
import math

import jax
import jax.numpy as jnp
from jax import lax
from jax.experimental import pallas as pl
from jax.experimental.pallas import tpu as pltpu
from jax.sharding import Mesh, PartitionSpec as P

EPS = 1e-05
F32 = jnp.float32
BF16 = jnp.bfloat16
NEAR = ("yl", "yh", "x", "c", "zl")
FAR = ("zh",)
BATCH = ("yl", "zh", "zl")
SEQ = ("yh", "x", "c")
GROUP = 8
PIECE = 6 * GROUP
BACK = 4
PARTS = 4
NEAR_FIRST = 56
KEPT = pltpu.VMEM
SENT = pltpu.HBM


def norm_rows(values):
    row_mean = jnp.mean(values, axis=-1, keepdims=True)
    centred = values - row_mean
    variance = jnp.mean(centred * centred, axis=-1, keepdims=True)
    inv_std = lax.rsqrt(variance + EPS)
    return (centred * inv_std, inv_std)


def norm_back(upstream, normed, inv_std):
    first = jnp.mean(upstream, axis=-1, keepdims=True)
    second = jnp.mean(upstream * normed, axis=-1, keepdims=True)
    return inv_std * (upstream - first - normed * second)


def silu_and_slope(pre_act):
    sigmoid = jax.nn.sigmoid(pre_act)
    value = pre_act * sigmoid
    return (value, sigmoid * (1.0 + pre_act * (1.0 - sigmoid)))


def dot(left, right, dims=((1,), (0,))):
    return lax.dot_general(left, right, (dims, ((), ())), preferred_element_type=F32)


ROWS_BY_ROWS = ((1,), (1,))
COLS_BY_COLS = ((0,), (0,))


def lane_gather(table, index):
    return jnp.take_along_axis(table, index, axis=1, mode="promise_in_bounds")


class Band:
    def __init__(self, heads, window, width):
        self.heads, self.window, self.head = heads, window, width // heads
        row = lax.broadcasted_iota(jnp.int32, (window, window), 0)
        lane = lax.broadcasted_iota(jnp.int32, (window, window), 1)
        self.offset = (row - lane) & (window - 1)
        self.row = jnp.concatenate([row] * heads, axis=0)
        self.recent = jnp.concatenate([lane <= row] * heads, axis=0)
        self.column_head = lax.broadcasted_iota(jnp.int32, (window, width), 1) // self.head

    def bias(self, bucket_rows, pos_ref, time_ref):
        shape = (self.window, self.window)
        buckets = lane_gather(bucket_rows, self.offset)
        return jnp.concatenate(
            [
                lane_gather(jnp.broadcast_to(pos_ref[h : h + 1, :], shape), self.offset)
                + lane_gather(jnp.broadcast_to(time_ref[h : h + 1, :], shape), buckets)
                for h in range(self.heads)
            ],
            axis=0,
        )

    def by_head(self, block):
        zero = jnp.zeros_like(block)
        return jnp.concatenate(
            [jnp.where(self.column_head == h, block, zero) for h in range(self.heads)], axis=0
        )

    def pick_heads(self, stack):
        total = stack[: self.window]
        for h in range(1, self.heads):
            part = stack[h * self.window : (h + 1) * self.window]
            total = jnp.where(self.column_head == h, part, total)
        return total

    def split(self, band):
        zero = jnp.zeros_like(band)
        return jnp.concatenate(
            [jnp.where(self.recent, band, zero), jnp.where(self.recent, zero, band)], axis=1
        ).astype(BF16)

    def join(self, pair):
        return jnp.where(self.recent, pair[:, : self.window], pair[:, self.window :])

    def block(self, queries, pair_keys, pair_values, gate, bias, allowed, ev, cot, w_out):
        root = math.sqrt(self.head)
        stack_queries = self.by_head(queries)
        scores = self.join(dot(stack_queries, pair_keys, ROWS_BY_ROWS)) / root + bias
        act, slope = silu_and_slope(scores)
        weights = self.split(jnp.where(allowed, act * (1.0 / self.window), 0.0))
        att_hat, att_inv = norm_rows(self.pick_heads(dot(weights, pair_values)))
        gate_u = gate.astype(F32)
        gated = (att_hat * gate_u).astype(BF16)
        out = (ev.astype(F32) + dot(gated, w_out)).astype(BF16)
        upstream = dot(cot, w_out, ROWS_BY_ROWS)
        grad_att = self.by_head(norm_back(upstream * gate_u, att_hat, att_inv).astype(BF16))
        grad_weights = self.join(dot(grad_att, pair_values, ROWS_BY_ROWS))
        grad_scores = self.split(
            jnp.where(allowed, grad_weights * slope * (1.0 / self.window), 0.0)
        )
        grad_values = dot(weights, grad_att, COLS_BY_COLS)
        grad_queries = self.pick_heads(dot(grad_scores, pair_keys)) / root
        grad_keys = dot(grad_scores, stack_queries, COLS_BY_COLS) / root
        return (out, gated, upstream * att_hat, grad_values, grad_queries, grad_keys)


def own_kernel(
    length_ref, ev_hbm, cot_hbm, ids_hbm, w_in_hbm, b_in_hbm, w_out_hbm, pos_hbm, time_hbm,
    out_ref, gated_ref, pre_ref, own_ref, normed_ref, proj_ref, slope_ref, base_ref, mask_ref,
    grads_ref, stack_ref, att_ref, ratio_ref, ev_ref, cot_ref, w_in_ref, b_in_ref, w_out_ref,
    ids_ref, pos_ref, time_ref, sems,
):
    pairs = [
        (ev_hbm, ev_ref), (w_in_hbm, w_in_ref), (b_in_hbm, b_in_ref), (ids_hbm, ids_ref),
        (pos_hbm, pos_ref), (time_hbm, time_ref), (cot_hbm, cot_ref), (w_out_hbm, w_out_ref),
    ]
    copies = [pltpu.make_async_copy(a, b, sems.at[i]) for i, (a, b) in enumerate(pairs)]
    for copy in copies:
        copy.start()
    rows, width = ev_ref.shape
    heads, window = pos_ref.shape
    slab = lax.axis_index(SEQ)
    band = Band(heads, window, width)
    copies[0].wait()
    hat, _ = norm_rows(ev_ref[...].astype(F32))
    normed = hat.astype(BF16)
    normed_ref[...] = normed
    copies[1].wait()
    copies[2].wait()
    value, slope = silu_and_slope(dot(normed, w_in_ref[...]) + b_in_ref[...])
    projected = value.astype(BF16)
    first, last = slice(0, window), slice(window, 2 * window)
    proj_ref[...] = projected[first]
    slope_ref[...] = slope[first]
    gate, values, queries, keys = [projected[:, i * width : (i + 1) * width] for i in range(4)]
    for copy in copies[3:]:
        copy.wait()
    real = length_ref[0] - slab * rows
    bias = band.bias(ids_ref[last, :], pos_ref, time_ref)
    out, gated, grad_gate, grad_values, grad_queries, grad_keys = band.block(
        queries[last],
        jnp.concatenate([keys[last], keys[first]], axis=0),
        jnp.concatenate([values[last], values[first]], axis=0),
        gate[last], bias, band.row < real - window, ev_ref[last, :], cot_ref[last, :],
        w_out_ref[...],
    )
    out_ref[...] = out
    gated_ref[...] = gated
    grads_ref[:, :width] = grad_values[window:]
    grads_ref[:, width:] = grad_keys[window:]
    grads = jnp.concatenate(
        [grad_gate, grad_values[:window], grad_queries, grad_keys[:window]], axis=1
    )
    pre = (grads * slope[last]).astype(BF16)
    pre_ref[...] = pre
    own_ref[...] = dot(pre, w_in_ref[...], ROWS_BY_ROWS)

    stack = band.by_head(queries[first])
    stack_ref[...] = stack
    near = dot(stack, keys[first], ROWS_BY_ROWS) / math.sqrt(band.head)
    bias = band.bias(ids_ref[first, :], pos_ref, time_ref)
    base = jnp.where(band.recent, near, 0.0) + bias
    base_ref[...] = base
    allowed = (band.row < real) & (band.recent | (slab > 0))
    mask = jnp.where(allowed, 1.0 / window, 0.0)
    mask_ref[...] = mask
    act, _ = silu_and_slope(base)
    weights = jnp.where(band.recent, act * mask, 0.0).astype(BF16)
    att_ref[...] = band.pick_heads(dot(weights, values[first]))
    upstream = dot(cot_ref[first, :], w_out_ref[...], ROWS_BY_ROWS)
    ratio_ref[:, :width] = upstream * gate[first].astype(F32)
    ratio_ref[:, width:] = upstream * slope[first, :width]


def edge_kernel(
    scale, moved_ref, out_last_ref, gated_ref, pre_ref, normed_ref, proj_ref, slope_ref, base_ref,
    mask_ref, grads_ref, stack_ref, att_ref, ratio_ref, ev_ref, cot_ref, w_in_ref, b_in_ref,
    w_out_ref,
    out_ref, parts_ref, own_ref,
):
    rows, width = ev_ref.shape
    window = out_last_ref.shape[0]
    heads = base_ref.shape[0] // window
    band = Band(heads, window, width)
    root = math.sqrt(band.head)
    first, last = slice(0, window), slice(window, 2 * window)
    tail_hat, _ = norm_rows(moved_ref[0, rows - window :, :].astype(F32))
    tail_normed = tail_hat.astype(BF16)

    def columns(i):
        return slice(i * width, (i + 1) * width)

    def project(i):
        pre_act = dot(tail_normed, w_in_ref[:, columns(i)]) + b_in_ref[:, columns(i)]
        value, slope = silu_and_slope(pre_act)
        return (value.astype(BF16), slope)

    tail_keys, tail_keys_slope = project(3)
    stack = stack_ref[...]
    behind = dot(stack, tail_keys, ROWS_BY_ROWS) / root
    tail_values, tail_values_slope = project(1)
    act, slope = silu_and_slope(base_ref[...] + jnp.where(band.recent, 0.0, behind))
    weights = band.split(act * mask_ref[...])
    attended = att_ref[...] + band.pick_heads(dot(weights[:, window:], tail_values))
    att_hat, att_inv = norm_rows(attended)
    grad_att = band.by_head(
        norm_back(ratio_ref[:, :width], att_hat, att_inv).astype(BF16)
    )
    pair_values = jnp.concatenate([proj_ref[:, columns(1)], tail_values], axis=0)
    grad_weights = band.join(dot(grad_att, pair_values, ROWS_BY_ROWS))
    grad_scores = band.split(grad_weights * slope * mask_ref[...])
    grad_values = dot(weights, grad_att, COLS_BY_COLS)
    pair_keys = jnp.concatenate([proj_ref[:, columns(3)], tail_keys], axis=0)
    grad_queries = band.pick_heads(dot(grad_scores, pair_keys)) / root
    grad_keys = dot(grad_scores, stack, COLS_BY_COLS) / root
    gated = (att_hat * proj_ref[:, columns(0)].astype(F32)).astype(BF16)
    out_ref[first, :] = (ev_ref[first, :].astype(F32) + dot(gated, w_out_ref[...])).astype(BF16)
    out_ref[last, :] = out_last_ref[...]
    own_pre = [
        (ratio_ref[:, width:] * att_hat).astype(BF16),
        ((grad_values[:window] + grads_ref[:, :width]) * slope_ref[:, columns(1)]).astype(BF16),
        (grad_queries * slope_ref[:, columns(2)]).astype(BF16),
        ((grad_keys[:window] + grads_ref[:, width:]) * slope_ref[:, columns(3)]).astype(BF16),
    ]
    tail_pre = {
        1: (grad_values[window:] * tail_values_slope).astype(BF16),
        3: (grad_keys[window:] * tail_keys_slope).astype(BF16),
    }
    left = jnp.concatenate([normed_ref[...], tail_normed], axis=0)
    own_total, back_total, in_blocks, bias_rows = None, None, [], []
    for i in range(4):
        part = dot(own_pre[i], w_in_ref[:, columns(i)], ROWS_BY_ROWS)
        own_total = part if own_total is None else own_total + part
        right = [own_pre[i], pre_ref[:, columns(i)]]
        if i in tail_pre:
            part = dot(tail_pre[i], w_in_ref[:, columns(i)], ROWS_BY_ROWS)
            back_total = part if back_total is None else back_total + part
            right.append(tail_pre[i])
        right = jnp.concatenate(right, axis=0)
        in_blocks.append(dot(left[: right.shape[0]], right, COLS_BY_COLS) * scale)
        bias_rows.append(jnp.sum(right.astype(F32), axis=0, keepdims=True) * scale)
    own_ref[...] = own_total
    part_out = dot(
        jnp.concatenate([gated, gated_ref[...]], axis=0), cot_ref[...], COLS_BY_COLS
    ) * scale
    tile_row = lax.broadcasted_iota(jnp.int32, (GROUP, 128), 0)
    for piece in range(parts_ref.shape[0]):
        group, half = piece // 2, piece % 2
        here = slice(group * GROUP, (group + 1) * GROUP)
        tiles = [
            in_blocks[2 * half + k // 2][here, (k % 2) * 128 : (k % 2 + 1) * 128]
            for k in range(4)
        ]
        tiles.append(part_out[here, half * 128 : (half + 1) * 128])
        rest = back_total[
            piece // 4 * GROUP : (piece // 4 + 1) * GROUP,
            piece // 2 % 2 * 128 : (piece // 2 % 2 + 1) * 128,
        ]
        if piece % 2:
            rest = pltpu.roll(rest, BACK, 0)
        line = piece // 8
        bias = bias_rows[line // 2][:, line % 2 * 128 : (line % 2 + 1) * 128]
        tiles.append(jnp.where(tile_row < BACK, rest, jnp.broadcast_to(bias, (GROUP, 128))))
        parts_ref[piece] = jnp.concatenate(tiles, axis=0).astype(BF16)


def near_kernel(parts_ref, sum_ref, back_ref):
    total = None
    for i in range(parts_ref.shape[0]):
        piece = parts_ref[i].astype(F32)
        back_ref[i] = piece[5 * GROUP :]
        total = piece if total is None else total + piece
    sums = total.astype(BF16)
    for i in range(sum_ref.shape[0]):
        sum_ref[i] = sums


def far_kernel(sources, parts_ref, back_ref, sum_ref):
    total = parts_ref[0].astype(F32)
    for i in range(1, parts_ref.shape[0]):
        total = total + parts_ref[i].astype(F32)
    tile_row = lax.broadcasted_iota(jnp.int32, (GROUP, 128), 0)
    rest = total[5 * GROUP :]
    for i, source in enumerate(sources):
        back = jnp.zeros_like(rest) if source is None else back_ref[source]
        last = jnp.where(tile_row < BACK, back, rest)
        sum_ref[i] = jnp.concatenate([total[: 5 * GROUP], last], axis=0).astype(BF16)


def unpack_kernel(
    all_ref, own_first_ref, own_last_ref, ev_ref, cot_ref, out_ref,
    w_in_hbm, b_in_hbm, w_out_hbm, grad_hbm, out_hbm,
    w_in_ref, b_in_ref, w_out_ref, grad_ref, sems,
):
    copies = []

    def send(source, target):
        copy = pltpu.make_async_copy(source, target, sems.at[len(copies)])
        copy.start()
        copies.append(copy)

    send(out_ref, out_hbm)
    tile_row = lax.broadcasted_iota(jnp.int32, (GROUP, 128), 0)
    lasts = []
    pieces = all_ref.shape[0]
    part = pieces // PARTS
    for piece in range(pieces):
        rows = all_ref[piece].astype(F32)
        group, half = piece // 2, piece % 2
        here = slice(group * GROUP, (group + 1) * GROUP)
        tiles = [rows[k * GROUP : (k + 1) * GROUP] for k in range(6)]
        w_in_ref[here, half * 512 : (half + 1) * 512] = jnp.concatenate(tiles[:4], axis=1)
        w_out_ref[here, half * 128 : (half + 1) * 128] = tiles[4]
        if piece % 8 == 0:
            b_in_ref[piece // 8 : piece // 8 + 1, :] = tiles[5][BACK : BACK + 1]
        lasts.append(tiles[5])
        if (piece + 1) % part == 0:
            done = pl.ds((piece + 1 - part) // 2 * GROUP, part // 2 * GROUP)
            send(w_in_ref.at[done], w_in_hbm.at[done])
    send(w_out_ref, w_out_hbm)
    send(b_in_ref, b_in_hbm)
    back = jnp.concatenate(
        [
            jnp.concatenate(
                [
                    jnp.where(tile_row < BACK, lasts[i], pltpu.roll(lasts[i + 1], BACK, 0))
                    for i in (4 * t, 4 * t + 2)
                ],
                axis=1,
            )
            for t in range(len(lasts) // 4)
        ],
        axis=0,
    )
    window = back.shape[0]
    for half, grad in enumerate((own_first_ref[...], own_last_ref[...] + back)):
        here = slice(half * window, (half + 1) * window)
        hat, inv = norm_rows(ev_ref[here, :].astype(F32))
        grad_ref[here, :] = (cot_ref[here, :].astype(F32) + norm_back(grad, hat, inv)).astype(BF16)
    send(grad_ref, grad_hbm)
    for copy in copies:
        copy.wait()


def call(kernel, outs, *args, spaces=None, scratch=(), flops=0, moved=0):
    spaces = spaces or [pltpu.VMEM] * len(args)
    args = [
        pltpu.with_memory_space_constraint(arg, space) if space == pltpu.HBM else arg
        for arg, space in zip(args, spaces)
    ]
    return pl.pallas_call(
        kernel,
        out_shape=[
            pltpu.VMEM(shape, kind) if KEPT in place else jax.ShapeDtypeStruct(shape, kind)
            for shape, kind, *place in outs
        ],
        in_specs=[pl.BlockSpec(memory_space=space) for space in spaces],
        out_specs=[
            pl.BlockSpec(memory_space=SENT if SENT in place else pltpu.VMEM)
            for _, _, *place in outs
        ],
        scratch_shapes=scratch,
        compiler_params=pltpu.CompilerParams(vmem_limit_bytes=24 * 1024 * 1024),
        cost_estimate=pl.CostEstimate(flops=flops, bytes_accessed=moved, transcendentals=0),
    )(*args)


def on_device(
    events, cotangent, bucket_ids, history_lengths, w_in, b_in, w_out, pos_table, time_table
):
    rows, width = events.shape[1:]
    heads, window = pos_table.shape
    slabs = lax.axis_size(SEQ)
    scale = 1.0 / math.sqrt(lax.axis_size(BATCH) * slabs * rows)
    near, far = lax.axis_size(NEAR), lax.axis_size(FAR)
    moved = lax.ppermute(events, SEQ, [(i, i + 1) for i in range(slabs - 1)])
    half = (window, width)
    band = (heads * window, window)
    own_last, *kept = call(
        own_kernel,
        [
            (shape, kind, KEPT)
            for shape, kind in [
                (half, BF16), (half, BF16), ((window, 4 * width), BF16), (half, F32),
                ((rows, width), BF16), ((window, 4 * width), BF16), ((window, 4 * width), F32),
                (band, F32), (band, F32), ((window, 2 * width), F32),
                ((heads * window, width), BF16), (half, F32), ((window, 2 * width), F32),
                ((rows, width), BF16), ((rows, width), BF16), (w_in.shape, BF16),
                ((1, 4 * width), F32), (w_out.shape, BF16),
            ]
        ],
        history_lengths, events[0], cotangent[0], bucket_ids[0], w_in, b_in[None], w_out,
        pos_table, time_table,
        spaces=[pltpu.SMEM] + [pltpu.HBM] * 8,
        scratch=[
            pltpu.VMEM((rows, window), jnp.int32),
            pltpu.VMEM(pos_table.shape, F32),
            pltpu.VMEM(time_table.shape, F32),
            pltpu.SemaphoreType.DMA((8,)),
        ],
        flops=10**9, moved=10**7,
    )
    own_last, kept = kept[2], [own_last, *kept[:2], *kept[3:]]
    ev, cot = kept[12:14]
    layer_out, parts, own_first = call(
        functools.partial(edge_kernel, scale),
        [((rows, width), BF16, KEPT), ((near, PIECE, 128), BF16, KEPT), (half, F32, KEPT)],
        moved, *kept,
        flops=10**9, moved=10**7,
    )
    zl = lax.axis_size("zl")
    order = [(i + NEAR_FIRST) % near for i in range(near)]
    sources = [
        order.index(i + zl) if i // zl % slabs < slabs - 1 else None for i in order
    ]
    parts = lax.all_to_all(parts, NEAR, 0, 0, axis_index_groups=[order])
    sums, back = call(
        near_kernel, [((far, PIECE, 128), BF16, KEPT), ((near, GROUP, 128), F32, KEPT)], parts
    )
    sums = lax.all_to_all(
        sums, FAR, 0, 0, axis_index_groups=[[(i + 5) % far for i in range(far)]]
    )
    (sums,) = call(
        functools.partial(far_kernel, sources), [((near, PIECE, 128), BF16, KEPT)], sums, back
    )
    sums = lax.all_to_all(sums, NEAR, 0, 0, axis_index_groups=[order])
    sum_in, sum_bias, sum_out, grad_events, layer_out = call(
        unpack_kernel,
        [
            ((width, 4 * width), F32, SENT), ((8, 128), F32, SENT), ((width, width), F32, SENT),
            ((rows, width), BF16, SENT), ((rows, width), BF16, SENT),
        ],
        sums, own_first, own_last, ev, cot, layer_out,
        scratch=[
            pltpu.VMEM((width, 4 * width), F32), pltpu.VMEM((8, 128), F32),
            pltpu.VMEM((width, width), F32), pltpu.VMEM((rows, width), BF16),
            pltpu.SemaphoreType.DMA((PARTS + 4,)),
        ],
    )
    return (layer_out[None], grad_events[None], sum_in, sum_bias.reshape(4 * width), sum_out)


def solution(mesh):
    fine = Mesh(
        mesh.devices.reshape(2, 8, 2, 2, 4, 2), ("yl", "zh", "zl", "yh", "x", "c")
    )
    slabs = P(BATCH, SEQ, None)
    return jax.shard_map(
        on_device,
        mesh=fine,
        in_specs=(slabs, slabs, slabs, P(BATCH), P(), P(), P(), P(), P()),
        out_specs=(slabs, slabs, P(), P(), P()),
        check_vma=False,
    )
```

```python
import functools
import math

import jax
import jax.numpy as jnp
from jax import lax
from jax.experimental import pallas as pl
from jax.experimental.pallas import tpu as pltpu
from jax.sharding import Mesh, PartitionSpec as P

EPS = 1e-05
F32 = jnp.float32
BF16 = jnp.bfloat16
NEAR = ("yl", "yh", "x", "c", "zl")
FAR = ("zh",)
BATCH = ("yl", "zh", "zl")
SEQ = ("yh", "x", "c")
GROUP = 8
PIECE = 6 * GROUP
BACK = 4
PARTS = 4
FIRST_OUT = 50
FIRST_BACK = 58
KEPT = pltpu.VMEM
SENT = pltpu.HBM


def norm_rows(values):
    row_mean = jnp.mean(values, axis=-1, keepdims=True)
    centred = values - row_mean
    variance = jnp.mean(centred * centred, axis=-1, keepdims=True)
    inv_std = lax.rsqrt(variance + EPS)
    return (centred * inv_std, inv_std)


def norm_back(upstream, normed, inv_std):
    first = jnp.mean(upstream, axis=-1, keepdims=True)
    second = jnp.mean(upstream * normed, axis=-1, keepdims=True)
    return inv_std * (upstream - first - normed * second)


def silu_and_slope(pre_act):
    sigmoid = jax.nn.sigmoid(pre_act)
    value = pre_act * sigmoid
    return (value, sigmoid * (1.0 + pre_act * (1.0 - sigmoid)))


def dot(left, right, dims=((1,), (0,))):
    return lax.dot_general(left, right, (dims, ((), ())), preferred_element_type=F32)


ROWS_BY_ROWS = ((1,), (1,))
COLS_BY_COLS = ((0,), (0,))


def lane_gather(table, index):
    return jnp.take_along_axis(table, index, axis=1, mode="promise_in_bounds")


class Band:
    def __init__(self, heads, window, width):
        self.heads, self.window, self.head = heads, window, width // heads
        row = lax.broadcasted_iota(jnp.int32, (window, window), 0)
        lane = lax.broadcasted_iota(jnp.int32, (window, window), 1)
        self.offset = (row - lane) & (window - 1)
        self.row = jnp.concatenate([row] * heads, axis=0)
        self.recent = jnp.concatenate([lane <= row] * heads, axis=0)
        self.column_head = lax.broadcasted_iota(jnp.int32, (window, width), 1) // self.head

    def bias(self, bucket_rows, pos_ref, time_ref):
        shape = (self.window, self.window)
        buckets = lane_gather(bucket_rows, self.offset)
        return jnp.concatenate(
            [
                lane_gather(jnp.broadcast_to(pos_ref[h : h + 1, :], shape), self.offset)
                + lane_gather(jnp.broadcast_to(time_ref[h : h + 1, :], shape), buckets)
                for h in range(self.heads)
            ],
            axis=0,
        )

    def by_head(self, block):
        zero = jnp.zeros_like(block)
        return jnp.concatenate(
            [jnp.where(self.column_head == h, block, zero) for h in range(self.heads)], axis=0
        )

    def pick_heads(self, stack):
        total = stack[: self.window]
        for h in range(1, self.heads):
            part = stack[h * self.window : (h + 1) * self.window]
            total = jnp.where(self.column_head == h, part, total)
        return total

    def split(self, band):
        zero = jnp.zeros_like(band)
        return jnp.concatenate(
            [jnp.where(self.recent, band, zero), jnp.where(self.recent, zero, band)], axis=1
        ).astype(BF16)

    def join(self, pair):
        return jnp.where(self.recent, pair[:, : self.window], pair[:, self.window :])

    def block(self, queries, pair_keys, pair_values, gate, bias, allowed, ev, cot, w_out):
        root = math.sqrt(self.head)
        stack_queries = self.by_head(queries)
        scores = self.join(dot(stack_queries, pair_keys, ROWS_BY_ROWS)) / root + bias
        act, slope = silu_and_slope(scores)
        weights = self.split(jnp.where(allowed, act * (1.0 / self.window), 0.0))
        att_hat, att_inv = norm_rows(self.pick_heads(dot(weights, pair_values)))
        gate_u = gate.astype(F32)
        gated = (att_hat * gate_u).astype(BF16)
        out = (ev.astype(F32) + dot(gated, w_out)).astype(BF16)
        upstream = dot(cot, w_out, ROWS_BY_ROWS)
        grad_att = self.by_head(norm_back(upstream * gate_u, att_hat, att_inv).astype(BF16))
        grad_weights = self.join(dot(grad_att, pair_values, ROWS_BY_ROWS))
        grad_scores = self.split(
            jnp.where(allowed, grad_weights * slope * (1.0 / self.window), 0.0)
        )
        grad_values = dot(weights, grad_att, COLS_BY_COLS)
        grad_queries = self.pick_heads(dot(grad_scores, pair_keys)) / root
        grad_keys = dot(grad_scores, stack_queries, COLS_BY_COLS) / root
        return (out, gated, upstream * att_hat, grad_values, grad_queries, grad_keys)


def own_kernel(
    length_ref, ev_hbm, cot_hbm, ids_hbm, w_in_hbm, b_in_hbm, w_out_hbm, pos_hbm, time_hbm,
    out_ref, gated_ref, pre_ref, own_ref, normed_ref, proj_ref, slope_ref, base_ref, mask_ref,
    grads_ref, stack_ref, att_ref, ratio_ref, ev_ref, cot_ref, w_in_ref, b_in_ref, w_out_ref,
    ids_ref, pos_ref, time_ref, sems,
):
    pairs = [
        (ev_hbm, ev_ref), (w_in_hbm, w_in_ref), (b_in_hbm, b_in_ref), (ids_hbm, ids_ref),
        (pos_hbm, pos_ref), (time_hbm, time_ref), (cot_hbm, cot_ref), (w_out_hbm, w_out_ref),
    ]
    copies = [pltpu.make_async_copy(a, b, sems.at[i]) for i, (a, b) in enumerate(pairs)]
    for copy in copies:
        copy.start()
    rows, width = ev_ref.shape
    heads, window = pos_ref.shape
    slab = lax.axis_index(SEQ)
    band = Band(heads, window, width)
    copies[0].wait()
    hat, _ = norm_rows(ev_ref[...].astype(F32))
    normed = hat.astype(BF16)
    normed_ref[...] = normed
    copies[1].wait()
    copies[2].wait()
    value, slope = silu_and_slope(dot(normed, w_in_ref[...]) + b_in_ref[...])
    projected = value.astype(BF16)
    first, last = slice(0, window), slice(window, 2 * window)
    proj_ref[...] = projected[first]
    slope_ref[...] = slope[first]
    gate, values, queries, keys = [projected[:, i * width : (i + 1) * width] for i in range(4)]
    for copy in copies[3:]:
        copy.wait()
    real = length_ref[0] - slab * rows
    bias = band.bias(ids_ref[last, :], pos_ref, time_ref)
    out, gated, grad_gate, grad_values, grad_queries, grad_keys = band.block(
        queries[last],
        jnp.concatenate([keys[last], keys[first]], axis=0),
        jnp.concatenate([values[last], values[first]], axis=0),
        gate[last], bias, band.row < real - window, ev_ref[last, :], cot_ref[last, :],
        w_out_ref[...],
    )
    out_ref[...] = out
    gated_ref[...] = gated
    grads_ref[:, :width] = grad_values[window:]
    grads_ref[:, width:] = grad_keys[window:]
    grads = jnp.concatenate(
        [grad_gate, grad_values[:window], grad_queries, grad_keys[:window]], axis=1
    )
    pre = (grads * slope[last]).astype(BF16)
    pre_ref[...] = pre
    own_ref[...] = dot(pre, w_in_ref[...], ROWS_BY_ROWS)

    stack = band.by_head(queries[first])
    stack_ref[...] = stack
    near = dot(stack, keys[first], ROWS_BY_ROWS) / math.sqrt(band.head)
    bias = band.bias(ids_ref[first, :], pos_ref, time_ref)
    base = jnp.where(band.recent, near, 0.0) + bias
    base_ref[...] = base
    allowed = (band.row < real) & (band.recent | (slab > 0))
    mask = jnp.where(allowed, 1.0 / window, 0.0)
    mask_ref[...] = mask
    act, _ = silu_and_slope(base)
    weights = jnp.where(band.recent, act * mask, 0.0).astype(BF16)
    att_ref[...] = band.pick_heads(dot(weights, values[first]))
    upstream = dot(cot_ref[first, :], w_out_ref[...], ROWS_BY_ROWS)
    ratio_ref[:, :width] = upstream * gate[first].astype(F32)
    ratio_ref[:, width:] = upstream * slope[first, :width]


def edge_kernel(
    scale, moved_ref, out_last_ref, gated_ref, pre_ref, normed_ref, proj_ref, slope_ref, base_ref,
    mask_ref, grads_ref, stack_ref, att_ref, ratio_ref, ev_ref, cot_ref, w_in_ref, b_in_ref,
    w_out_ref,
    out_ref, parts_ref, own_ref,
):
    rows, width = ev_ref.shape
    window = out_last_ref.shape[0]
    heads = base_ref.shape[0] // window
    band = Band(heads, window, width)
    root = math.sqrt(band.head)
    first, last = slice(0, window), slice(window, 2 * window)
    tail_hat, _ = norm_rows(moved_ref[0, rows - window :, :].astype(F32))
    tail_normed = tail_hat.astype(BF16)

    def columns(i):
        return slice(i * width, (i + 1) * width)

    def project(i):
        pre_act = dot(tail_normed, w_in_ref[:, columns(i)]) + b_in_ref[:, columns(i)]
        value, slope = silu_and_slope(pre_act)
        return (value.astype(BF16), slope)

    tail_keys, tail_keys_slope = project(3)
    stack = stack_ref[...]
    behind = dot(stack, tail_keys, ROWS_BY_ROWS) / root
    tail_values, tail_values_slope = project(1)
    act, slope = silu_and_slope(base_ref[...] + jnp.where(band.recent, 0.0, behind))
    weights = band.split(act * mask_ref[...])
    attended = att_ref[...] + band.pick_heads(dot(weights[:, window:], tail_values))
    att_hat, att_inv = norm_rows(attended)
    grad_att = band.by_head(
        norm_back(ratio_ref[:, :width], att_hat, att_inv).astype(BF16)
    )
    pair_values = jnp.concatenate([proj_ref[:, columns(1)], tail_values], axis=0)
    grad_weights = band.join(dot(grad_att, pair_values, ROWS_BY_ROWS))
    grad_scores = band.split(grad_weights * slope * mask_ref[...])
    grad_values = dot(weights, grad_att, COLS_BY_COLS)
    pair_keys = jnp.concatenate([proj_ref[:, columns(3)], tail_keys], axis=0)
    grad_queries = band.pick_heads(dot(grad_scores, pair_keys)) / root
    grad_keys = dot(grad_scores, stack, COLS_BY_COLS) / root
    gated = (att_hat * proj_ref[:, columns(0)].astype(F32)).astype(BF16)
    out_ref[first, :] = (ev_ref[first, :].astype(F32) + dot(gated, w_out_ref[...])).astype(BF16)
    out_ref[last, :] = out_last_ref[...]
    own_pre = [
        (ratio_ref[:, width:] * att_hat).astype(BF16),
        ((grad_values[:window] + grads_ref[:, :width]) * slope_ref[:, columns(1)]).astype(BF16),
        (grad_queries * slope_ref[:, columns(2)]).astype(BF16),
        ((grad_keys[:window] + grads_ref[:, width:]) * slope_ref[:, columns(3)]).astype(BF16),
    ]
    tail_pre = {
        1: (grad_values[window:] * tail_values_slope).astype(BF16),
        3: (grad_keys[window:] * tail_keys_slope).astype(BF16),
    }
    left = jnp.concatenate([normed_ref[...], tail_normed], axis=0)
    own_total, back_total, in_blocks, bias_rows = None, None, [], []
    for i in range(4):
        part = dot(own_pre[i], w_in_ref[:, columns(i)], ROWS_BY_ROWS)
        own_total = part if own_total is None else own_total + part
        right = [own_pre[i], pre_ref[:, columns(i)]]
        if i in tail_pre:
            part = dot(tail_pre[i], w_in_ref[:, columns(i)], ROWS_BY_ROWS)
            back_total = part if back_total is None else back_total + part
            right.append(tail_pre[i])
        right = jnp.concatenate(right, axis=0)
        in_blocks.append(dot(left[: right.shape[0]], right, COLS_BY_COLS) * scale)
        bias_rows.append(jnp.sum(right.astype(F32), axis=0, keepdims=True) * scale)
    own_ref[...] = own_total
    part_out = dot(
        jnp.concatenate([gated, gated_ref[...]], axis=0), cot_ref[...], COLS_BY_COLS
    ) * scale
    tile_row = lax.broadcasted_iota(jnp.int32, (GROUP, 128), 0)
    for piece in range(parts_ref.shape[0]):
        group, half = piece // 2, piece % 2
        here = slice(group * GROUP, (group + 1) * GROUP)
        tiles = [
            in_blocks[2 * half + k // 2][here, (k % 2) * 128 : (k % 2 + 1) * 128]
            for k in range(4)
        ]
        tiles.append(part_out[here, half * 128 : (half + 1) * 128])
        rest = back_total[
            piece // 4 * GROUP : (piece // 4 + 1) * GROUP,
            piece // 2 % 2 * 128 : (piece // 2 % 2 + 1) * 128,
        ]
        if piece % 2:
            rest = pltpu.roll(rest, BACK, 0)
        line = piece // 8
        bias = bias_rows[line // 2][:, line % 2 * 128 : (line % 2 + 1) * 128]
        tiles.append(jnp.where(tile_row < BACK, rest, jnp.broadcast_to(bias, (GROUP, 128))))
        parts_ref[piece] = jnp.concatenate(tiles, axis=0).astype(BF16)


def near_kernel(parts_ref, sum_ref, back_ref):
    total = None
    for i in range(parts_ref.shape[0]):
        piece = parts_ref[i].astype(F32)
        back_ref[i] = piece[5 * GROUP :]
        total = piece if total is None else total + piece
    sums = total.astype(BF16)
    for i in range(sum_ref.shape[0]):
        sum_ref[i] = sums


def far_kernel(sources, parts_ref, back_ref, sum_ref):
    total = parts_ref[0].astype(F32)
    for i in range(1, parts_ref.shape[0]):
        total = total + parts_ref[i].astype(F32)
    tile_row = lax.broadcasted_iota(jnp.int32, (GROUP, 128), 0)
    rest = total[5 * GROUP :]
    for i, source in enumerate(sources):
        back = jnp.zeros_like(rest) if source is None else back_ref[source]
        last = jnp.where(tile_row < BACK, back, rest)
        sum_ref[i] = jnp.concatenate([total[: 5 * GROUP], last], axis=0).astype(BF16)


def unpack_kernel(
    places, all_ref, own_first_ref, own_last_ref, ev_ref, cot_ref, out_ref,
    w_in_hbm, b_in_hbm, w_out_hbm, grad_hbm, out_hbm,
    w_in_ref, b_in_ref, w_out_ref, grad_ref, sems,
):
    copies = []

    def send(source, target):
        copy = pltpu.make_async_copy(source, target, sems.at[len(copies)])
        copy.start()
        copies.append(copy)

    send(out_ref, out_hbm)
    tile_row = lax.broadcasted_iota(jnp.int32, (GROUP, 128), 0)
    lasts = []
    pieces = all_ref.shape[0]
    part = pieces // PARTS
    for piece in range(pieces):
        rows = all_ref[places[piece]].astype(F32)
        group, half = piece // 2, piece % 2
        here = slice(group * GROUP, (group + 1) * GROUP)
        tiles = [rows[k * GROUP : (k + 1) * GROUP] for k in range(6)]
        w_in_ref[here, half * 512 : (half + 1) * 512] = jnp.concatenate(tiles[:4], axis=1)
        w_out_ref[here, half * 128 : (half + 1) * 128] = tiles[4]
        if piece % 8 == 0:
            b_in_ref[piece // 8 : piece // 8 + 1, :] = tiles[5][BACK : BACK + 1]
        lasts.append(tiles[5])
        if (piece + 1) % part == 0:
            done = pl.ds((piece + 1 - part) // 2 * GROUP, part // 2 * GROUP)
            send(w_in_ref.at[done], w_in_hbm.at[done])
    send(w_out_ref, w_out_hbm)
    send(b_in_ref, b_in_hbm)
    back = jnp.concatenate(
        [
            jnp.concatenate(
                [
                    jnp.where(tile_row < BACK, lasts[i], pltpu.roll(lasts[i + 1], BACK, 0))
                    for i in (4 * t, 4 * t + 2)
                ],
                axis=1,
            )
            for t in range(len(lasts) // 4)
        ],
        axis=0,
    )
    window = back.shape[0]
    for half, grad in enumerate((own_first_ref[...], own_last_ref[...] + back)):
        here = slice(half * window, (half + 1) * window)
        hat, inv = norm_rows(ev_ref[here, :].astype(F32))
        grad_ref[here, :] = (cot_ref[here, :].astype(F32) + norm_back(grad, hat, inv)).astype(BF16)
    send(grad_ref, grad_hbm)
    for copy in copies:
        copy.wait()


def call(kernel, outs, *args, spaces=None, scratch=(), flops=0, moved=0):
    spaces = spaces or [pltpu.VMEM] * len(args)
    args = [
        pltpu.with_memory_space_constraint(arg, space) if space == pltpu.HBM else arg
        for arg, space in zip(args, spaces)
    ]
    return pl.pallas_call(
        kernel,
        out_shape=[
            pltpu.VMEM(shape, kind) if KEPT in place else jax.ShapeDtypeStruct(shape, kind)
            for shape, kind, *place in outs
        ],
        in_specs=[pl.BlockSpec(memory_space=space) for space in spaces],
        out_specs=[
            pl.BlockSpec(memory_space=SENT if SENT in place else pltpu.VMEM)
            for _, _, *place in outs
        ],
        scratch_shapes=scratch,
        compiler_params=pltpu.CompilerParams(vmem_limit_bytes=24 * 1024 * 1024),
        cost_estimate=pl.CostEstimate(flops=flops, bytes_accessed=moved, transcendentals=0),
    )(*args)


def on_device(
    events, cotangent, bucket_ids, history_lengths, w_in, b_in, w_out, pos_table, time_table
):
    rows, width = events.shape[1:]
    heads, window = pos_table.shape
    slabs = lax.axis_size(SEQ)
    scale = 1.0 / math.sqrt(lax.axis_size(BATCH) * slabs * rows)
    near, far = lax.axis_size(NEAR), lax.axis_size(FAR)
    moved = lax.ppermute(events, SEQ, [(i, i + 1) for i in range(slabs - 1)])
    half = (window, width)
    band = (heads * window, window)
    own_last, *kept = call(
        own_kernel,
        [
            (shape, kind, KEPT)
            for shape, kind in [
                (half, BF16), (half, BF16), ((window, 4 * width), BF16), (half, F32),
                ((rows, width), BF16), ((window, 4 * width), BF16), ((window, 4 * width), F32),
                (band, F32), (band, F32), ((window, 2 * width), F32),
                ((heads * window, width), BF16), (half, F32), ((window, 2 * width), F32),
                ((rows, width), BF16), ((rows, width), BF16), (w_in.shape, BF16),
                ((1, 4 * width), F32), (w_out.shape, BF16),
            ]
        ],
        history_lengths, events[0], cotangent[0], bucket_ids[0], w_in, b_in[None], w_out,
        pos_table, time_table,
        spaces=[pltpu.SMEM] + [pltpu.HBM] * 8,
        scratch=[
            pltpu.VMEM((rows, window), jnp.int32),
            pltpu.VMEM(pos_table.shape, F32),
            pltpu.VMEM(time_table.shape, F32),
            pltpu.SemaphoreType.DMA((8,)),
        ],
        flops=10**9, moved=10**7,
    )
    own_last, kept = kept[2], [own_last, *kept[:2], *kept[3:]]
    ev, cot = kept[12:14]
    layer_out, parts, own_first = call(
        functools.partial(edge_kernel, scale),
        [((rows, width), BF16, KEPT), ((near, PIECE, 128), BF16, KEPT), (half, F32, KEPT)],
        moved, *kept,
        flops=10**9, moved=10**7,
    )
    zl = lax.axis_size("zl")
    order = [(i + FIRST_OUT) % near for i in range(near)]
    back_order = [(i + FIRST_BACK) % near for i in range(near)]
    places = [back_order.index(i) for i in order]
    sources = [
        order.index(i + zl) if i // zl % slabs < slabs - 1 else None for i in back_order
    ]
    parts = lax.all_to_all(parts, NEAR, 0, 0, axis_index_groups=[order])
    sums, back = call(
        near_kernel, [((far, PIECE, 128), BF16, KEPT), ((near, GROUP, 128), F32, KEPT)], parts
    )
    sums = lax.all_to_all(
        sums, FAR, 0, 0, axis_index_groups=[[(i + 5) % far for i in range(far)]]
    )
    (sums,) = call(
        functools.partial(far_kernel, sources), [((near, PIECE, 128), BF16, KEPT)], sums, back
    )
    sums = lax.all_to_all(sums, NEAR, 0, 0, axis_index_groups=[back_order])
    sum_in, sum_bias, sum_out, grad_events, layer_out = call(
        functools.partial(unpack_kernel, places),
        [
            ((width, 4 * width), F32, SENT), ((8, 128), F32, SENT), ((width, width), F32, SENT),
            ((rows, width), BF16, SENT), ((rows, width), BF16, SENT),
        ],
        sums, own_first, own_last, ev, cot, layer_out,
        scratch=[
            pltpu.VMEM((width, 4 * width), F32), pltpu.VMEM((8, 128), F32),
            pltpu.VMEM((width, width), F32), pltpu.VMEM((rows, width), BF16),
            pltpu.SemaphoreType.DMA((PARTS + 4,)),
        ],
    )
    return (layer_out[None], grad_events[None], sum_in, sum_bias.reshape(4 * width), sum_out)


def solution(mesh):
    fine = Mesh(
        mesh.devices.reshape(2, 8, 2, 2, 4, 2), ("yl", "zh", "zl", "yh", "x", "c")
    )
    slabs = P(BATCH, SEQ, None)
    return jax.shard_map(
        on_device,
        mesh=fine,
        in_specs=(slabs, slabs, slabs, P(BATCH), P(), P(), P(), P(), P()),
        out_specs=(slabs, slabs, P(), P(), P()),
        check_vma=False,
    )
```

```python
import functools
import math

import jax
import jax.numpy as jnp
from jax import lax
from jax.experimental import pallas as pl
from jax.experimental.pallas import tpu as pltpu
from jax.sharding import Mesh, PartitionSpec as P

EPS = 1e-05
F32 = jnp.float32
BF16 = jnp.bfloat16
NEAR = ("yl", "yh", "x", "c", "zl")
FAR = ("zh",)
BATCH = ("yl", "zh", "zl")
SEQ = ("yh", "x", "c")
GROUP = 8
PIECE = 5 * GROUP + 5
BACK = 4
PARTS = 4
FIRST_OUT = 50
FIRST_BACK = 58
KEPT = pltpu.VMEM
SENT = pltpu.HBM


def norm_rows(values):
    row_mean = jnp.mean(values, axis=-1, keepdims=True)
    centred = values - row_mean
    variance = jnp.mean(centred * centred, axis=-1, keepdims=True)
    inv_std = lax.rsqrt(variance + EPS)
    return (centred * inv_std, inv_std)


def norm_back(upstream, normed, inv_std):
    first = jnp.mean(upstream, axis=-1, keepdims=True)
    second = jnp.mean(upstream * normed, axis=-1, keepdims=True)
    return inv_std * (upstream - first - normed * second)


def silu_and_slope(pre_act):
    sigmoid = jax.nn.sigmoid(pre_act)
    value = pre_act * sigmoid
    return (value, sigmoid * (1.0 + pre_act * (1.0 - sigmoid)))


def dot(left, right, dims=((1,), (0,))):
    return lax.dot_general(left, right, (dims, ((), ())), preferred_element_type=F32)


ROWS_BY_ROWS = ((1,), (1,))
COLS_BY_COLS = ((0,), (0,))


def lane_gather(table, index):
    return jnp.take_along_axis(table, index, axis=1, mode="promise_in_bounds")


class Band:
    def __init__(self, heads, window, width):
        self.heads, self.window, self.head = heads, window, width // heads
        row = lax.broadcasted_iota(jnp.int32, (window, window), 0)
        lane = lax.broadcasted_iota(jnp.int32, (window, window), 1)
        self.offset = (row - lane) & (window - 1)
        self.row = jnp.concatenate([row] * heads, axis=0)
        self.recent = jnp.concatenate([lane <= row] * heads, axis=0)
        self.column_head = lax.broadcasted_iota(jnp.int32, (window, width), 1) // self.head

    def bias(self, bucket_rows, pos_ref, time_ref):
        shape = (self.window, self.window)
        buckets = lane_gather(bucket_rows, self.offset)
        return jnp.concatenate(
            [
                lane_gather(jnp.broadcast_to(pos_ref[h : h + 1, :], shape), self.offset)
                + lane_gather(jnp.broadcast_to(time_ref[h : h + 1, :], shape), buckets)
                for h in range(self.heads)
            ],
            axis=0,
        )

    def by_head(self, block):
        zero = jnp.zeros_like(block)
        return jnp.concatenate(
            [jnp.where(self.column_head == h, block, zero) for h in range(self.heads)], axis=0
        )

    def pick_heads(self, stack):
        total = stack[: self.window]
        for h in range(1, self.heads):
            part = stack[h * self.window : (h + 1) * self.window]
            total = jnp.where(self.column_head == h, part, total)
        return total

    def split(self, band):
        zero = jnp.zeros_like(band)
        return jnp.concatenate(
            [jnp.where(self.recent, band, zero), jnp.where(self.recent, zero, band)], axis=1
        ).astype(BF16)

    def join(self, pair):
        return jnp.where(self.recent, pair[:, : self.window], pair[:, self.window :])

    def block(self, queries, pair_keys, pair_values, gate, bias, allowed, ev, cot, w_out):
        root = math.sqrt(self.head)
        stack_queries = self.by_head(queries)
        scores = self.join(dot(stack_queries, pair_keys, ROWS_BY_ROWS)) / root + bias
        act, slope = silu_and_slope(scores)
        weights = self.split(jnp.where(allowed, act * (1.0 / self.window), 0.0))
        att_hat, att_inv = norm_rows(self.pick_heads(dot(weights, pair_values)))
        gate_u = gate.astype(F32)
        gated = (att_hat * gate_u).astype(BF16)
        out = (ev.astype(F32) + dot(gated, w_out)).astype(BF16)
        upstream = dot(cot, w_out, ROWS_BY_ROWS)
        grad_att = self.by_head(norm_back(upstream * gate_u, att_hat, att_inv).astype(BF16))
        grad_weights = self.join(dot(grad_att, pair_values, ROWS_BY_ROWS))
        grad_scores = self.split(
            jnp.where(allowed, grad_weights * slope * (1.0 / self.window), 0.0)
        )
        grad_values = dot(weights, grad_att, COLS_BY_COLS)
        grad_queries = self.pick_heads(dot(grad_scores, pair_keys)) / root
        grad_keys = dot(grad_scores, stack_queries, COLS_BY_COLS) / root
        return (out, gated, upstream * att_hat, grad_values, grad_queries, grad_keys)


def own_kernel(
    length_ref, ev_hbm, cot_hbm, ids_hbm, w_in_hbm, b_in_hbm, w_out_hbm, pos_hbm, time_hbm,
    out_ref, gated_ref, pre_ref, own_ref, normed_ref, proj_ref, slope_ref, base_ref, mask_ref,
    grads_ref, stack_ref, att_ref, ratio_ref, early_ref, ev_ref, cot_ref, w_in_ref, b_in_ref,
    w_out_ref, ids_ref, pos_ref, time_ref, sems,
):
    pairs = [
        (ev_hbm, ev_ref), (w_in_hbm, w_in_ref), (b_in_hbm, b_in_ref), (ids_hbm, ids_ref),
        (pos_hbm, pos_ref), (time_hbm, time_ref), (cot_hbm, cot_ref), (w_out_hbm, w_out_ref),
    ]
    copies = [pltpu.make_async_copy(a, b, sems.at[i]) for i, (a, b) in enumerate(pairs)]
    for copy in copies:
        copy.start()
    rows, width = ev_ref.shape
    heads, window = pos_ref.shape
    slab = lax.axis_index(SEQ)
    band = Band(heads, window, width)
    copies[0].wait()
    hat, _ = norm_rows(ev_ref[...].astype(F32))
    normed = hat.astype(BF16)
    normed_ref[...] = normed
    copies[1].wait()
    copies[2].wait()
    value, slope = silu_and_slope(dot(normed, w_in_ref[...]) + b_in_ref[...])
    projected = value.astype(BF16)
    first, last = slice(0, window), slice(window, 2 * window)
    proj_ref[...] = projected[first]
    slope_ref[...] = slope[first]
    gate, values, queries, keys = [projected[:, i * width : (i + 1) * width] for i in range(4)]
    for copy in copies[3:]:
        copy.wait()
    real = length_ref[0] - slab * rows
    bias = band.bias(ids_ref[last, :], pos_ref, time_ref)
    out, gated, grad_gate, grad_values, grad_queries, grad_keys = band.block(
        queries[last],
        jnp.concatenate([keys[last], keys[first]], axis=0),
        jnp.concatenate([values[last], values[first]], axis=0),
        gate[last], bias, band.row < real - window, ev_ref[last, :], cot_ref[last, :],
        w_out_ref[...],
    )
    out_ref[...] = out
    gated_ref[...] = gated
    grads_ref[:, :width] = grad_values[window:]
    grads_ref[:, width:] = grad_keys[window:]
    grads = jnp.concatenate(
        [grad_gate, grad_values[:window], grad_queries, grad_keys[:window]], axis=1
    )
    pre = (grads * slope[last]).astype(BF16)
    pre_ref[...] = pre
    own_ref[...] = dot(pre, w_in_ref[...], ROWS_BY_ROWS)
    early_ref[:, : 4 * width] = dot(normed[last], pre, COLS_BY_COLS)
    early_ref[:, 4 * width :] = dot(gated, cot_ref[last, :], COLS_BY_COLS)

    stack = band.by_head(queries[first])
    stack_ref[...] = stack
    near = dot(stack, keys[first], ROWS_BY_ROWS) / math.sqrt(band.head)
    bias = band.bias(ids_ref[first, :], pos_ref, time_ref)
    base = jnp.where(band.recent, near, 0.0) + bias
    base_ref[...] = base
    allowed = (band.row < real) & (band.recent | (slab > 0))
    mask = jnp.where(allowed, 1.0 / window, 0.0)
    mask_ref[...] = mask
    act, _ = silu_and_slope(base)
    weights = jnp.where(band.recent, act * mask, 0.0).astype(BF16)
    att_ref[...] = band.pick_heads(dot(weights, values[first]))
    upstream = dot(cot_ref[first, :], w_out_ref[...], ROWS_BY_ROWS)
    ratio_ref[:, :width] = upstream * gate[first].astype(F32)
    ratio_ref[:, width:] = upstream * slope[first, :width]


def edge_kernel(
    scale, moved_ref, out_last_ref, gated_ref, pre_ref, normed_ref, proj_ref, slope_ref, base_ref,
    mask_ref, grads_ref, stack_ref, att_ref, ratio_ref, early_ref, ev_ref, cot_ref, w_in_ref,
    b_in_ref, w_out_ref,
    out_ref, parts_ref, own_ref,
):
    rows, width = ev_ref.shape
    window = out_last_ref.shape[0]
    heads = base_ref.shape[0] // window
    band = Band(heads, window, width)
    root = math.sqrt(band.head)
    first, last = slice(0, window), slice(window, 2 * window)
    tail_hat, _ = norm_rows(moved_ref[0, rows - window :, :].astype(F32))
    tail_normed = tail_hat.astype(BF16)

    def columns(i):
        return slice(i * width, (i + 1) * width)

    def project(i):
        pre_act = dot(tail_normed, w_in_ref[:, columns(i)]) + b_in_ref[:, columns(i)]
        value, slope = silu_and_slope(pre_act)
        return (value.astype(BF16), slope)

    tail_keys, tail_keys_slope = project(3)
    stack = stack_ref[...]
    behind = dot(stack, tail_keys, ROWS_BY_ROWS) / root
    tail_values, tail_values_slope = project(1)
    act, slope = silu_and_slope(base_ref[...] + jnp.where(band.recent, 0.0, behind))
    weights = band.split(act * mask_ref[...])
    attended = att_ref[...] + band.pick_heads(dot(weights[:, window:], tail_values))
    att_hat, att_inv = norm_rows(attended)
    grad_att = band.by_head(
        norm_back(ratio_ref[:, :width], att_hat, att_inv).astype(BF16)
    )
    pair_values = jnp.concatenate([proj_ref[:, columns(1)], tail_values], axis=0)
    grad_weights = band.join(dot(grad_att, pair_values, ROWS_BY_ROWS))
    grad_scores = band.split(grad_weights * slope * mask_ref[...])
    grad_values = dot(weights, grad_att, COLS_BY_COLS)
    pair_keys = jnp.concatenate([proj_ref[:, columns(3)], tail_keys], axis=0)
    grad_queries = band.pick_heads(dot(grad_scores, pair_keys)) / root
    grad_keys = dot(grad_scores, stack, COLS_BY_COLS) / root
    gated = (att_hat * proj_ref[:, columns(0)].astype(F32)).astype(BF16)
    out_ref[first, :] = (ev_ref[first, :].astype(F32) + dot(gated, w_out_ref[...])).astype(BF16)
    out_ref[last, :] = out_last_ref[...]
    own_pre = [
        (ratio_ref[:, width:] * att_hat).astype(BF16),
        ((grad_values[:window] + grads_ref[:, :width]) * slope_ref[:, columns(1)]).astype(BF16),
        (grad_queries * slope_ref[:, columns(2)]).astype(BF16),
        ((grad_keys[:window] + grads_ref[:, width:]) * slope_ref[:, columns(3)]).astype(BF16),
    ]
    tail_pre = {
        1: (grad_values[window:] * tail_values_slope).astype(BF16),
        3: (grad_keys[window:] * tail_keys_slope).astype(BF16),
    }
    left = jnp.concatenate([normed_ref[first, :], tail_normed], axis=0)
    own_total, back_total, in_blocks, bias_rows = None, None, [], []
    for i in range(4):
        part = dot(own_pre[i], w_in_ref[:, columns(i)], ROWS_BY_ROWS)
        own_total = part if own_total is None else own_total + part
        right = [own_pre[i]]
        if i in tail_pre:
            part = dot(tail_pre[i], w_in_ref[:, columns(i)], ROWS_BY_ROWS)
            back_total = part if back_total is None else back_total + part
            right.append(tail_pre[i])
        right = jnp.concatenate(right, axis=0)
        part = early_ref[:, columns(i)] + dot(left[: right.shape[0]], right, COLS_BY_COLS)
        in_blocks.append(part * scale)
        right = jnp.concatenate([right, pre_ref[:, columns(i)]], axis=0)
        bias_rows.append(jnp.sum(right.astype(F32), axis=0, keepdims=True) * scale)
    own_ref[...] = own_total
    part_out = early_ref[:, columns(4)] + dot(gated, cot_ref[first, :], COLS_BY_COLS)
    part_out = part_out * scale
    tile_row = lax.broadcasted_iota(jnp.int32, (GROUP, 128), 0)
    for piece in range(parts_ref.shape[0]):
        group, half = piece // 2, piece % 2
        here = slice(group * GROUP, (group + 1) * GROUP)
        tiles = [
            in_blocks[2 * half + k // 2][here, (k % 2) * 128 : (k % 2 + 1) * 128]
            for k in range(4)
        ]
        tiles.append(part_out[here, half * 128 : (half + 1) * 128])
        rest = back_total[
            piece // 4 * GROUP : (piece // 4 + 1) * GROUP,
            piece // 2 % 2 * 128 : (piece // 2 % 2 + 1) * 128,
        ]
        if piece % 2:
            rest = pltpu.roll(rest, BACK, 0)
        line = piece // 8
        bias = bias_rows[line // 2][:, line % 2 * 128 : (line % 2 + 1) * 128]
        tiles.append(jnp.where(tile_row < BACK, rest, jnp.broadcast_to(bias, (GROUP, 128))))
        parts_ref[piece] = jnp.concatenate(tiles, axis=0)[:PIECE].astype(BF16)


def whole(rows):
    return jnp.concatenate([rows.astype(F32), jnp.zeros((6 * GROUP - PIECE, 128), F32)], axis=0)


def near_kernel(parts_ref, sum_ref, back_ref):
    total = None
    for i in range(parts_ref.shape[0]):
        piece = whole(parts_ref[i])
        back_ref[i] = piece[5 * GROUP :]
        total = piece if total is None else total + piece
    sums = total[:PIECE].astype(BF16)
    for i in range(sum_ref.shape[0]):
        sum_ref[i] = sums


def far_kernel(sources, parts_ref, back_ref, sum_ref):
    total = whole(parts_ref[0])
    for i in range(1, parts_ref.shape[0]):
        total = total + whole(parts_ref[i])
    tile_row = lax.broadcasted_iota(jnp.int32, (GROUP, 128), 0)
    rest = total[5 * GROUP :]
    for i, source in enumerate(sources):
        back = jnp.zeros_like(rest) if source is None else back_ref[source]
        last = jnp.where(tile_row < BACK, back, rest)
        sum_ref[i] = jnp.concatenate([total[: 5 * GROUP], last], axis=0)[:PIECE].astype(BF16)


def unpack_kernel(
    places, all_ref, own_first_ref, own_last_ref, ev_ref, cot_ref, out_ref,
    w_in_hbm, b_in_hbm, w_out_hbm, grad_hbm, out_hbm,
    w_in_ref, b_in_ref, w_out_ref, grad_ref, sems,
):
    copies = []

    def send(source, target):
        copy = pltpu.make_async_copy(source, target, sems.at[len(copies)])
        copy.start()
        copies.append(copy)

    send(out_ref, out_hbm)
    tile_row = lax.broadcasted_iota(jnp.int32, (GROUP, 128), 0)
    lasts = []
    pieces = all_ref.shape[0]
    part = pieces // PARTS
    for piece in range(pieces):
        rows = whole(all_ref[places[piece]])
        group, half = piece // 2, piece % 2
        here = slice(group * GROUP, (group + 1) * GROUP)
        tiles = [rows[k * GROUP : (k + 1) * GROUP] for k in range(6)]
        w_in_ref[here, half * 512 : (half + 1) * 512] = jnp.concatenate(tiles[:4], axis=1)
        w_out_ref[here, half * 128 : (half + 1) * 128] = tiles[4]
        if piece % 8 == 0:
            b_in_ref[piece // 8 : piece // 8 + 1, :] = tiles[5][BACK : BACK + 1]
        lasts.append(tiles[5])
        if (piece + 1) % part == 0:
            done = pl.ds((piece + 1 - part) // 2 * GROUP, part // 2 * GROUP)
            send(w_in_ref.at[done], w_in_hbm.at[done])
    send(w_out_ref, w_out_hbm)
    send(b_in_ref, b_in_hbm)
    back = jnp.concatenate(
        [
            jnp.concatenate(
                [
                    jnp.where(tile_row < BACK, lasts[i], pltpu.roll(lasts[i + 1], BACK, 0))
                    for i in (4 * t, 4 * t + 2)
                ],
                axis=1,
            )
            for t in range(len(lasts) // 4)
        ],
        axis=0,
    )
    window = back.shape[0]
    for half, grad in enumerate((own_first_ref[...], own_last_ref[...] + back)):
        here = slice(half * window, (half + 1) * window)
        hat, inv = norm_rows(ev_ref[here, :].astype(F32))
        grad_ref[here, :] = (cot_ref[here, :].astype(F32) + norm_back(grad, hat, inv)).astype(BF16)
    send(grad_ref, grad_hbm)
    for copy in copies:
        copy.wait()


def call(kernel, outs, *args, spaces=None, scratch=(), flops=0, moved=0):
    spaces = spaces or [pltpu.VMEM] * len(args)
    args = [
        pltpu.with_memory_space_constraint(arg, space) if space == pltpu.HBM else arg
        for arg, space in zip(args, spaces)
    ]
    return pl.pallas_call(
        kernel,
        out_shape=[
            pltpu.VMEM(shape, kind) if KEPT in place else jax.ShapeDtypeStruct(shape, kind)
            for shape, kind, *place in outs
        ],
        in_specs=[pl.BlockSpec(memory_space=space) for space in spaces],
        out_specs=[
            pl.BlockSpec(memory_space=SENT if SENT in place else pltpu.VMEM)
            for _, _, *place in outs
        ],
        scratch_shapes=scratch,
        compiler_params=pltpu.CompilerParams(vmem_limit_bytes=24 * 1024 * 1024),
        cost_estimate=pl.CostEstimate(flops=flops, bytes_accessed=moved, transcendentals=0),
    )(*args)


def on_device(
    events, cotangent, bucket_ids, history_lengths, w_in, b_in, w_out, pos_table, time_table
):
    rows, width = events.shape[1:]
    heads, window = pos_table.shape
    slabs = lax.axis_size(SEQ)
    scale = 1.0 / math.sqrt(lax.axis_size(BATCH) * slabs * rows)
    near, far = lax.axis_size(NEAR), lax.axis_size(FAR)
    moved = lax.ppermute(events, SEQ, [(i, i + 1) for i in range(slabs - 1)])
    half = (window, width)
    band = (heads * window, window)
    own_last, *kept = call(
        own_kernel,
        [
            (shape, kind, KEPT)
            for shape, kind in [
                (half, BF16), (half, BF16), ((window, 4 * width), BF16), (half, F32),
                ((rows, width), BF16), ((window, 4 * width), BF16), ((window, 4 * width), F32),
                (band, F32), (band, F32), ((window, 2 * width), F32),
                ((heads * window, width), BF16), (half, F32), ((window, 2 * width), F32),
                ((width, 5 * width), F32),
                ((rows, width), BF16), ((rows, width), BF16), (w_in.shape, BF16),
                ((1, 4 * width), F32), (w_out.shape, BF16),
            ]
        ],
        history_lengths, events[0], cotangent[0], bucket_ids[0], w_in, b_in[None], w_out,
        pos_table, time_table,
        spaces=[pltpu.SMEM] + [pltpu.HBM] * 8,
        scratch=[
            pltpu.VMEM((rows, window), jnp.int32),
            pltpu.VMEM(pos_table.shape, F32),
            pltpu.VMEM(time_table.shape, F32),
            pltpu.SemaphoreType.DMA((8,)),
        ],
        flops=10**9, moved=10**7,
    )
    own_last, kept = kept[2], [own_last, *kept[:2], *kept[3:]]
    ev, cot = kept[13:15]
    layer_out, parts, own_first = call(
        functools.partial(edge_kernel, scale),
        [((rows, width), BF16, KEPT), ((near, PIECE, 128), BF16, KEPT), (half, F32, KEPT)],
        moved, *kept,
        flops=10**9, moved=10**7,
    )
    zl = lax.axis_size("zl")
    order = [(i + FIRST_OUT) % near for i in range(near)]
    back_order = [(i + FIRST_BACK) % near for i in range(near)]
    places = [back_order.index(i) for i in order]
    sources = [
        order.index(i + zl) if i // zl % slabs < slabs - 1 else None for i in back_order
    ]
    parts = lax.all_to_all(parts, NEAR, 0, 0, axis_index_groups=[order])
    sums, back = call(
        near_kernel, [((far, PIECE, 128), BF16, KEPT), ((near, GROUP, 128), F32, KEPT)], parts
    )
    sums = lax.all_to_all(
        sums, FAR, 0, 0, axis_index_groups=[[(i + 5) % far for i in range(far)]]
    )
    (sums,) = call(
        functools.partial(far_kernel, sources), [((near, PIECE, 128), BF16, KEPT)], sums, back
    )
    sums = lax.all_to_all(sums, NEAR, 0, 0, axis_index_groups=[back_order])
    sum_in, sum_bias, sum_out, grad_events, layer_out = call(
        functools.partial(unpack_kernel, places),
        [
            ((width, 4 * width), F32, SENT), ((8, 128), F32, SENT), ((width, width), F32, SENT),
            ((rows, width), BF16, SENT), ((rows, width), BF16, SENT),
        ],
        sums, own_first, own_last, ev, cot, layer_out,
        scratch=[
            pltpu.VMEM((width, 4 * width), F32), pltpu.VMEM((8, 128), F32),
            pltpu.VMEM((width, width), F32), pltpu.VMEM((rows, width), BF16),
            pltpu.SemaphoreType.DMA((PARTS + 4,)),
        ],
    )
    return (layer_out[None], grad_events[None], sum_in, sum_bias.reshape(4 * width), sum_out)


def solution(mesh):
    fine = Mesh(
        mesh.devices.reshape(2, 8, 2, 2, 4, 2), ("yl", "zh", "zl", "yh", "x", "c")
    )
    slabs = P(BATCH, SEQ, None)
    return jax.shard_map(
        on_device,
        mesh=fine,
        in_specs=(slabs, slabs, slabs, P(BATCH), P(), P(), P(), P(), P()),
        out_specs=(slabs, slabs, P(), P(), P()),
        check_vma=False,
    )
```

```python
import functools
import math

import jax
import jax.numpy as jnp
from jax import lax
from jax.experimental import pallas as pl
from jax.experimental.pallas import tpu as pltpu
from jax.sharding import Mesh, PartitionSpec as P

EPS = 1e-05
F32 = jnp.float32
BF16 = jnp.bfloat16
NEAR = ("yl", "yh", "x", "c", "zl")
FAR = ("zh",)
BATCH = ("yl", "zh", "zl")
SEQ = ("yh", "x", "c")
GROUP = 8
PIECE = 6 * GROUP
BACK = 4
PARTS = 4
FIRST_OUT = 50
FIRST_BACK = 58
KEPT = pltpu.VMEM
SENT = pltpu.HBM


def norm_rows(values):
    row_mean = jnp.mean(values, axis=-1, keepdims=True)
    centred = values - row_mean
    variance = jnp.mean(centred * centred, axis=-1, keepdims=True)
    inv_std = lax.rsqrt(variance + EPS)
    return (centred * inv_std, inv_std)


def norm_back(upstream, normed, inv_std):
    first = jnp.mean(upstream, axis=-1, keepdims=True)
    second = jnp.mean(upstream * normed, axis=-1, keepdims=True)
    return inv_std * (upstream - first - normed * second)


def silu_and_slope(pre_act):
    sigmoid = jax.nn.sigmoid(pre_act)
    value = pre_act * sigmoid
    return (value, sigmoid * (1.0 + pre_act * (1.0 - sigmoid)))


def dot(left, right, dims=((1,), (0,))):
    return lax.dot_general(left, right, (dims, ((), ())), preferred_element_type=F32)


ROWS_BY_ROWS = ((1,), (1,))
COLS_BY_COLS = ((0,), (0,))


def lane_gather(table, index):
    return jnp.take_along_axis(table, index, axis=1, mode="promise_in_bounds")


class Band:
    def __init__(self, heads, window, width):
        self.heads, self.window, self.head = heads, window, width // heads
        row = lax.broadcasted_iota(jnp.int32, (window, window), 0)
        lane = lax.broadcasted_iota(jnp.int32, (window, window), 1)
        self.offset = (row - lane) & (window - 1)
        self.row = jnp.concatenate([row] * heads, axis=0)
        self.recent = jnp.concatenate([lane <= row] * heads, axis=0)
        self.column_head = lax.broadcasted_iota(jnp.int32, (window, width), 1) // self.head

    def bias(self, bucket_rows, pos_ref, time_ref):
        shape = (self.window, self.window)
        buckets = lane_gather(bucket_rows, self.offset)
        return jnp.concatenate(
            [
                lane_gather(jnp.broadcast_to(pos_ref[h : h + 1, :], shape), self.offset)
                + lane_gather(jnp.broadcast_to(time_ref[h : h + 1, :], shape), buckets)
                for h in range(self.heads)
            ],
            axis=0,
        )

    def by_head(self, block):
        zero = jnp.zeros_like(block)
        return jnp.concatenate(
            [jnp.where(self.column_head == h, block, zero) for h in range(self.heads)], axis=0
        )

    def pick_heads(self, stack):
        total = stack[: self.window]
        for h in range(1, self.heads):
            part = stack[h * self.window : (h + 1) * self.window]
            total = jnp.where(self.column_head == h, part, total)
        return total

    def split(self, band):
        zero = jnp.zeros_like(band)
        return jnp.concatenate(
            [jnp.where(self.recent, band, zero), jnp.where(self.recent, zero, band)], axis=1
        ).astype(BF16)

    def join(self, pair):
        return jnp.where(self.recent, pair[:, : self.window], pair[:, self.window :])

    def block(self, queries, pair_keys, pair_values, gate, bias, allowed, ev, cot, w_out):
        root = math.sqrt(self.head)
        stack_queries = self.by_head(queries)
        scores = self.join(dot(stack_queries, pair_keys, ROWS_BY_ROWS)) / root + bias
        act, slope = silu_and_slope(scores)
        weights = self.split(jnp.where(allowed, act * (1.0 / self.window), 0.0))
        att_hat, att_inv = norm_rows(self.pick_heads(dot(weights, pair_values)))
        gate_u = gate.astype(F32)
        gated = (att_hat * gate_u).astype(BF16)
        out = (ev.astype(F32) + dot(gated, w_out)).astype(BF16)
        upstream = dot(cot, w_out, ROWS_BY_ROWS)
        grad_att = self.by_head(norm_back(upstream * gate_u, att_hat, att_inv).astype(BF16))
        grad_weights = self.join(dot(grad_att, pair_values, ROWS_BY_ROWS))
        grad_scores = self.split(
            jnp.where(allowed, grad_weights * slope * (1.0 / self.window), 0.0)
        )
        grad_values = dot(weights, grad_att, COLS_BY_COLS)
        grad_queries = self.pick_heads(dot(grad_scores, pair_keys)) / root
        grad_keys = dot(grad_scores, stack_queries, COLS_BY_COLS) / root
        return (out, gated, upstream * att_hat, grad_values, grad_queries, grad_keys)


def own_kernel(
    length_ref, ev_hbm, cot_hbm, ids_hbm, w_in_hbm, b_in_hbm, w_out_hbm, pos_hbm, time_hbm,
    out_ref, gated_ref, pre_ref, own_ref, normed_ref, proj_ref, slope_ref, base_ref, mask_ref,
    grads_ref, stack_ref, att_ref, ratio_ref, ev_ref, cot_ref, w_in_ref, b_in_ref, w_out_ref,
    ids_ref, pos_ref, time_ref, sems,
):
    pairs = [
        (ev_hbm, ev_ref), (w_in_hbm, w_in_ref), (b_in_hbm, b_in_ref), (ids_hbm, ids_ref),
        (pos_hbm, pos_ref), (time_hbm, time_ref), (cot_hbm, cot_ref), (w_out_hbm, w_out_ref),
    ]
    copies = [pltpu.make_async_copy(a, b, sems.at[i]) for i, (a, b) in enumerate(pairs)]
    for copy in copies:
        copy.start()
    rows, width = ev_ref.shape
    heads, window = pos_ref.shape
    slab = lax.axis_index(SEQ)
    band = Band(heads, window, width)
    copies[0].wait()
    hat, _ = norm_rows(ev_ref[...].astype(F32))
    normed = hat.astype(BF16)
    normed_ref[...] = normed
    copies[1].wait()
    copies[2].wait()
    value, slope = silu_and_slope(dot(normed, w_in_ref[...]) + b_in_ref[...])
    projected = value.astype(BF16)
    first, last = slice(0, window), slice(window, 2 * window)
    proj_ref[...] = projected[first]
    slope_ref[...] = slope[first]
    gate, values, queries, keys = [projected[:, i * width : (i + 1) * width] for i in range(4)]
    for copy in copies[3:]:
        copy.wait()
    real = length_ref[0] - slab * rows
    bias = band.bias(ids_ref[last, :], pos_ref, time_ref)
    out, gated, grad_gate, grad_values, grad_queries, grad_keys = band.block(
        queries[last],
        jnp.concatenate([keys[last], keys[first]], axis=0),
        jnp.concatenate([values[last], values[first]], axis=0),
        gate[last], bias, band.row < real - window, ev_ref[last, :], cot_ref[last, :],
        w_out_ref[...],
    )
    out_ref[...] = out
    gated_ref[...] = gated
    grads_ref[:, :width] = grad_values[window:]
    grads_ref[:, width:] = grad_keys[window:]
    grads = jnp.concatenate(
        [grad_gate, grad_values[:window], grad_queries, grad_keys[:window]], axis=1
    )
    pre = (grads * slope[last]).astype(BF16)
    pre_ref[...] = pre
    own_ref[...] = dot(pre, w_in_ref[...], ROWS_BY_ROWS)

    stack = band.by_head(queries[first])
    stack_ref[...] = stack
    near = dot(stack, keys[first], ROWS_BY_ROWS) / math.sqrt(band.head)
    bias = band.bias(ids_ref[first, :], pos_ref, time_ref)
    base = jnp.where(band.recent, near, 0.0) + bias
    base_ref[...] = base
    allowed = (band.row < real) & (band.recent | (slab > 0))
    mask = jnp.where(allowed, 1.0 / window, 0.0)
    mask_ref[...] = mask
    act, _ = silu_and_slope(base)
    weights = jnp.where(band.recent, act * mask, 0.0).astype(BF16)
    att_ref[...] = band.pick_heads(dot(weights, values[first]))
    upstream = dot(cot_ref[first, :], w_out_ref[...], ROWS_BY_ROWS)
    ratio_ref[:, :width] = upstream * gate[first].astype(F32)
    ratio_ref[:, width:] = upstream * slope[first, :width]


def edge_kernel(
    scale, moved_ref, out_last_ref, gated_ref, pre_ref, normed_ref, proj_ref, slope_ref, base_ref,
    mask_ref, grads_ref, stack_ref, att_ref, ratio_ref, ev_ref, cot_ref, w_in_ref, b_in_ref,
    w_out_ref,
    out_ref, parts_ref, own_ref,
):
    rows, width = ev_ref.shape
    window = out_last_ref.shape[0]
    heads = base_ref.shape[0] // window
    band = Band(heads, window, width)
    root = math.sqrt(band.head)
    first, last = slice(0, window), slice(window, 2 * window)
    tail_hat, _ = norm_rows(moved_ref[0, rows - window :, :].astype(F32))
    tail_normed = tail_hat.astype(BF16)

    def columns(i):
        return slice(i * width, (i + 1) * width)

    def project(i):
        pre_act = dot(tail_normed, w_in_ref[:, columns(i)]) + b_in_ref[:, columns(i)]
        value, slope = silu_and_slope(pre_act)
        return (value.astype(BF16), slope)

    tail_keys, tail_keys_slope = project(3)
    stack = stack_ref[...]
    behind = dot(stack, tail_keys, ROWS_BY_ROWS) / root
    tail_values, tail_values_slope = project(1)
    act, slope = silu_and_slope(base_ref[...] + jnp.where(band.recent, 0.0, behind))
    weights = band.split(act * mask_ref[...])
    attended = att_ref[...] + band.pick_heads(dot(weights[:, window:], tail_values))
    att_hat, att_inv = norm_rows(attended)
    grad_att = band.by_head(
        norm_back(ratio_ref[:, :width], att_hat, att_inv).astype(BF16)
    )
    pair_values = jnp.concatenate([proj_ref[:, columns(1)], tail_values], axis=0)
    grad_weights = band.join(dot(grad_att, pair_values, ROWS_BY_ROWS))
    grad_scores = band.split(grad_weights * slope * mask_ref[...])
    grad_values = dot(weights, grad_att, COLS_BY_COLS)
    pair_keys = jnp.concatenate([proj_ref[:, columns(3)], tail_keys], axis=0)
    grad_queries = band.pick_heads(dot(grad_scores, pair_keys)) / root
    grad_keys = dot(grad_scores, stack, COLS_BY_COLS) / root
    gated = (att_hat * proj_ref[:, columns(0)].astype(F32)).astype(BF16)
    out_ref[first, :] = (ev_ref[first, :].astype(F32) + dot(gated, w_out_ref[...])).astype(BF16)
    out_ref[last, :] = out_last_ref[...]
    own_pre = [
        (ratio_ref[:, width:] * att_hat).astype(BF16),
        ((grad_values[:window] + grads_ref[:, :width]) * slope_ref[:, columns(1)]).astype(BF16),
        (grad_queries * slope_ref[:, columns(2)]).astype(BF16),
        ((grad_keys[:window] + grads_ref[:, width:]) * slope_ref[:, columns(3)]).astype(BF16),
    ]
    tail_pre = {
        1: (grad_values[window:] * tail_values_slope).astype(BF16),
        3: (grad_keys[window:] * tail_keys_slope).astype(BF16),
    }
    left = jnp.concatenate([normed_ref[...], tail_normed], axis=0)
    own_total, back_total, in_blocks, bias_rows = None, None, [], []
    for i in range(4):
        part = dot(own_pre[i], w_in_ref[:, columns(i)], ROWS_BY_ROWS)
        own_total = part if own_total is None else own_total + part
        right = [own_pre[i], pre_ref[:, columns(i)]]
        if i in tail_pre:
            part = dot(tail_pre[i], w_in_ref[:, columns(i)], ROWS_BY_ROWS)
            back_total = part if back_total is None else back_total + part
            right.append(tail_pre[i])
        right = jnp.concatenate(right, axis=0)
        in_blocks.append(dot(left[: right.shape[0]], right, COLS_BY_COLS) * scale)
        bias_rows.append(jnp.sum(right.astype(F32), axis=0, keepdims=True) * scale)
    own_ref[...] = own_total
    part_out = dot(
        jnp.concatenate([gated, gated_ref[...]], axis=0), cot_ref[...], COLS_BY_COLS
    ) * scale
    tile_row = lax.broadcasted_iota(jnp.int32, (GROUP, 128), 0)
    for piece in range(parts_ref.shape[0]):
        group, half = piece // 2, piece % 2
        here = slice(group * GROUP, (group + 1) * GROUP)
        tiles = [
            in_blocks[2 * half + k // 2][here, (k % 2) * 128 : (k % 2 + 1) * 128]
            for k in range(4)
        ]
        tiles.append(part_out[here, half * 128 : (half + 1) * 128])
        rest = back_total[
            piece // 4 * GROUP : (piece // 4 + 1) * GROUP,
            piece // 2 % 2 * 128 : (piece // 2 % 2 + 1) * 128,
        ]
        if piece % 2:
            rest = pltpu.roll(rest, BACK, 0)
        line = piece // 8
        bias = bias_rows[line // 2][:, line % 2 * 128 : (line % 2 + 1) * 128]
        tiles.append(jnp.where(tile_row < BACK, rest, jnp.broadcast_to(bias, (GROUP, 128))))
        parts_ref[piece] = jnp.concatenate(tiles, axis=0).astype(BF16)


def near_kernel(parts_ref, sum_ref, back_ref):
    total = None
    for i in range(parts_ref.shape[0]):
        piece = parts_ref[i].astype(F32)
        back_ref[i] = piece[5 * GROUP :]
        total = piece if total is None else total + piece
    sums = total.astype(BF16)
    for i in range(sum_ref.shape[0]):
        sum_ref[i] = sums


def far_kernel(sources, parts_ref, back_ref, sum_ref):
    total = parts_ref[0].astype(F32)
    for i in range(1, parts_ref.shape[0]):
        total = total + parts_ref[i].astype(F32)
    tile_row = lax.broadcasted_iota(jnp.int32, (GROUP, 128), 0)
    rest = total[5 * GROUP :]
    for i, source in enumerate(sources):
        back = jnp.zeros_like(rest) if source is None else back_ref[source]
        last = jnp.where(tile_row < BACK, back, rest)
        sum_ref[i] = jnp.concatenate([total[: 5 * GROUP], last], axis=0).astype(BF16)


def unpack_kernel(
    places, all_ref, own_first_ref, own_last_ref, ev_ref, cot_ref, out_ref,
    w_in_hbm, b_in_hbm, w_out_hbm, grad_hbm, out_hbm,
    w_in_ref, b_in_ref, w_out_ref, grad_ref, sems,
):
    copies = []

    def send(source, target):
        copy = pltpu.make_async_copy(source, target, sems.at[len(copies)])
        copy.start()
        copies.append(copy)

    send(out_ref, out_hbm)
    tile_row = lax.broadcasted_iota(jnp.int32, (GROUP, 128), 0)
    lasts = []
    pieces = all_ref.shape[0]
    part = pieces // PARTS
    for piece in range(pieces):
        rows = all_ref[places[piece]].astype(F32)
        group, half = piece // 2, piece % 2
        here = slice(group * GROUP, (group + 1) * GROUP)
        tiles = [rows[k * GROUP : (k + 1) * GROUP] for k in range(6)]
        w_in_ref[here, half * 512 : (half + 1) * 512] = jnp.concatenate(tiles[:4], axis=1)
        w_out_ref[here, half * 128 : (half + 1) * 128] = tiles[4]
        if piece % 8 == 0:
            b_in_ref[piece // 8 : piece // 8 + 1, :] = tiles[5][BACK : BACK + 1]
        lasts.append(tiles[5])
        if (piece + 1) % part == 0:
            done = pl.ds((piece + 1 - part) // 2 * GROUP, part // 2 * GROUP)
            send(w_in_ref.at[done], w_in_hbm.at[done])
    send(w_out_ref, w_out_hbm)
    send(b_in_ref, b_in_hbm)
    back = jnp.concatenate(
        [
            jnp.concatenate(
                [
                    jnp.where(tile_row < BACK, lasts[i], pltpu.roll(lasts[i + 1], BACK, 0))
                    for i in (4 * t, 4 * t + 2)
                ],
                axis=1,
            )
            for t in range(len(lasts) // 4)
        ],
        axis=0,
    )
    window = back.shape[0]
    for half, grad in enumerate((own_first_ref[...], own_last_ref[...] + back)):
        here = slice(half * window, (half + 1) * window)
        hat, inv = norm_rows(ev_ref[here, :].astype(F32))
        grad_ref[here, :] = (cot_ref[here, :].astype(F32) + norm_back(grad, hat, inv)).astype(BF16)
    send(grad_ref, grad_hbm)
    for copy in copies:
        copy.wait()


def call(kernel, outs, *args, spaces=None, scratch=(), flops=0, moved=0):
    spaces = spaces or [pltpu.VMEM] * len(args)
    args = [
        pltpu.with_memory_space_constraint(arg, space) if space == pltpu.HBM else arg
        for arg, space in zip(args, spaces)
    ]
    return pl.pallas_call(
        kernel,
        out_shape=[
            pltpu.VMEM(shape, kind) if KEPT in place else jax.ShapeDtypeStruct(shape, kind)
            for shape, kind, *place in outs
        ],
        in_specs=[pl.BlockSpec(memory_space=space) for space in spaces],
        out_specs=[
            pl.BlockSpec(memory_space=SENT if SENT in place else pltpu.VMEM)
            for _, _, *place in outs
        ],
        scratch_shapes=scratch,
        compiler_params=pltpu.CompilerParams(vmem_limit_bytes=24 * 1024 * 1024),
        cost_estimate=pl.CostEstimate(flops=flops, bytes_accessed=moved, transcendentals=0),
    )(*args)


def on_device(
    events, cotangent, bucket_ids, history_lengths, w_in, b_in, w_out, pos_table, time_table
):
    rows, width = events.shape[1:]
    heads, window = pos_table.shape
    slabs = lax.axis_size(SEQ)
    scale = 1.0 / math.sqrt(lax.axis_size(BATCH) * slabs * rows)
    near, far = lax.axis_size(NEAR), lax.axis_size(FAR)
    moved = lax.ppermute(events, SEQ, [(i, i + 1) for i in range(slabs - 1)])
    half = (window, width)
    band = (heads * window, window)
    own_last, *kept = call(
        own_kernel,
        [
            (shape, kind, KEPT)
            for shape, kind in [
                (half, BF16), (half, BF16), ((window, 4 * width), BF16), (half, F32),
                ((rows, width), BF16), ((window, 4 * width), BF16), ((window, 4 * width), F32),
                (band, F32), (band, F32), ((window, 2 * width), F32),
                ((heads * window, width), BF16), (half, F32), ((window, 2 * width), F32),
                ((rows, width), BF16), ((rows, width), BF16), (w_in.shape, BF16),
                ((1, 4 * width), F32), (w_out.shape, BF16),
            ]
        ],
        history_lengths, events[0], cotangent[0], bucket_ids[0], w_in, b_in[None], w_out,
        pos_table, time_table,
        spaces=[pltpu.SMEM] + [pltpu.HBM] * 8,
        scratch=[
            pltpu.VMEM((rows, window), jnp.int32),
            pltpu.VMEM(pos_table.shape, F32),
            pltpu.VMEM(time_table.shape, F32),
            pltpu.SemaphoreType.DMA((8,)),
        ],
        flops=10**9, moved=10**7,
    )
    own_last, kept = kept[2], [own_last, *kept[:2], *kept[3:]]
    ev, cot = kept[12:14]
    layer_out, parts, own_first = call(
        functools.partial(edge_kernel, scale),
        [((rows, width), BF16, KEPT), ((near, PIECE, 128), BF16, KEPT), (half, F32, KEPT)],
        moved, *kept,
        flops=10**9, moved=10**7,
    )
    zl = lax.axis_size("zl")
    order = [(i + FIRST_OUT) % near for i in range(near)]
    back_order = [(i + FIRST_BACK) % near for i in range(near)]
    places = [back_order.index(i) for i in order]
    sources = [
        order.index(i + zl) if i // zl % slabs < slabs - 1 else None for i in back_order
    ]
    parts = lax.all_to_all(parts, NEAR, 0, 0, axis_index_groups=[order])
    sums, back = call(
        near_kernel, [((far, PIECE, 128), BF16, KEPT), ((near, GROUP, 128), F32, KEPT)], parts
    )
    sums = lax.all_to_all(
        sums, FAR, 0, 0, axis_index_groups=[[5, 4, 3, 2, 1, 0, 7, 6]]
    )
    (sums,) = call(
        functools.partial(far_kernel, sources), [((near, PIECE, 128), BF16, KEPT)], sums, back
    )
    sums = lax.all_to_all(sums, NEAR, 0, 0, axis_index_groups=[back_order])
    sum_in, sum_bias, sum_out, grad_events, layer_out = call(
        functools.partial(unpack_kernel, places),
        [
            ((width, 4 * width), F32, SENT), ((8, 128), F32, SENT), ((width, width), F32, SENT),
            ((rows, width), BF16, SENT), ((rows, width), BF16, SENT),
        ],
        sums, own_first, own_last, ev, cot, layer_out,
        scratch=[
            pltpu.VMEM((width, 4 * width), F32), pltpu.VMEM((8, 128), F32),
            pltpu.VMEM((width, width), F32), pltpu.VMEM((rows, width), BF16),
            pltpu.SemaphoreType.DMA((PARTS + 4,)),
        ],
    )
    return (layer_out[None], grad_events[None], sum_in, sum_bias.reshape(4 * width), sum_out)


def solution(mesh):
    fine = Mesh(
        mesh.devices.reshape(2, 8, 2, 2, 4, 2), ("yl", "zh", "zl", "yh", "x", "c")
    )
    slabs = P(BATCH, SEQ, None)
    return jax.shard_map(
        on_device,
        mesh=fine,
        in_specs=(slabs, slabs, slabs, P(BATCH), P(), P(), P(), P(), P()),
        out_specs=(slabs, slabs, P(), P(), P()),
        check_vma=False,
    )
```

```python
import functools
import math

import jax
import jax.numpy as jnp
from jax import lax
from jax.experimental import pallas as pl
from jax.experimental.pallas import tpu as pltpu
from jax.sharding import Mesh, PartitionSpec as P

EPS = 1e-05
F32 = jnp.float32
BF16 = jnp.bfloat16
NEAR = ("yl", "yh", "x", "c", "zl")
FAR = ("zh",)
BATCH = ("yl", "zh", "zl")
SEQ = ("yh", "x", "c")
GROUP = 8
PIECE = 6 * GROUP
BACK = 4
PARTS = 4
FIRST_OUT = 18
FIRST_BACK = 58
KEPT = pltpu.VMEM
SENT = pltpu.HBM


def norm_rows(values):
    row_mean = jnp.mean(values, axis=-1, keepdims=True)
    centred = values - row_mean
    variance = jnp.mean(centred * centred, axis=-1, keepdims=True)
    inv_std = lax.rsqrt(variance + EPS)
    return (centred * inv_std, inv_std)


def norm_back(upstream, normed, inv_std):
    first = jnp.mean(upstream, axis=-1, keepdims=True)
    second = jnp.mean(upstream * normed, axis=-1, keepdims=True)
    return inv_std * (upstream - first - normed * second)


def silu_and_slope(pre_act):
    sigmoid = jax.nn.sigmoid(pre_act)
    value = pre_act * sigmoid
    return (value, sigmoid * (1.0 + pre_act * (1.0 - sigmoid)))


def dot(left, right, dims=((1,), (0,))):
    return lax.dot_general(left, right, (dims, ((), ())), preferred_element_type=F32)


ROWS_BY_ROWS = ((1,), (1,))
COLS_BY_COLS = ((0,), (0,))


def lane_gather(table, index):
    return jnp.take_along_axis(table, index, axis=1, mode="promise_in_bounds")


class Band:
    def __init__(self, heads, window, width):
        self.heads, self.window, self.head = heads, window, width // heads
        row = lax.broadcasted_iota(jnp.int32, (window, window), 0)
        lane = lax.broadcasted_iota(jnp.int32, (window, window), 1)
        self.offset = (row - lane) & (window - 1)
        self.row = jnp.concatenate([row] * heads, axis=0)
        self.recent = jnp.concatenate([lane <= row] * heads, axis=0)
        self.column_head = lax.broadcasted_iota(jnp.int32, (window, width), 1) // self.head

    def bias(self, bucket_rows, pos_ref, time_ref):
        shape = (self.window, self.window)
        buckets = lane_gather(bucket_rows, self.offset)
        return jnp.concatenate(
            [
                lane_gather(jnp.broadcast_to(pos_ref[h : h + 1, :], shape), self.offset)
                + lane_gather(jnp.broadcast_to(time_ref[h : h + 1, :], shape), buckets)
                for h in range(self.heads)
            ],
            axis=0,
        )

    def by_head(self, block):
        zero = jnp.zeros_like(block)
        return jnp.concatenate(
            [jnp.where(self.column_head == h, block, zero) for h in range(self.heads)], axis=0
        )

    def pick_heads(self, stack):
        total = stack[: self.window]
        for h in range(1, self.heads):
            part = stack[h * self.window : (h + 1) * self.window]
            total = jnp.where(self.column_head == h, part, total)
        return total

    def split(self, band):
        zero = jnp.zeros_like(band)
        return jnp.concatenate(
            [jnp.where(self.recent, band, zero), jnp.where(self.recent, zero, band)], axis=1
        ).astype(BF16)

    def join(self, pair):
        return jnp.where(self.recent, pair[:, : self.window], pair[:, self.window :])

    def block(self, queries, pair_keys, pair_values, gate, bias, allowed, ev, cot, w_out):
        root = math.sqrt(self.head)
        stack_queries = self.by_head(queries)
        scores = self.join(dot(stack_queries, pair_keys, ROWS_BY_ROWS)) / root + bias
        act, slope = silu_and_slope(scores)
        weights = self.split(jnp.where(allowed, act * (1.0 / self.window), 0.0))
        att_hat, att_inv = norm_rows(self.pick_heads(dot(weights, pair_values)))
        gate_u = gate.astype(F32)
        gated = (att_hat * gate_u).astype(BF16)
        out = (ev.astype(F32) + dot(gated, w_out)).astype(BF16)
        upstream = dot(cot, w_out, ROWS_BY_ROWS)
        grad_att = self.by_head(norm_back(upstream * gate_u, att_hat, att_inv).astype(BF16))
        grad_weights = self.join(dot(grad_att, pair_values, ROWS_BY_ROWS))
        grad_scores = self.split(
            jnp.where(allowed, grad_weights * slope * (1.0 / self.window), 0.0)
        )
        grad_values = dot(weights, grad_att, COLS_BY_COLS)
        grad_queries = self.pick_heads(dot(grad_scores, pair_keys)) / root
        grad_keys = dot(grad_scores, stack_queries, COLS_BY_COLS) / root
        return (out, gated, upstream * att_hat, grad_values, grad_queries, grad_keys)


def own_kernel(
    length_ref, ev_hbm, cot_hbm, ids_hbm, w_in_hbm, b_in_hbm, w_out_hbm, pos_hbm, time_hbm,
    out_ref, gated_ref, pre_ref, own_ref, normed_ref, proj_ref, slope_ref, base_ref, mask_ref,
    grads_ref, stack_ref, att_ref, ratio_ref, ev_ref, cot_ref, w_in_ref, b_in_ref, w_out_ref,
    ids_ref, pos_ref, time_ref, sems,
):
    pairs = [
        (ev_hbm, ev_ref), (w_in_hbm, w_in_ref), (b_in_hbm, b_in_ref), (ids_hbm, ids_ref),
        (pos_hbm, pos_ref), (time_hbm, time_ref), (cot_hbm, cot_ref), (w_out_hbm, w_out_ref),
    ]
    copies = [pltpu.make_async_copy(a, b, sems.at[i]) for i, (a, b) in enumerate(pairs)]
    for copy in copies:
        copy.start()
    rows, width = ev_ref.shape
    heads, window = pos_ref.shape
    slab = lax.axis_index(SEQ)
    band = Band(heads, window, width)
    copies[0].wait()
    hat, _ = norm_rows(ev_ref[...].astype(F32))
    normed = hat.astype(BF16)
    normed_ref[...] = normed
    copies[1].wait()
    copies[2].wait()
    value, slope = silu_and_slope(dot(normed, w_in_ref[...]) + b_in_ref[...])
    projected = value.astype(BF16)
    first, last = slice(0, window), slice(window, 2 * window)
    proj_ref[...] = projected[first]
    slope_ref[...] = slope[first]
    gate, values, queries, keys = [projected[:, i * width : (i + 1) * width] for i in range(4)]
    for copy in copies[3:]:
        copy.wait()
    real = length_ref[0] - slab * rows
    bias = band.bias(ids_ref[last, :], pos_ref, time_ref)
    out, gated, grad_gate, grad_values, grad_queries, grad_keys = band.block(
        queries[last],
        jnp.concatenate([keys[last], keys[first]], axis=0),
        jnp.concatenate([values[last], values[first]], axis=0),
        gate[last], bias, band.row < real - window, ev_ref[last, :], cot_ref[last, :],
        w_out_ref[...],
    )
    out_ref[...] = out
    gated_ref[...] = gated
    grads_ref[:, :width] = grad_values[window:]
    grads_ref[:, width:] = grad_keys[window:]
    grads = jnp.concatenate(
        [grad_gate, grad_values[:window], grad_queries, grad_keys[:window]], axis=1
    )
    pre = (grads * slope[last]).astype(BF16)
    pre_ref[...] = pre
    own_ref[...] = dot(pre, w_in_ref[...], ROWS_BY_ROWS)

    stack = band.by_head(queries[first])
    stack_ref[...] = stack
    near = dot(stack, keys[first], ROWS_BY_ROWS) / math.sqrt(band.head)
    bias = band.bias(ids_ref[first, :], pos_ref, time_ref)
    base = jnp.where(band.recent, near, 0.0) + bias
    base_ref[...] = base
    allowed = (band.row < real) & (band.recent | (slab > 0))
    mask = jnp.where(allowed, 1.0 / window, 0.0)
    mask_ref[...] = mask
    act, _ = silu_and_slope(base)
    weights = jnp.where(band.recent, act * mask, 0.0).astype(BF16)
    att_ref[...] = band.pick_heads(dot(weights, values[first]))
    upstream = dot(cot_ref[first, :], w_out_ref[...], ROWS_BY_ROWS)
    ratio_ref[:, :width] = upstream * gate[first].astype(F32)
    ratio_ref[:, width:] = upstream * slope[first, :width]


def edge_kernel(
    scale, moved_ref, out_last_ref, gated_ref, pre_ref, normed_ref, proj_ref, slope_ref, base_ref,
    mask_ref, grads_ref, stack_ref, att_ref, ratio_ref, ev_ref, cot_ref, w_in_ref, b_in_ref,
    w_out_ref,
    out_ref, parts_ref, own_ref,
):
    rows, width = ev_ref.shape
    window = out_last_ref.shape[0]
    heads = base_ref.shape[0] // window
    band = Band(heads, window, width)
    root = math.sqrt(band.head)
    first, last = slice(0, window), slice(window, 2 * window)
    tail_hat, _ = norm_rows(moved_ref[0, rows - window :, :].astype(F32))
    tail_normed = tail_hat.astype(BF16)

    def columns(i):
        return slice(i * width, (i + 1) * width)

    def project(i):
        pre_act = dot(tail_normed, w_in_ref[:, columns(i)]) + b_in_ref[:, columns(i)]
        value, slope = silu_and_slope(pre_act)
        return (value.astype(BF16), slope)

    tail_keys, tail_keys_slope = project(3)
    stack = stack_ref[...]
    behind = dot(stack, tail_keys, ROWS_BY_ROWS) / root
    tail_values, tail_values_slope = project(1)
    act, slope = silu_and_slope(base_ref[...] + jnp.where(band.recent, 0.0, behind))
    weights = band.split(act * mask_ref[...])
    attended = att_ref[...] + band.pick_heads(dot(weights[:, window:], tail_values))
    att_hat, att_inv = norm_rows(attended)
    grad_att = band.by_head(
        norm_back(ratio_ref[:, :width], att_hat, att_inv).astype(BF16)
    )
    pair_values = jnp.concatenate([proj_ref[:, columns(1)], tail_values], axis=0)
    grad_weights = band.join(dot(grad_att, pair_values, ROWS_BY_ROWS))
    grad_scores = band.split(grad_weights * slope * mask_ref[...])
    grad_values = dot(weights, grad_att, COLS_BY_COLS)
    pair_keys = jnp.concatenate([proj_ref[:, columns(3)], tail_keys], axis=0)
    grad_queries = band.pick_heads(dot(grad_scores, pair_keys)) / root
    grad_keys = dot(grad_scores, stack, COLS_BY_COLS) / root
    gated = (att_hat * proj_ref[:, columns(0)].astype(F32)).astype(BF16)
    out_ref[first, :] = (ev_ref[first, :].astype(F32) + dot(gated, w_out_ref[...])).astype(BF16)
    out_ref[last, :] = out_last_ref[...]
    own_pre = [
        (ratio_ref[:, width:] * att_hat).astype(BF16),
        ((grad_values[:window] + grads_ref[:, :width]) * slope_ref[:, columns(1)]).astype(BF16),
        (grad_queries * slope_ref[:, columns(2)]).astype(BF16),
        ((grad_keys[:window] + grads_ref[:, width:]) * slope_ref[:, columns(3)]).astype(BF16),
    ]
    tail_pre = {
        1: (grad_values[window:] * tail_values_slope).astype(BF16),
        3: (grad_keys[window:] * tail_keys_slope).astype(BF16),
    }
    left = jnp.concatenate([normed_ref[...], tail_normed], axis=0)
    own_total, back_total, in_blocks, bias_rows = None, None, [], []
    for i in range(4):
        part = dot(own_pre[i], w_in_ref[:, columns(i)], ROWS_BY_ROWS)
        own_total = part if own_total is None else own_total + part
        right = [own_pre[i], pre_ref[:, columns(i)]]
        if i in tail_pre:
            part = dot(tail_pre[i], w_in_ref[:, columns(i)], ROWS_BY_ROWS)
            back_total = part if back_total is None else back_total + part
            right.append(tail_pre[i])
        right = jnp.concatenate(right, axis=0)
        in_blocks.append(dot(left[: right.shape[0]], right, COLS_BY_COLS) * scale)
        bias_rows.append(jnp.sum(right.astype(F32), axis=0, keepdims=True) * scale)
    own_ref[...] = own_total
    part_out = dot(
        jnp.concatenate([gated, gated_ref[...]], axis=0), cot_ref[...], COLS_BY_COLS
    ) * scale
    tile_row = lax.broadcasted_iota(jnp.int32, (GROUP, 128), 0)
    for piece in range(parts_ref.shape[0]):
        group, half = piece // 2, piece % 2
        here = slice(group * GROUP, (group + 1) * GROUP)
        tiles = [
            in_blocks[2 * half + k // 2][here, (k % 2) * 128 : (k % 2 + 1) * 128]
            for k in range(4)
        ]
        tiles.append(part_out[here, half * 128 : (half + 1) * 128])
        rest = back_total[
            piece // 4 * GROUP : (piece // 4 + 1) * GROUP,
            piece // 2 % 2 * 128 : (piece // 2 % 2 + 1) * 128,
        ]
        if piece % 2:
            rest = pltpu.roll(rest, BACK, 0)
        line = piece // 8
        bias = bias_rows[line // 2][:, line % 2 * 128 : (line % 2 + 1) * 128]
        tiles.append(jnp.where(tile_row < BACK, rest, jnp.broadcast_to(bias, (GROUP, 128))))
        parts_ref[piece] = jnp.concatenate(tiles, axis=0).astype(BF16)


def near_kernel(parts_ref, sum_ref, back_ref):
    total = None
    for i in range(parts_ref.shape[0]):
        piece = parts_ref[i].astype(F32)
        back_ref[i] = piece[5 * GROUP :]
        total = piece if total is None else total + piece
    sums = total.astype(BF16)
    for i in range(sum_ref.shape[0]):
        sum_ref[i] = sums


def far_kernel(sources, parts_ref, back_ref, sum_ref):
    total = parts_ref[0].astype(F32)
    for i in range(1, parts_ref.shape[0]):
        total = total + parts_ref[i].astype(F32)
    tile_row = lax.broadcasted_iota(jnp.int32, (GROUP, 128), 0)
    rest = total[5 * GROUP :]
    for i, source in enumerate(sources):
        back = jnp.zeros_like(rest) if source is None else back_ref[source]
        last = jnp.where(tile_row < BACK, back, rest)
        sum_ref[i] = jnp.concatenate([total[: 5 * GROUP], last], axis=0).astype(BF16)


def unpack_kernel(
    places, all_ref, own_first_ref, own_last_ref, ev_ref, cot_ref, out_ref,
    w_in_hbm, b_in_hbm, w_out_hbm, grad_hbm, out_hbm,
    w_in_ref, b_in_ref, w_out_ref, grad_ref, sems,
):
    copies = []

    def send(source, target):
        copy = pltpu.make_async_copy(source, target, sems.at[len(copies)])
        copy.start()
        copies.append(copy)

    send(out_ref, out_hbm)
    tile_row = lax.broadcasted_iota(jnp.int32, (GROUP, 128), 0)
    lasts = []
    pieces = all_ref.shape[0]
    part = pieces // PARTS
    for piece in range(pieces):
        rows = all_ref[places[piece]].astype(F32)
        group, half = piece // 2, piece % 2
        here = slice(group * GROUP, (group + 1) * GROUP)
        tiles = [rows[k * GROUP : (k + 1) * GROUP] for k in range(6)]
        w_in_ref[here, half * 512 : (half + 1) * 512] = jnp.concatenate(tiles[:4], axis=1)
        w_out_ref[here, half * 128 : (half + 1) * 128] = tiles[4]
        if piece % 8 == 0:
            b_in_ref[piece // 8 : piece // 8 + 1, :] = tiles[5][BACK : BACK + 1]
        lasts.append(tiles[5])
        if (piece + 1) % part == 0:
            done = pl.ds((piece + 1 - part) // 2 * GROUP, part // 2 * GROUP)
            send(w_in_ref.at[done], w_in_hbm.at[done])
    send(w_out_ref, w_out_hbm)
    send(b_in_ref, b_in_hbm)
    back = jnp.concatenate(
        [
            jnp.concatenate(
                [
                    jnp.where(tile_row < BACK, lasts[i], pltpu.roll(lasts[i + 1], BACK, 0))
                    for i in (4 * t, 4 * t + 2)
                ],
                axis=1,
            )
            for t in range(len(lasts) // 4)
        ],
        axis=0,
    )
    window = back.shape[0]
    for half, grad in enumerate((own_first_ref[...], own_last_ref[...] + back)):
        here = slice(half * window, (half + 1) * window)
        hat, inv = norm_rows(ev_ref[here, :].astype(F32))
        grad_ref[here, :] = (cot_ref[here, :].astype(F32) + norm_back(grad, hat, inv)).astype(BF16)
    send(grad_ref, grad_hbm)
    for copy in copies:
        copy.wait()


def call(kernel, outs, *args, spaces=None, scratch=(), flops=0, moved=0):
    spaces = spaces or [pltpu.VMEM] * len(args)
    args = [
        pltpu.with_memory_space_constraint(arg, space) if space == pltpu.HBM else arg
        for arg, space in zip(args, spaces)
    ]
    return pl.pallas_call(
        kernel,
        out_shape=[
            pltpu.VMEM(shape, kind) if KEPT in place else jax.ShapeDtypeStruct(shape, kind)
            for shape, kind, *place in outs
        ],
        in_specs=[pl.BlockSpec(memory_space=space) for space in spaces],
        out_specs=[
            pl.BlockSpec(memory_space=SENT if SENT in place else pltpu.VMEM)
            for _, _, *place in outs
        ],
        scratch_shapes=scratch,
        compiler_params=pltpu.CompilerParams(vmem_limit_bytes=24 * 1024 * 1024),
        cost_estimate=pl.CostEstimate(flops=flops, bytes_accessed=moved, transcendentals=0),
    )(*args)


def on_device(
    events, cotangent, bucket_ids, history_lengths, w_in, b_in, w_out, pos_table, time_table
):
    rows, width = events.shape[1:]
    heads, window = pos_table.shape
    slabs = lax.axis_size(SEQ)
    scale = 1.0 / math.sqrt(lax.axis_size(BATCH) * slabs * rows)
    near, far = lax.axis_size(NEAR), lax.axis_size(FAR)
    moved = lax.ppermute(events, SEQ, [(i, i + 1) for i in range(slabs - 1)])
    half = (window, width)
    band = (heads * window, window)
    own_last, *kept = call(
        own_kernel,
        [
            (shape, kind, KEPT)
            for shape, kind in [
                (half, BF16), (half, BF16), ((window, 4 * width), BF16), (half, F32),
                ((rows, width), BF16), ((window, 4 * width), BF16), ((window, 4 * width), F32),
                (band, F32), (band, F32), ((window, 2 * width), F32),
                ((heads * window, width), BF16), (half, F32), ((window, 2 * width), F32),
                ((rows, width), BF16), ((rows, width), BF16), (w_in.shape, BF16),
                ((1, 4 * width), F32), (w_out.shape, BF16),
            ]
        ],
        history_lengths, events[0], cotangent[0], bucket_ids[0], w_in, b_in[None], w_out,
        pos_table, time_table,
        spaces=[pltpu.SMEM] + [pltpu.HBM] * 8,
        scratch=[
            pltpu.VMEM((rows, window), jnp.int32),
            pltpu.VMEM(pos_table.shape, F32),
            pltpu.VMEM(time_table.shape, F32),
            pltpu.SemaphoreType.DMA((8,)),
        ],
        flops=10**9, moved=10**7,
    )
    own_last, kept = kept[2], [own_last, *kept[:2], *kept[3:]]
    ev, cot = kept[12:14]
    layer_out, parts, own_first = call(
        functools.partial(edge_kernel, scale),
        [((rows, width), BF16, KEPT), ((near, PIECE, 128), BF16, KEPT), (half, F32, KEPT)],
        moved, *kept,
        flops=10**9, moved=10**7,
    )
    zl = lax.axis_size("zl")
    order = [(i + FIRST_OUT) % near for i in range(near)]
    back_order = [(i + FIRST_BACK) % near for i in range(near)]
    places = [back_order.index(i) for i in order]
    sources = [
        order.index(i + zl) if i // zl % slabs < slabs - 1 else None for i in back_order
    ]
    parts = lax.all_to_all(parts, NEAR, 0, 0, axis_index_groups=[order])
    sums, back = call(
        near_kernel, [((far, PIECE, 128), BF16, KEPT), ((near, GROUP, 128), F32, KEPT)], parts
    )
    sums = lax.all_to_all(
        sums, FAR, 0, 0, axis_index_groups=[[(i + 5) % far for i in range(far)]]
    )
    (sums,) = call(
        functools.partial(far_kernel, sources), [((near, PIECE, 128), BF16, KEPT)], sums, back
    )
    sums = lax.all_to_all(sums, NEAR, 0, 0, axis_index_groups=[back_order])
    sum_in, sum_bias, sum_out, grad_events, layer_out = call(
        functools.partial(unpack_kernel, places),
        [
            ((width, 4 * width), F32, SENT), ((8, 128), F32, SENT), ((width, width), F32, SENT),
            ((rows, width), BF16, SENT), ((rows, width), BF16, SENT),
        ],
        sums, own_first, own_last, ev, cot, layer_out,
        scratch=[
            pltpu.VMEM((width, 4 * width), F32), pltpu.VMEM((8, 128), F32),
            pltpu.VMEM((width, width), F32), pltpu.VMEM((rows, width), BF16),
            pltpu.SemaphoreType.DMA((PARTS + 4,)),
        ],
    )
    return (layer_out[None], grad_events[None], sum_in, sum_bias.reshape(4 * width), sum_out)


def solution(mesh):
    fine = Mesh(
        mesh.devices.reshape(2, 8, 2, 2, 4, 2), ("yl", "zh", "zl", "yh", "x", "c")
    )
    slabs = P(BATCH, SEQ, None)
    return jax.shard_map(
        on_device,
        mesh=fine,
        in_specs=(slabs, slabs, slabs, P(BATCH), P(), P(), P(), P(), P()),
        out_specs=(slabs, slabs, P(), P(), P()),
        check_vma=False,
    )
```
